32 devices in a mesh: items: 4 (over y, x), seq: 8 (over z, core).
Axes of the slice: x: 2, y: 2, z: 4, core: 2. Of those that a mesh axis runs over, the one named last changes fastest.
Arguments:
- tokens: bfloat16 [24, 3072, 256], P('items', 'seq'), may hold values from -6 to 6
- lengths: int32 [24], P('items'), may hold values from 768 to 3072, as said below
- pad_mask: int32 [24, 3072], P('items'), may hold values 0 or 1
- w_qkv: bfloat16 [256, 768], replicated, may hold values from -0.375 to 0.375
- w_out: bfloat16 [256, 256], replicated, may hold values from -2 to 2
- w_up: bfloat16 [256, 1024], replicated, may hold values from -0.375 to 0.375
- w_down: bfloat16 [1024, 256], replicated, may hold values from -0.1875 to 0.1875
- gain_attn: float32 [256], replicated, may hold values from 0.25 to 1.75
- shift_attn: float32 [256], replicated, may hold values from -4 to 4
- gain_ffn: float32 [256], replicated, may hold values from 0.25 to 1.75
- shift_ffn: float32 [256], replicated, may hold values from -4 to 4
- cotangent: bfloat16 [24, 3072, 256], P('items', 'seq'), may hold values from -6 to 6
Outputs:
- output: bfloat16 [24, 3072, 256], P('items', 'seq')
- grad_tokens: float32 [24, 3072, 256], P('items', 'seq')
- grad_qkv: float32 [256, 768], replicated
- grad_out: float32 [256, 256], replicated
- grad_up: float32 [256, 1024], replicated
- grad_down: float32 [1024, 256], replicated
- grad_gain_attn: float32 [256], replicated
- grad_shift_attn: float32 [256], replicated
- grad_gain_ffn: float32 [256], replicated
- grad_shift_ffn: float32 [256], replicated
The draws below stay inside these ranges and needn't reach their ends.
Inputs may be any that keep to these rules, and one draw needn't show every extreme that they name: `lengths`: in each group of images 6g to 6g+5 one image has the full length 3072.
All inputs are finite; a program needn't handle non-finite values. No bound on the sum of `pad_mask` on one device may be relied on, other than what follows from the above.
Results may differ from the reference program's by a relative error of at most 0.01.
Values may be sent and summed in bfloat16 or wider, within the bound.
A program may use at most 128 MiB of HBM per device.

```python
import jax
import jax.numpy as jnp
from jax import lax

D = 256
HEADS = 2
HEAD_DIM = 128
FF = 1024
SEQ = 3072
ROW = 96
ITEMS_DEV = 6
ITEMS = 24


def draw_lengths(key, part):
    key = jax.random.fold_in(key, 11)
    first_key, second_key = jax.random.split(key)
    base_len = jax.random.randint(first_key, (ITEMS,), SEQ // 4, SEQ + 1)
    chosen = jax.random.randint(second_key, (ITEMS // ITEMS_DEV,), 0, ITEMS_DEV)
    slot_index = jnp.arange(ITEMS, dtype=jnp.int32) % ITEMS_DEV
    group_index = jnp.arange(ITEMS, dtype=jnp.int32) // ITEMS_DEV
    is_full = slot_index == chosen[group_index]
    return jnp.where(is_full, SEQ, base_len).astype(jnp.int32)


def touch_ends(values, key, least, top_value):
    shape = values.shape
    spot = [jax.random.randint(jax.random.fold_in(key, axis), (), 0, shape[axis]) for axis in range(len(shape))]
    values = values.at[tuple(spot)].set(least)
    longest = shape.index(max(shape))
    spot[longest] = (spot[longest] + 1) % shape[longest]
    return values.at[tuple(spot)].set(top_value)


def shard_levels(stream_key, dims, pieces, least, high):
    def one(dim, blocks):
        draws = jax.random.uniform(jax.random.fold_in(jax.random.fold_in(stream_key, 6), dim), (blocks,), jnp.float32, least / len(pieces), high / len(pieces))
        return jnp.repeat(jnp.exp(draws), dims[dim] // blocks).reshape((-1,) + (1,) * (len(dims) - dim - 1))

    level = one(*pieces[0])
    for cut in pieces[1:]:
        level = level * one(*cut)
    return level


def noise(key, dims, width, bound, shards=(), kind=jnp.bfloat16):
    result = jax.random.normal(key, dims, jnp.float32) * width
    if len(shards) > 0:
        result = shard_levels(key, dims, shards, -0.22, 0.18) * result
    return jnp.clip(result, min=-bound, max=bound).astype(kind)


def setup_inputs(seed: int = 0) -> dict:
    splits = jax.random.split(jax.random.key(seed), 13)
    tokens = noise(splits[0], (ITEMS, SEQ, D), 1.0, 6.0, ((0, 4), (1, 8)))
    lengths = draw_lengths(jax.random.fold_in(splits[12], 71), 0)
    pad_mask = touch_ends((jax.random.randint(splits[2], (ITEMS, SEQ), 0, 8) < 7).astype(jnp.int32), jax.random.fold_in(splits[2], 1), 0, 1)
    w_qkv = noise(splits[3], (D, 3 * D), D ** -0.5, 0.375)
    w_out = noise(splits[4], (D, D), (D // 32) ** -0.5, 2.0)
    w_up = noise(splits[5], (D, FF), D ** -0.5, 0.375)
    w_down = noise(splits[6], (FF, D), FF ** -0.5, 0.1875)
    gain_attn = jnp.clip(1.0 + 0.15 * jax.random.normal(splits[7], (D,), jnp.float32), 0.25, 1.75)
    shift_attn = noise(splits[8], (D,), 0.3, 4.0, (), jnp.float32)
    gain_ffn = jnp.clip(1.0 + 0.15 * jax.random.normal(splits[9], (D,), jnp.float32), 0.25, 1.75)
    shift_ffn = noise(splits[10], (D,), 0.3, 4.0, (), jnp.float32)
    cotangent = noise(splits[11], (ITEMS, SEQ, D), 1.0, 6.0, ((0, 4), (1, 8)))
    return {"tokens": tokens, "lengths": lengths, "pad_mask": pad_mask, "w_qkv": w_qkv, "w_out": w_out, "w_up": w_up, "w_down": w_down, "gain_attn": gain_attn, "shift_attn": shift_attn, "gain_ffn": gain_ffn, "shift_ffn": shift_ffn, "cotangent": cotangent}


epsilon = 1e-05
branch_scale = 0.7071067811865476
masked_value = -1e+30
highest = lax.Precision.HIGHEST

@jax.custom_vjp
def low(v):
    return lax.optimization_barrier(v.astype(jnp.bfloat16)).astype(jnp.float32)

@jax.custom_vjp
def low_back(v):
    return v

def low_keep(v):
    return (low(v), None)

def low_pass(kept, grad):
    return (grad,)

def back_keep(v):
    return (v, None)

def back_low(kept, grad):
    return (low(grad),)
low.defvjp(low_keep, low_pass)
low_back.defvjp(back_keep, back_low)

def layer_norm(inputs, gain_vec, shift_vec):
    average = lax.optimization_barrier(jnp.mean(inputs, -1, keepdims=True))
    centred = inputs - average
    spread = lax.optimization_barrier(jnp.mean(centred * centred, -1, keepdims=True))
    return centred * lax.rsqrt(spread + epsilon) * gain_vec + shift_vec

def with_before(source, blocks):
    before = jnp.concatenate([jnp.zeros_like(source[:1]), source[:-1]], 0)
    return jnp.concatenate([before, blocks], 1)

def forward(inputs_all, w_qkv, w_out, w_up, w_down, gain_attn, shift_attn, gain_ffn, shift_ffn, valid_mask):
    row_count = SEQ // ROW
    query_pos = jnp.arange(ROW, dtype=jnp.int32)[:, None]
    key_pos = jnp.arange(2 * ROW, dtype=jnp.int32)[None, :] - ROW
    score_scale = HEAD_DIM ** (-0.5)

    def one_item(item_pair):
        inputs, token_alive = item_pair
        normed = low(layer_norm(inputs, gain_attn, shift_attn))
        projected = low(jnp.dot(normed, w_qkv, precision=highest))
        head_shape = (row_count, ROW, HEADS, HEAD_DIM)
        queries = low_back(projected[:, :D]).reshape(head_shape)
        kv_own = low_back(projected[:, D:])
        kv_next = low_back(projected[:, D:])
        keys_all = with_before(kv_next[:, :D].reshape(head_shape), kv_own[:, :D].reshape(head_shape))
        values_all = with_before(kv_next[:, D:].reshape(head_shape), kv_own[:, D:].reshape(head_shape))
        alive_rows = token_alive.reshape(row_count, ROW)
        key_alive = with_before(alive_rows, alive_rows)[:, None, :] > 0.5
        allowed = (key_pos < 0) & key_alive | (key_pos >= 0) & (key_pos <= query_pos) & (key_alive | (key_pos == query_pos))
        scores = low_back(jnp.einsum('rqhd,rkhd->rhqk', queries, keys_all, precision=highest) * score_scale)
        scores = jnp.where(allowed[:, None], scores, masked_value)
        row_max = lax.optimization_barrier(jnp.max(scores, -1, keepdims=True))
        exp_scores = jnp.exp(scores - row_max)
        probs_low = low(exp_scores / lax.optimization_barrier(jnp.sum(exp_scores, -1, keepdims=True)))
        attended = jnp.einsum('rhqk,rkhd->rqhd', probs_low, values_all, precision=highest).reshape(SEQ, D)
        attended = low_back(low(attended))
        branch_attn = low_back(jnp.dot(attended, w_out, precision=highest))
        middle = inputs + branch_scale * branch_attn
        normed_ffn = low(layer_norm(middle, gain_ffn, shift_ffn))
        hidden_pre = low_back(jnp.dot(normed_ffn, w_up, precision=highest))
        hidden = low(jax.nn.gelu(hidden_pre, approximate=True))
        branch_ffn = low_back(jnp.dot(hidden, w_down, precision=highest))
        return token_alive[:, None] * (middle + branch_scale * branch_ffn)
    return lax.map(jax.checkpoint(one_item), (inputs_all, valid_mask))

def reference(tokens, lengths, pad_mask, w_qkv, w_out, w_up, w_down, gain_attn, shift_attn, gain_ffn, shift_ffn, cotangent):
    positions = jnp.arange(SEQ, dtype=jnp.int32)
    valid_mask = ((positions[None, :] < lengths[:, None]) & (pad_mask == 1)).astype(jnp.float32)

    def run(inputs_all, qkv_f, out_f, up_f, down_f, gain_a, shift_a, gain_f, shift_f):
        return forward(inputs_all, qkv_f, out_f, up_f, down_f, gain_a, shift_a, gain_f, shift_f, valid_mask)
    output, pullback = jax.vjp(run, tokens.astype(jnp.float32), w_qkv.astype(jnp.float32), w_out.astype(jnp.float32), w_up.astype(jnp.float32), w_down.astype(jnp.float32), gain_attn.astype(jnp.float32), shift_attn.astype(jnp.float32), gain_ffn.astype(jnp.float32), shift_ffn.astype(jnp.float32))
    grads = pullback(cotangent.astype(jnp.float32))
    return (output.astype(jnp.bfloat16), grads[0], grads[1], grads[2], grads[3], grads[4], grads[5], grads[6], grads[7], grads[8])
```

```python
import functools
import math

import jax
import jax.numpy as jnp
from jax import lax
from jax.experimental import pallas as pl
from jax.experimental.pallas import tpu as pltpu
from jax.sharding import PartitionSpec as P

HEADS = 2
HEAD_DIM = 128
ROW = 96
D = HEADS * HEAD_DIM

epsilon = 1e-05
branch_scale = 0.7071067811865476
masked_value = -1e30
score_scale = HEAD_DIM ** (-0.5)
log2e = math.log2(math.e)
gelu_in = math.sqrt(2 / math.pi)
gelu_cube = gelu_in * 0.044715
f32 = jnp.float32
bf16 = jnp.bfloat16


def dot(left, right, left_dim=1, right_dim=0):
    return lax.dot_general(
        left, right, (((left_dim,), (right_dim,)), ((), ())), preferred_element_type=f32
    )


def normalise(inputs):
    average = jnp.mean(inputs, -1, keepdims=True)
    centred = inputs - average
    spread = jnp.mean(centred * centred, -1, keepdims=True)
    factor = lax.rsqrt(spread + epsilon)
    return centred * factor, factor


def norm_back(grad, normed, factor, gain):
    e = grad * gain
    first = jnp.mean(e, -1, keepdims=True)
    second = jnp.mean(e * normed, -1, keepdims=True)
    return factor * (e - first - normed * second)


def fold_rows(values):
    count = values.shape[0] // 8
    return jnp.sum(values.reshape(count, 8, values.shape[1]), 0)


def layer_kernel(
    items,
    rows,
    tokens_ref,
    halo_ref,
    cot_ref,
    alive_ref,
    keys_ref,
    wqkv_ref,
    wout_ref,
    wup_ref,
    wdown_ref,
    vecs_ref,
    output_ref,
    gtok_ref,
    ghalo_ref,
    gqkv_ref,
    gout_ref,
    gup_ref,
    gdown_ref,
    gvec_ref,
    h1,
    n1,
    r1,
    proj,
    exps,
    inv,
    att,
    middle,
    n2,
    r2,
    h2,
    dbr,
    hid,
    dpre,
    dmid,
    datt,
    dproj,
):
    block = rows * ROW
    total = items * block
    steps = 3
    size = total // steps
    gain_attn = vecs_ref[0:1]
    shift_attn = vecs_ref[1:2]
    gain_ffn = vecs_ref[2:3]
    shift_ffn = vecs_ref[3:4]
    ff = wup_ref.shape[1]
    chunks = ff // 256

    def first_norm(x, i, at, count):
        normed, factor = normalise(x)
        low = (normed * gain_attn + shift_attn).astype(bf16)
        h1[i, at : at + count] = low
        n1[i, at : at + count] = normed.astype(bf16)
        r1[i, at : at + count] = jnp.broadcast_to(factor, (count, 128))
        return low

    def project(i, _):
        low = first_norm(tokens_ref[i].astype(f32), i, ROW, block)
        proj[i, ROW:] = dot(low, wqkv_ref[...]).astype(bf16)
        return _

    lax.fori_loop(0, items, project, 0)

    def project_halo(i, _):
        low = first_norm(halo_ref[i].astype(f32), i, 0, ROW)
        proj[i, :ROW, D:] = dot(low, wqkv_ref[:, D:]).astype(bf16)
        return _

    lax.fori_loop(0, items, project_halo, 0)

    query_pos = lax.broadcasted_iota(jnp.int32, (ROW, 2 * ROW), 0)
    key_pos = lax.broadcasted_iota(jnp.int32, (ROW, 2 * ROW), 1) - ROW
    causal = jnp.where(key_pos <= query_pos, 0.0, masked_value)
    itself = jnp.where(key_pos == query_pos, 0.0, masked_value)

    def attend(i, _):
        for r in range(rows):
            bias = jnp.maximum(jnp.minimum(causal, keys_ref[i, r : r + 1]), itself)
            for h in range(HEADS):
                at = h * HEAD_DIM
                q = proj[i, (r + 1) * ROW : (r + 2) * ROW, at : at + HEAD_DIM]
                k = proj[i, r * ROW : (r + 2) * ROW, D + at : D + at + HEAD_DIM]
                v = proj[i, r * ROW : (r + 2) * ROW, 2 * D + at : 2 * D + at + HEAD_DIM]
                scores = dot(q, k, 1, 1) * (score_scale * log2e) + bias
                top = jnp.max(scores, -1, keepdims=True)
                e = jnp.exp2(scores - top)
                share = 1.0 / jnp.sum(e, -1, keepdims=True)
                low = e.astype(bf16)
                exps[i, r * HEADS + h, :, : 2 * ROW] = low
                share = jnp.broadcast_to(share, (ROW, HEAD_DIM))
                inv[i, r * ROW : (r + 1) * ROW, at : at + HEAD_DIM] = share
                att[i, r * ROW : (r + 1) * ROW, at : at + HEAD_DIM] = (dot(low, v) * share).astype(bf16)
        mid = tokens_ref[i].astype(f32) + branch_scale * dot(att[i], wout_ref[...])
        middle[i] = mid
        normed, factor = normalise(mid)
        n2[i] = normed.astype(bf16)
        r2[i] = jnp.broadcast_to(factor, (block, 128))
        h2[pl.ds(i * block, block)] = (normed * gain_ffn + shift_ffn).astype(bf16)
        mask = jnp.concatenate([alive_ref[i]] * 2, 1)
        dbr[pl.ds(i * block, block)] = (branch_scale * (mask * cot_ref[i].astype(f32))).astype(bf16)
        return _

    lax.fori_loop(0, items, attend, 0)

    gup_ref[...] = jnp.zeros_like(gup_ref)
    gdown_ref[...] = jnp.zeros_like(gdown_ref)
    for c in range(chunks):
        cols = slice(c * 256, (c + 1) * 256)

        def feed(t, _):
            here = pl.ds(pl.multiple_of(t * size, 128), size)
            u = dot(h2[here], wup_ref[:, cols])
            back = dot(dbr[here], wdown_ref[cols], 1, 1)
            square = u * u
            s = 0.5 * jnp.tanh(u * (gelu_in + gelu_cube * square)) + 0.5
            hidden = (u * s).astype(bf16)
            slope = s + u * ((s - s * s) * (2 * gelu_in + 6 * gelu_cube * square))
            before = (back * slope).astype(bf16)
            hid[here, cols] = hidden
            dpre[here, cols] = before
            gdown_ref[:, cols] += dot(dbr[here], hidden, 0, 0)
            gup_ref[:, cols] += dot(h2[here], before, 0, 0)
            return _

        lax.fori_loop(0, steps, feed, 0)

    gvec_ref[...] = jnp.zeros_like(gvec_ref)
    gout_ref[...] = jnp.zeros_like(gout_ref)

    def middle_back(i, _):
        here = pl.ds(pl.multiple_of(i * block, 64), block)
        grad = dot(dpre[here], wup_ref[...], 1, 1)
        normed = n2[i].astype(f32)
        gvec_ref[16:24] += fold_rows(grad * normed)
        gvec_ref[24:32] += fold_rows(grad)
        factor = jnp.concatenate([r2[i]] * 2, 1)
        mask = jnp.concatenate([alive_ref[i]] * 2, 1)
        grad = mask * cot_ref[i].astype(f32) + norm_back(grad, normed, factor, gain_ffn)
        dmid[i] = grad
        low = (branch_scale * grad).astype(bf16)
        gout_ref[...] += dot(att[i], low, 0, 0)
        datt[i] = dot(low, wout_ref[...], 1, 1).astype(bf16)
        return _

    lax.fori_loop(0, items, middle_back, 0)

    def attend_back(i, _):
        for h in range(HEADS):
            at = h * HEAD_DIM
            held_k = None
            held_v = None
            for r in range(rows):
                q = proj[i, (r + 1) * ROW : (r + 2) * ROW, at : at + HEAD_DIM]
                k = proj[i, r * ROW : (r + 2) * ROW, D + at : D + at + HEAD_DIM]
                v = proj[i, r * ROW : (r + 2) * ROW, 2 * D + at : 2 * D + at + HEAD_DIM]
                own = slice(r * ROW, (r + 1) * ROW)
                grad = datt[i, own, at : at + HEAD_DIM].astype(f32) * inv[i, own, at : at + HEAD_DIM]
                low = grad.astype(bf16)
                row_dot = jnp.sum(grad * att[i, own, at : at + HEAD_DIM].astype(f32), -1, keepdims=True)
                e = exps[i, r * HEADS + h, :, : 2 * ROW]
                ds = (e.astype(f32) * ((dot(low, v, 1, 1) - row_dot) * score_scale)).astype(bf16)
                dv = dot(e, low, 0, 0)
                dk = dot(ds, q, 0, 0)
                dproj[i, (r + 1) * ROW : (r + 2) * ROW, at : at + HEAD_DIM] = dot(ds, k).astype(bf16)
                first_k, first_v = dk[:ROW], dv[:ROW]
                if held_k is not None:
                    first_k += held_k
                    first_v += held_v
                dproj[i, r * ROW : (r + 1) * ROW, D + at : D + at + HEAD_DIM] = first_k.astype(bf16)
                dproj[i, r * ROW : (r + 1) * ROW, 2 * D + at : 2 * D + at + HEAD_DIM] = first_v.astype(bf16)
                held_k, held_v = dk[ROW:], dv[ROW:]
            dproj[i, rows * ROW :, D + at : D + at + HEAD_DIM] = held_k.astype(bf16)
            dproj[i, rows * ROW :, 2 * D + at : 2 * D + at + HEAD_DIM] = held_v.astype(bf16)
        dproj[i, :ROW, :D] = jnp.zeros((ROW, D), bf16)
        return _

    lax.fori_loop(0, items, attend_back, 0)

    gqkv_ref[...] = jnp.zeros_like(gqkv_ref)

    def weight_back(i, _):
        gqkv_ref[...] += dot(h1[i], dproj[i], 0, 0)
        return _

    lax.fori_loop(0, items, weight_back, 0)

    def tokens_back(i, _):
        grad = dot(dproj[i], wqkv_ref[...], 1, 1)
        normed = n1[i].astype(f32)
        gvec_ref[0:8] += fold_rows(grad * normed)
        gvec_ref[8:16] += fold_rows(grad)
        factor = jnp.concatenate([r1[i]] * 2, 1)
        grad = norm_back(grad, normed, factor, gain_attn)
        ghalo_ref[i] = grad[:ROW].astype(bf16)
        gtok_ref[i] = dmid[i] + grad[ROW:]
        return _

    lax.fori_loop(0, items, tokens_back, 0)

    def finish(i, _):
        here = pl.ds(pl.multiple_of(i * block, 64), block)
        branch = dot(hid[here], wdown_ref[...])
        mask = jnp.concatenate([alive_ref[i]] * 2, 1)
        output_ref[i] = (mask * (middle[i] + branch_scale * branch)).astype(bf16)
        return _

    lax.fori_loop(0, items, finish, 0)


def from_behind(block, axis, distance):
    devices = range(lax.axis_size(axis))
    route = [(i - distance, i) for i in devices if i - distance in devices]
    return lax.ppermute(block, axis, route)


def shards(
    tokens,
    lengths,
    pad_mask,
    w_qkv,
    w_out,
    w_up,
    w_down,
    gain_attn,
    shift_attn,
    gain_ffn,
    shift_ffn,
    cotangent,
):
    items, block, width = tokens.shape
    rows = block // ROW
    total = items * block
    ff = w_up.shape[1]
    first_pos = lax.axis_index("seq") * block
    padded = jnp.pad(pad_mask, ((0, 0), (ROW, 0)))
    positions = first_pos - ROW + jnp.arange(block + ROW, dtype=jnp.int32)
    here = lax.dynamic_slice_in_dim(padded, first_pos, block + ROW, 1)
    alive = (positions[None, :] < lengths[:, None]) & (here == 1)
    alive_cols = jnp.broadcast_to(alive[:, ROW:, None].astype(f32), (items, block, 128))
    key_bias = jnp.where(alive, 0.0, masked_value)
    key_bias = jnp.stack([key_bias[:, r * ROW : (r + 2) * ROW] for r in range(rows)], 1)
    halo = from_behind(tokens[:, -ROW:], "seq", 1)
    vecs = jnp.stack([gain_attn, shift_attn, gain_ffn, shift_ffn])
    ext = block + ROW
    shapes = [
        jax.ShapeDtypeStruct((items, block, width), bf16),
        jax.ShapeDtypeStruct((items, block, width), f32),
        jax.ShapeDtypeStruct((items, ROW, width), bf16),
        jax.ShapeDtypeStruct((width, 3 * width), f32),
        jax.ShapeDtypeStruct((width, width), f32),
        jax.ShapeDtypeStruct((width, ff), f32),
        jax.ShapeDtypeStruct((width, ff), f32),
        jax.ShapeDtypeStruct((32, width), f32),
    ]
    outs = pl.pallas_call(
        functools.partial(layer_kernel, items, rows),
        out_shape=shapes,
        in_specs=[pl.BlockSpec(memory_space=pltpu.VMEM)] * 10,
        out_specs=[pl.BlockSpec(memory_space=pltpu.VMEM)] * 8,
        scratch_shapes=[
            pltpu.VMEM((items, ext, width), bf16),
            pltpu.VMEM((items, ext, width), bf16),
            pltpu.VMEM((items, ext, 128), f32),
            pltpu.VMEM((items, ext, 3 * width), bf16),
            pltpu.VMEM((items, rows * HEADS, ROW, 256), bf16),
            pltpu.VMEM((items, block, width), f32),
            pltpu.VMEM((items, block, width), bf16),
            pltpu.VMEM((items, block, width), f32),
            pltpu.VMEM((items, block, width), bf16),
            pltpu.VMEM((items, block, 128), f32),
            pltpu.VMEM((total, width), bf16),
            pltpu.VMEM((total, width), bf16),
            pltpu.VMEM((total, ff), bf16),
            pltpu.VMEM((total, ff), bf16),
            pltpu.VMEM((items, block, width), f32),
            pltpu.VMEM((items, block, width), bf16),
            pltpu.VMEM((items, ext, 3 * width), bf16),
        ],
        compiler_params=pltpu.CompilerParams(vmem_limit_bytes=60 * 2**20),
    )(tokens, halo, cotangent, alive_cols, key_bias, w_qkv, w_out, w_up, w_down, vecs)
    output, gtok, ghalo, gqkv, gout, gup, gdown, gvec = outs
    returned = from_behind(ghalo, "seq", -1)
    gtok = gtok.at[:, -ROW:].add(returned.astype(f32))
    gvec = jnp.sum(gvec.reshape(4, 8, width), 1)
    gqkv, gout, gup, gdown, gvec = lax.psum((gqkv, gout, gup, gdown.T, gvec), ("items", "seq"))
    return (output, gtok, gqkv, gout, gup, gdown, gvec[0], gvec[1], gvec[2], gvec[3])


def solution(mesh):
    split = P("items", "seq", None)
    return jax.shard_map(
        shards,
        mesh=mesh,
        in_specs=(split, P("items"), P("items", None)) + (P(),) * 8 + (split,),
        out_specs=(split, split) + (P(),) * 8,
        check_vma=False,
    )
```

```python
import functools
import math

import jax
import jax.numpy as jnp
from jax import lax
from jax.experimental import pallas as pl
from jax.experimental.pallas import tpu as pltpu
from jax.sharding import PartitionSpec as P

HEADS = 2
HEAD_DIM = 128
ROW = 96
D = HEADS * HEAD_DIM

epsilon = 1e-05
branch_scale = 0.7071067811865476
masked_value = -1e30
score_scale = HEAD_DIM ** (-0.5)
log2e = math.log2(math.e)
gelu_in = math.sqrt(2 / math.pi)
gelu_cube = gelu_in * 0.044715
f32 = jnp.float32
bf16 = jnp.bfloat16


def dot(left, right, left_dim=1, right_dim=0):
    return lax.dot_general(
        left, right, (((left_dim,), (right_dim,)), ((), ())), preferred_element_type=f32
    )


def normalise(inputs):
    average = jnp.mean(inputs, -1, keepdims=True)
    centred = inputs - average
    spread = jnp.mean(centred * centred, -1, keepdims=True)
    factor = lax.rsqrt(spread + epsilon)
    return centred * factor, factor


def norm_back(grad, normed, factor, gain):
    e = grad * gain
    first = jnp.mean(e, -1, keepdims=True)
    second = jnp.mean(e * normed, -1, keepdims=True)
    return factor * (e - first - normed * second)


def fold_rows(values):
    count = values.shape[0] // 8
    return jnp.sum(values.reshape(count, 8, values.shape[1]), 0)


class Sums:
    def __init__(self, mesh_sizes, refs):
        (self.partial, self.c_out, self.c_in, self.i_out, self.i_in, self.z_out, self.z_in,
         self.full, self.send, self.recv) = refs
        self.n_items, self.n_z = mesh_sizes
        self.item = lax.axis_index("items")
        seq = lax.axis_index("seq")
        self.core = lax.rem(seq, 2)
        self.z = seq // 2

    def partner(self, kind, step):
        if kind == "core":
            return {"items": self.item, "seq": self.z * 2 + 1 - self.core}
        if kind == "items":
            return {"items": lax.rem(self.item + step, self.n_items), "seq": self.z * 2 + self.core}
        return {"items": self.item, "seq": lax.rem(self.z + step, self.n_z) * 2 + self.core}

    def steps_of(self, kind):
        return range(1, {"core": 2, "items": self.n_items, "z": self.n_z}[kind])

    def copies(self, part, phase, kind, source, target):
        result = []
        base = {"core": 0, "items": 1, "z": self.n_items}[kind]
        for step in self.steps_of(kind):
            slot = (part * 2 + phase, base + step - 1)
            result.append(
                pltpu.make_async_remote_copy(
                    src_ref=source(step),
                    dst_ref=target(step),
                    send_sem=self.send.at[slot],
                    recv_sem=self.recv.at[slot],
                    device_id=self.partner(kind, step),
                    device_id_type=pl.DeviceIdType.MESH,
                )
            )
        return result

    def start(self, copies):
        for copy in copies:
            copy.start()

    def finish(self, copies):
        for copy in copies:
            copy.wait_recv()
        for copy in copies:
            copy.wait_send()

    def place(self, first, rows):
        half = rows // 2
        quarter = half // self.n_items
        split = quarter % (16 * self.n_z) == 0
        last = quarter // self.n_z if split else quarter
        return half, quarter, split, last

    def first_copies(self, part, first, rows):
        half, _, _, _ = self.place(first, rows)
        here = pl.ds(first // 2, half)
        return self.copies(part, 0, "core", lambda s: self.c_out.at[here], lambda s: self.c_in.at[here])

    def items_copies(self, part, first, rows):
        half, quarter, _, _ = self.place(first, rows)

        def source(step):
            to = lax.rem(self.item + step, self.n_items)
            return self.i_out.at[pl.ds(pl.multiple_of(first // 2 + to * quarter, 16), quarter)]

        at = pl.ds(first // 2 // self.n_items, quarter)
        return self.copies(part, 0, "items", source, lambda s: self.i_in.at[s - 1, at])

    def z_copies(self, part, first, rows):
        half, quarter, split, last = self.place(first, rows)
        base = first // 2 // self.n_items
        if split:
            def source(step):
                to = lax.rem(self.z + step, self.n_z)
                return self.z_out.at[pl.ds(pl.multiple_of(base + to * last, 16), last)]

            at = pl.ds(base // self.n_z, last)
            return self.copies(part, 0, "z", source, lambda s: self.z_in.at[s - 1, at])
        at = pl.ds(base, quarter)
        return self.copies(part, 0, "z", lambda s: self.z_out.at[at], lambda s: self.z_in.at[self.z, at])

    def held(self, first, rows, level):
        half, quarter, split, last = self.place(first, rows)
        at = first + self.core * half
        count = half
        if level > 0:
            at += self.item * quarter
            count = quarter
        if level > 1 and split:
            at += self.z * last
            count = last
        return self.full.at[pl.ds(pl.multiple_of(at, 16), count)]

    def back_copies(self, part, first, rows, kind):
        level = {"core": 0, "items": 1, "z": 2}[kind]
        ref = self.held(first, rows, level)
        return self.copies(part, 1, kind, lambda s: ref, lambda s: ref)

    def step(self, part, first, rows, number):
        half, quarter, split, last = self.place(first, rows)
        base_c = first // 2
        base_i = base_c // self.n_items
        if number == 0:
            away = pl.ds(pl.multiple_of(first + (1 - self.core) * half, 16), half)
            self.c_out[pl.ds(base_c, half)] = self.partial[away].astype(bf16)
            self.start(self.first_copies(part, first, rows))
        if number == 1:
            self.finish(self.first_copies(part, first, rows))
            here = pl.ds(base_c, half)
            own = pl.ds(pl.multiple_of(first + self.core * half, 16), half)
            self.i_out[here] = (self.partial[own] + self.c_in[here].astype(f32)).astype(bf16)
            self.start(self.items_copies(part, first, rows))
        if number == 2:
            self.finish(self.items_copies(part, first, rows))
            own = pl.ds(pl.multiple_of(base_c + self.item * quarter, 16), quarter)
            at = pl.ds(base_i, quarter)
            value = self.i_out[own].astype(f32)
            for step in self.steps_of("items"):
                value += self.i_in[step - 1, at].astype(f32)
            self.z_out[at] = value.astype(bf16)
            if not split:
                self.z_in[self.z, at] = value.astype(bf16)
            self.start(self.z_copies(part, first, rows))
        if number == 3:
            self.finish(self.z_copies(part, first, rows))
            if split:
                own = pl.ds(pl.multiple_of(base_i + self.z * last, 16), last)
                at = pl.ds(base_i // self.n_z, last)
                value = self.z_out[own].astype(f32)
                for step in self.steps_of("z"):
                    value += self.z_in[step - 1, at].astype(f32)
            else:
                at = pl.ds(base_i, quarter)
                value = self.z_in[0, at].astype(f32)
                for step in self.steps_of("z"):
                    value += self.z_in[step, at].astype(f32)
            self.held(first, rows, 2)[...] = value.astype(bf16)
            if split:
                self.start(self.back_copies(part, first, rows, "z"))
            else:
                self.start(self.back_copies(part, first, rows, "items"))
        if number == 4 and split:
            self.finish(self.back_copies(part, first, rows, "z"))
            self.start(self.back_copies(part, first, rows, "items"))
        if number == 5:
            self.finish(self.back_copies(part, first, rows, "items"))
            self.start(self.back_copies(part, first, rows, "core"))
        if number == 6:
            self.finish(self.back_copies(part, first, rows, "core"))


def layer_kernel(
    items,
    rows,
    mesh_sizes,
    seq_size,
    lengths_ref,
    pad_ref,
    tokens_ref,
    cot_hbm,
    wqkv_hbm,
    wout_hbm,
    wup_hbm,
    wdown_hbm,
    gain_attn_ref,
    shift_attn_ref,
    gain_ffn_ref,
    shift_ffn_ref,
    output_ref,
    gtok_ref,
    grads_ref,
    gvec_ref,
    x,
    cot,
    alive,
    keys,
    wqkv,
    wout,
    wup,
    wdown,
    h1,
    n1,
    r1,
    proj,
    exps,
    inv,
    att,
    middle,
    n2,
    r2,
    h2,
    dbr,
    hid,
    dpre,
    dmid,
    datt,
    dproj,
    ghalo,
    ghalo_in,
    out,
    gvec,
    vec_buf,
    partial,
    c_out,
    c_in,
    i_out,
    i_in,
    z_out,
    z_in,
    full,
    load_sems,
    store_sems,
    halo_sems,
    vec_sems,
    send_sems,
    recv_sems,
):
    block = rows * ROW
    total = items * block
    steps = 3
    size = total // steps
    gain_attn = gain_attn_ref[...]
    shift_attn = shift_attn_ref[...]
    gain_ffn = gain_ffn_ref[...]
    shift_ffn = shift_ffn_ref[...]
    ff = wup.shape[1]
    chunks = ff // D
    n_items, n_z = mesh_sizes
    item = lax.axis_index("items")
    seq = lax.axis_index("seq")
    MESH = pl.DeviceIdType.MESH
    sums = Sums(
        mesh_sizes, (partial, c_out, c_in, i_out, i_in, z_out, z_in, full, send_sems, recv_sems)
    )
    parts = [(c * 2 * D, 2 * D) for c in range(chunks)] + [(chunks * 2 * D, 4 * D)]

    def step(part, number):
        sums.step(part, *parts[part], number)

    after = {"items": item, "seq": lax.rem(seq + 1, seq_size)}
    ahead = {"items": item, "seq": lax.rem(seq + seq_size - 1, seq_size)}
    barrier = pltpu.get_barrier_semaphore()
    greeted = [after, ahead]
    for kind in ("core", "items", "z"):
        greeted += [sums.partner(kind, s) for s in sums.steps_of(kind)]
    for device in greeted:
        pl.semaphore_signal(barrier, inc=1, device_id=device, device_id_type=MESH)

    loads = [
        (wqkv_hbm, wqkv),
        (wout_hbm, wout),
        (wup_hbm, wup),
        (wdown_hbm, wdown),
        (cot_hbm, cot),
    ]
    token_loads = [
        pltpu.make_async_copy(tokens_ref.at[i], x.at[i, pl.ds(ROW, block)], load_sems.at[5 + i])
        for i in range(items)
    ]
    weight_loads = [
        pltpu.make_async_copy(source, target, load_sems.at[k])
        for k, (source, target) in enumerate(loads)
    ]
    weight_loads[0].start()
    for copy in token_loads:
        copy.start()
    for copy in weight_loads[1:]:
        copy.start()

    pl.semaphore_wait(barrier, len(greeted))
    halo_copy = pltpu.make_async_remote_copy(
        src_ref=tokens_ref.at[:, pl.ds(block - ROW, ROW)],
        dst_ref=x.at[:, pl.ds(0, ROW)],
        send_sem=halo_sems.at[0],
        recv_sem=halo_sems.at[1],
        device_id=after,
        device_id_type=MESH,
    )
    halo_copy.start()

    first_pos = seq * block

    def window(start, width):
        spots = sorted({(s * block + (start if s else 0)) % 128 for s in range(seq_size)})
        if start:
            spots = sorted({(s * block + start) % 128 for s in range(1, seq_size)})
        at = jnp.maximum(first_pos + start, 0)
        low = pl.multiple_of(at // 128 * 128, 128)
        wide = (spots[-1] + width + 127) // 128 * 128
        held = pad_ref[:, pl.ds(low, wide)]
        result = held[:, spots[0] : spots[0] + width]
        for spot in spots[1:]:
            result = jnp.where(at % 128 == spot, held[:, spot : spot + width], result)
        return result

    count = jnp.zeros((items, 1), jnp.int32)
    which = lax.broadcasted_iota(jnp.int32, (items, 1), 0)
    for i in range(items):
        count = jnp.where(which == i, lengths_ref[i], count)

    def there(start, width):
        position = first_pos + start + lax.broadcasted_iota(jnp.int32, (items, width), 1)
        good = (position >= 0) & (position < count) & (window(start, width) == 1)
        return jnp.where(good, 1.0, 0.0)

    row_there = [there((r - 1) * ROW, ROW) for r in range(rows + 1)]
    spread = lax.broadcasted_iota(jnp.int32, (items, items * 128), 1) // 128
    spread = jnp.where(spread == lax.broadcasted_iota(jnp.int32, (items, items * 128), 0), 1.0, 0.0)
    for r in range(rows):
        both = jnp.concatenate([row_there[r], row_there[r + 1]], 1)
        keys[r, :items, : 2 * ROW] = (1.0 - both) * masked_value
        column = dot(row_there[r + 1].astype(bf16), spread.astype(bf16), 0, 0)
        for i in range(items):
            alive[i, r * ROW : (r + 1) * ROW] = column[:, i * 128 : (i + 1) * 128]

    def alive_of(i):
        mask = alive[i]
        return jnp.concatenate([mask, mask], 1)

    def first_norm(values, i, at, count):
        normed, factor = normalise(values)
        low = (normed * gain_attn + shift_attn).astype(bf16)
        h1[i, at : at + count] = low
        n1[i, at : at + count] = normed.astype(bf16)
        r1[i, at : at + count] = jnp.broadcast_to(factor, (count, 128))
        return low

    weight_loads[0].wait()

    def project(i, _):
        pltpu.make_async_copy(
            tokens_ref.at[i], x.at[i, pl.ds(ROW, block)], load_sems.at[5 + i]
        ).wait()
        low = first_norm(x[i, ROW:].astype(f32), i, ROW, block)
        proj[i, ROW:] = dot(low, wqkv[...]).astype(bf16)
        return _

    lax.fori_loop(0, items, project, 0)
    halo_copy.wait()

    def project_halo(i, _):
        low = first_norm(x[i, :ROW].astype(f32), i, 0, ROW)
        proj[i, :ROW, D:] = dot(low, wqkv[:, D:]).astype(bf16)
        return _

    lax.fori_loop(0, items, project_halo, 0)

    query_pos = lax.broadcasted_iota(jnp.int32, (ROW, 2 * ROW), 0)
    key_pos = lax.broadcasted_iota(jnp.int32, (ROW, 2 * ROW), 1) - ROW
    causal = jnp.where(key_pos <= query_pos, 0.0, masked_value)
    itself = jnp.where(key_pos == query_pos, 0.0, masked_value)
    for copy in weight_loads[1:]:
        copy.wait()

    def attend(i, _):
        for r in range(rows):
            bias = jnp.maximum(jnp.minimum(causal, keys[r, pl.ds(i, 1), : 2 * ROW]), itself)
            for h in range(HEADS):
                at = h * HEAD_DIM
                q = proj[i, (r + 1) * ROW : (r + 2) * ROW, at : at + HEAD_DIM]
                k = proj[i, r * ROW : (r + 2) * ROW, D + at : D + at + HEAD_DIM]
                v = proj[i, r * ROW : (r + 2) * ROW, 2 * D + at : 2 * D + at + HEAD_DIM]
                scores = dot(q, k, 1, 1) * (score_scale * log2e) + bias
                top = jnp.max(scores, -1, keepdims=True)
                e = jnp.exp2(scores - top)
                share = 1.0 / jnp.sum(e, -1, keepdims=True)
                low = e.astype(bf16)
                exps[i, r * HEADS + h, :, : 2 * ROW] = low
                share = jnp.broadcast_to(share, (ROW, HEAD_DIM))
                inv[i, r * ROW : (r + 1) * ROW, at : at + HEAD_DIM] = share
                att[i, r * ROW : (r + 1) * ROW, at : at + HEAD_DIM] = (dot(low, v) * share).astype(bf16)
        mid = x[i, ROW:].astype(f32) + branch_scale * dot(att[i], wout[...])
        middle[i] = mid
        normed, factor = normalise(mid)
        n2[i] = normed.astype(bf16)
        r2[i] = jnp.broadcast_to(factor, (block, 128))
        here = pl.ds(pl.multiple_of(i * block, 64), block)
        h2[here] = (normed * gain_ffn + shift_ffn).astype(bf16)
        dbr[here] = (branch_scale * (alive_of(i) * cot[i].astype(f32))).astype(bf16)
        return _

    lax.fori_loop(0, items, attend, 0)

    partial[...] = jnp.zeros_like(partial)
    for c in range(chunks):
        cols = slice(c * D, (c + 1) * D)
        down = slice(c * 2 * D, c * 2 * D + D)
        up = slice(c * 2 * D + D, (c + 1) * 2 * D)

        def feed(t, _):
            here = pl.ds(pl.multiple_of(t * size, 128), size)
            u = dot(h2[here], wup[:, cols])
            back = dot(dbr[here], wdown[cols], 1, 1)
            square = u * u
            s = 0.5 * jnp.tanh(u * (gelu_in + gelu_cube * square)) + 0.5
            hidden = (u * s).astype(bf16)
            slope = s + u * ((s - s * s) * (2 * gelu_in + 6 * gelu_cube * square))
            before = (back * slope).astype(bf16)
            hid[here, cols] = hidden
            dpre[here, cols] = before
            partial[down] += dot(hidden, dbr[here], 0, 0)
            partial[up] += dot(h2[here], before, 0, 0)
            return _

        lax.fori_loop(0, steps, feed, 0)
        step(c, 0)
        if c >= 1:
            step(c - 1, 1)
        if c >= 2:
            step(c - 2, 2)
        if c >= 3:
            step(c - 3, 3)

    gvec[...] = jnp.zeros_like(gvec)
    last = parts[-1][0]

    def at_step(i, when, tasks):
        @pl.when(i == when)
        def _():
            for part, number in tasks:
                step(part, number)

    def middle_back(i, _):
        at_step(i, 2, [(3, 1), (2, 2), (1, 3), (0, 4)])
        at_step(i, 5, [(3, 2), (2, 3), (1, 4), (0, 5)])
        here = pl.ds(pl.multiple_of(i * block, 64), block)
        grad = dot(dpre[here], wup[...], 1, 1)
        normed = n2[i].astype(f32)
        gvec[16:24] += fold_rows(grad * normed)
        gvec[24:32] += fold_rows(grad)
        factor = jnp.concatenate([r2[i]] * 2, 1)
        grad = alive_of(i) * cot[i].astype(f32) + norm_back(grad, normed, factor, gain_ffn)
        dmid[i] = grad
        low = (branch_scale * grad).astype(bf16)
        partial[last + 3 * D :] += dot(att[i], low, 0, 0)
        datt[i] = dot(low, wout[...], 1, 1).astype(bf16)
        return _

    lax.fori_loop(0, items, middle_back, 0)

    def attend_back(i, _):
        at_step(i, 1, [(3, 3), (2, 4), (1, 5), (0, 6)])
        at_step(i, 3, [(3, 4), (2, 5), (1, 6)])
        at_step(i, 5, [(3, 5), (2, 6)])
        for h in range(HEADS):
            at = h * HEAD_DIM
            held_k = None
            held_v = None
            for r in range(rows):
                q = proj[i, (r + 1) * ROW : (r + 2) * ROW, at : at + HEAD_DIM]
                k = proj[i, r * ROW : (r + 2) * ROW, D + at : D + at + HEAD_DIM]
                v = proj[i, r * ROW : (r + 2) * ROW, 2 * D + at : 2 * D + at + HEAD_DIM]
                own = slice(r * ROW, (r + 1) * ROW)
                grad = datt[i, own, at : at + HEAD_DIM].astype(f32) * inv[i, own, at : at + HEAD_DIM]
                low = grad.astype(bf16)
                row_dot = jnp.sum(grad * att[i, own, at : at + HEAD_DIM].astype(f32), -1, keepdims=True)
                e = exps[i, r * HEADS + h, :, : 2 * ROW]
                ds = (e.astype(f32) * ((dot(low, v, 1, 1) - row_dot) * score_scale)).astype(bf16)
                dv = dot(e, low, 0, 0)
                dk = dot(ds, q, 0, 0)
                dproj[i, (r + 1) * ROW : (r + 2) * ROW, at : at + HEAD_DIM] = dot(ds, k).astype(bf16)
                first_k, first_v = dk[:ROW], dv[:ROW]
                if held_k is not None:
                    first_k += held_k
                    first_v += held_v
                dproj[i, r * ROW : (r + 1) * ROW, D + at : D + at + HEAD_DIM] = first_k.astype(bf16)
                dproj[i, r * ROW : (r + 1) * ROW, 2 * D + at : 2 * D + at + HEAD_DIM] = first_v.astype(bf16)
                held_k, held_v = dk[ROW:], dv[ROW:]
            dproj[i, rows * ROW :, D + at : D + at + HEAD_DIM] = held_k.astype(bf16)
            dproj[i, rows * ROW :, 2 * D + at : 2 * D + at + HEAD_DIM] = held_v.astype(bf16)
        dproj[i, :ROW, :D] = jnp.zeros((ROW, D), bf16)
        return _

    lax.fori_loop(0, items, attend_back, 0)

    def weight_back(i, _):
        for p in range(3):
            partial[last + p * D : last + (p + 1) * D] += dot(
                h1[i], dproj[i, :, p * D : (p + 1) * D], 0, 0
            )
        return _

    lax.fori_loop(0, items, weight_back, 0)
    step(4, 0)
    step(3, 6)

    def tokens_back(i, _):
        at_step(i, 2, [(4, 1)])
        grad = dot(dproj[i], wqkv[...], 1, 1)
        normed = n1[i].astype(f32)
        gvec[0:8] += fold_rows(grad * normed)
        gvec[8:16] += fold_rows(grad)
        factor = jnp.concatenate([r1[i]] * 2, 1)
        grad = norm_back(grad, normed, factor, gain_attn)
        ghalo[i] = grad[:ROW].astype(bf16)
        dmid[i] += grad[ROW:]
        return _

    lax.fori_loop(0, items, tokens_back, 0)
    ghalo_copy = pltpu.make_async_remote_copy(
        src_ref=ghalo,
        dst_ref=ghalo_in,
        send_sem=halo_sems.at[2],
        recv_sem=halo_sems.at[3],
        device_id=ahead,
        device_id_type=MESH,
    )
    ghalo_copy.start()

    def vec_copies(kind, number):
        result = []
        place = {"core": sums.core, "items": item, "z": sums.z}[kind]
        base = {"core": 0, "items": 1, "z": n_items}[kind]
        for s in sums.steps_of(kind):
            here = vec_buf.at[number, place]
            result.append(
                pltpu.make_async_remote_copy(
                    src_ref=here,
                    dst_ref=here,
                    send_sem=vec_sems.at[0, base + s - 1],
                    recv_sem=vec_sems.at[1, base + s - 1],
                    device_id=sums.partner(kind, s),
                    device_id_type=MESH,
                )
            )
        return result

    def vec_total(number, size):
        value = vec_buf[number, 0]
        for k in range(1, size):
            value += vec_buf[number, k]
        return value

    lines = [jnp.sum(gvec[8 * k : 8 * k + 8], 0, keepdims=True) for k in range(4)]
    vec_buf[0, sums.core] = jnp.concatenate(lines + [jnp.zeros((4, D), f32)], 0)
    sums.start(vec_copies("core", 0))

    def vec_step(number):
        if number == 1:
            sums.finish(vec_copies("core", 0))
            vec_buf[1, item] = vec_total(0, 2)
            sums.start(vec_copies("items", 1))
        if number == 2:
            sums.finish(vec_copies("items", 1))
            vec_buf[2, sums.z] = vec_total(1, n_items)
            sums.start(vec_copies("z", 2))
        if number == 3:
            sums.finish(vec_copies("z", 2))
            gvec[0:8] = vec_total(2, n_z)

    def finish(i, _):
        at_step(i, 1, [(4, 2)])
        here = pl.ds(pl.multiple_of(i * block, 64), block)
        branch = dot(hid[here], wdown[...])
        out[i] = (alive_of(i) * (middle[i] + branch_scale * branch)).astype(bf16)
        return _

    lax.fori_loop(0, items, finish, 0)
    out_copy = pltpu.make_async_copy(out, output_ref, store_sems.at[0])
    out_copy.start()
    vec_step(1)
    step(4, 3)
    ghalo_copy.wait()
    for i in range(items):
        dmid[i, block - ROW :] += ghalo_in[i].astype(f32)
    tok_copy = pltpu.make_async_copy(dmid, gtok_ref, store_sems.at[1])
    tok_copy.start()
    vec_step(2)
    step(4, 4)
    step(4, 5)
    vec_step(3)
    vec_copy = pltpu.make_async_copy(gvec.at[pl.ds(0, 8)], gvec_ref, store_sems.at[2])
    vec_copy.start()
    step(4, 6)
    grad_copy = pltpu.make_async_copy(full, grads_ref, store_sems.at[3])
    grad_copy.start()
    out_copy.wait()
    tok_copy.wait()
    vec_copy.wait()
    grad_copy.wait()


def split_kernel(
    raw_out,
    raw_tok,
    grads,
    gvec,
    output,
    gtok,
    gqkv,
    gout,
    gup,
    gdown,
    gain_attn,
    shift_attn,
    gain_ffn,
    shift_ffn,
    qkv,
    wout,
    up,
    down,
    sems,
):
    copies = [
        pltpu.make_async_copy(raw_tok, gtok, sems.at[0]),
        pltpu.make_async_copy(raw_out, output, sems.at[1]),
    ]
    for copy in copies:
        copy.start()
    chunks = up.shape[1] // D

    def send(source, target, number):
        copy = pltpu.make_async_copy(source, target, sems.at[number])
        copy.start()
        copies.append(copy)

    for c in range(chunks):
        down[c * D : (c + 1) * D] = grads[c * 2 * D : c * 2 * D + D].astype(f32)
    send(down, gdown, 2)
    for c in range(chunks):
        up[:, c * D : (c + 1) * D] = grads[c * 2 * D + D : (c + 1) * 2 * D].astype(f32)
    send(up, gup, 3)
    last = chunks * 2 * D
    for p in range(3):
        qkv[:, p * D : (p + 1) * D] = grads[last + p * D : last + (p + 1) * D].astype(f32)
    send(qkv, gqkv, 4)
    wout[...] = grads[last + 3 * D :].astype(f32)
    send(wout, gout, 5)
    gain_attn[...] = gvec[0:1]
    shift_attn[...] = gvec[1:2]
    gain_ffn[...] = gvec[2:3]
    shift_ffn[...] = gvec[3:4]
    for copy in copies:
        copy.wait()


def shards(
    seq_size,
    mesh_sizes,
    tokens,
    lengths,
    pad_mask,
    w_qkv,
    w_out,
    w_up,
    w_down,
    gain_attn,
    shift_attn,
    gain_ffn,
    shift_ffn,
    cotangent,
):
    items, block, width = tokens.shape
    rows = block // ROW
    total = items * block
    ff = w_up.shape[1]
    ext = block + ROW
    n_items, n_z = mesh_sizes
    grad_rows = 2 * ff + 4 * width
    half = grad_rows // 2
    links = n_items + n_z - 1
    vmem = pl.BlockSpec(memory_space=pltpu.VMEM)
    anywhere = pl.BlockSpec(memory_space=pl.ANY)
    raw = [
        jax.ShapeDtypeStruct((items, block, width), bf16),
        jax.ShapeDtypeStruct((items, block, width), f32),
        jax.ShapeDtypeStruct((grad_rows, width), bf16),
        jax.ShapeDtypeStruct((8, width), f32),
    ]
    vectors = [v.reshape(1, width) for v in (gain_attn, shift_attn, gain_ffn, shift_ffn)]
    parts = ff // width + 1
    vm = pltpu.VMEM
    raw = pl.pallas_call(
        functools.partial(layer_kernel, items, rows, mesh_sizes, seq_size),
        out_shape=raw,
        in_specs=[pl.BlockSpec(memory_space=pltpu.SMEM), vmem] + [anywhere] * 6 + [vmem] * 4,
        out_specs=[anywhere] * 4,
        scratch_shapes=[
            vm((items, ext, width), bf16),
            vm((items, block, width), bf16),
            vm((items, block, 128), f32),
            vm((rows, 8, 256), f32),
            vm((width, 3 * width), bf16),
            vm((width, width), bf16),
            vm((width, ff), bf16),
            vm((ff, width), bf16),
            vm((items, ext, width), bf16),
            vm((items, ext, width), bf16),
            vm((items, ext, 128), f32),
            vm((items, ext, 3 * width), bf16),
            vm((items, rows * HEADS, ROW, 256), bf16),
            vm((items, block, width), f32),
            vm((items, block, width), bf16),
            vm((items, block, width), f32),
            vm((items, block, width), bf16),
            vm((items, block, 128), f32),
            vm((total, width), bf16),
            vm((total, width), bf16),
            vm((total, ff), bf16),
            vm((total, ff), bf16),
            vm((items, block, width), f32),
            vm((items, block, width), bf16),
            vm((items, ext, 3 * width), bf16),
            vm((items, ROW, width), bf16),
            vm((items, ROW, width), bf16),
            vm((items, block, width), bf16),
            vm((32, width), f32),
            vm((3, max(n_items, n_z), 8, width), f32),
            vm((grad_rows, width), f32),
            vm((half, width), bf16),
            vm((half, width), bf16),
            vm((half, width), bf16),
            vm((n_items - 1, half // n_items, width), bf16),
            vm((half // n_items, width), bf16),
            vm((n_z, half // n_items, width), bf16),
            vm((grad_rows, width), bf16),
            pltpu.SemaphoreType.DMA((5 + items,)),
            pltpu.SemaphoreType.DMA((4,)),
            pltpu.SemaphoreType.DMA((4,)),
            pltpu.SemaphoreType.DMA((2, links)),
            pltpu.SemaphoreType.DMA((2 * parts, links)),
            pltpu.SemaphoreType.DMA((2 * parts, links)),
        ],
        compiler_params=pltpu.CompilerParams(
            vmem_limit_bytes=63 * 2**20, collective_id=0, has_side_effects=True
        ),
    )(lengths, pad_mask, tokens, cotangent, w_qkv, w_out, w_up, w_down, *vectors)
    shapes = [
        jax.ShapeDtypeStruct((items, block, width), bf16),
        jax.ShapeDtypeStruct((items, block, width), f32),
        jax.ShapeDtypeStruct((width, 3 * width), f32),
        jax.ShapeDtypeStruct((width, width), f32),
        jax.ShapeDtypeStruct((width, ff), f32),
        jax.ShapeDtypeStruct((ff, width), f32),
    ] + [jax.ShapeDtypeStruct((1, width), f32)] * 4
    outs = pl.pallas_call(
        split_kernel,
        out_shape=shapes,
        in_specs=[anywhere] * 2 + [vmem] * 2,
        out_specs=[anywhere] * 6 + [vmem] * 4,
        scratch_shapes=[
            vm((width, 3 * width), f32),
            vm((width, width), f32),
            vm((width, ff), f32),
            vm((ff, width), f32),
            pltpu.SemaphoreType.DMA((6,)),
        ],
        compiler_params=pltpu.CompilerParams(vmem_limit_bytes=16 * 2**20),
    )(*raw)
    return tuple(outs[:6]) + tuple(v.reshape(width) for v in outs[6:])


def solution(mesh):
    split = P("items", "seq", None)
    seq_size = mesh.shape["seq"]
    mesh_sizes = (mesh.shape["items"], seq_size // 2)
    return jax.shard_map(
        functools.partial(shards, seq_size, mesh_sizes),
        mesh=mesh,
        in_specs=(split, P("items"), P("items", None)) + (P(),) * 8 + (split,),
        out_specs=(split, split) + (P(),) * 8,
        check_vma=False,
    )
```

```python
import functools
import math

import jax
import jax.numpy as jnp
from jax import lax
from jax.experimental import pallas as pl
from jax.experimental.pallas import tpu as pltpu
from jax.sharding import PartitionSpec as P

HEADS = 2
HEAD_DIM = 128
ROW = 96
D = HEADS * HEAD_DIM

epsilon = 1e-05
branch_scale = 0.7071067811865476
masked_value = -1e30
score_scale = HEAD_DIM ** (-0.5)
log2e = math.log2(math.e)
gelu_in = math.sqrt(2 / math.pi)
gelu_cube = gelu_in * 0.044715
f32 = jnp.float32
bf16 = jnp.bfloat16


def dot(left, right, left_dim=1, right_dim=0):
    return lax.dot_general(
        left, right, (((left_dim,), (right_dim,)), ((), ())), preferred_element_type=f32
    )


def normalise(inputs):
    average = jnp.mean(inputs, -1, keepdims=True)
    centred = inputs - average
    spread = jnp.mean(centred * centred, -1, keepdims=True)
    factor = lax.rsqrt(spread + epsilon)
    return centred * factor, factor


def norm_back(grad, normed, factor, gain):
    e = grad * gain
    first = jnp.mean(e, -1, keepdims=True)
    second = jnp.mean(e * normed, -1, keepdims=True)
    return factor * (e - first - normed * second)


def fold_rows(values):
    count = values.shape[0] // 8
    return jnp.sum(values.reshape(count, 8, values.shape[1]), 0)


class Sums:
    def __init__(self, mesh_sizes, refs):
        (self.partial, self.c_out, self.c_in, self.i_out, self.i_in, self.z_out, self.z_in,
         self.d_in, self.full, self.send, self.recv) = refs
        self.n_items, self.n_z = mesh_sizes
        self.item = lax.axis_index("items")
        seq = lax.axis_index("seq")
        self.core = lax.rem(seq, 2)
        self.z = seq // 2

    def partner(self, kind, step):
        if kind == "core":
            return {"items": self.item, "seq": self.z * 2 + 1 - self.core}
        item, z = self.spot(kind, step)
        return {"items": item, "seq": z * 2 + self.core}

    def spot(self, kind, step):
        items_step, z_step = {
            "items": (step, 0),
            "z": (0, step),
            "plane": (step // self.n_z, step % self.n_z),
        }[kind]
        return (
            lax.rem(self.item + items_step, self.n_items),
            lax.rem(self.z + z_step, self.n_z),
        )

    def steps_of(self, kind):
        counts = {"core": 2, "items": self.n_items, "z": self.n_z, "plane": self.n_items * self.n_z}
        return range(1, counts[kind])

    def copies(self, part, phase, kind, source, target):
        result = []
        base = {"core": 0, "items": 1, "z": self.n_items, "plane": 1}[kind]
        for step in self.steps_of(kind):
            slot = (part * 2 + phase, base + step - 1)
            result.append(
                pltpu.make_async_remote_copy(
                    src_ref=source(step),
                    dst_ref=target(step),
                    send_sem=self.send.at[slot],
                    recv_sem=self.recv.at[slot],
                    device_id=self.partner(kind, step),
                    device_id_type=pl.DeviceIdType.MESH,
                )
            )
        return result

    def start(self, copies):
        for copy in copies:
            copy.start()

    def finish(self, copies):
        for copy in copies:
            copy.wait_recv()
        for copy in copies:
            copy.wait_send()

    def place(self, first, rows):
        half = rows // 2
        quarter = half // self.n_items
        split = quarter % (16 * self.n_z) == 0
        last = quarter // self.n_z if split else quarter
        return half, quarter, split, last

    def first_copies(self, part, first, rows):
        half, _, _, _ = self.place(first, rows)
        here = pl.ds(first // 2, half)
        return self.copies(part, 0, "core", lambda s: self.c_out.at[here], lambda s: self.c_in.at[here])

    def items_copies(self, part, first, rows):
        half, quarter, _, _ = self.place(first, rows)

        def source(step):
            to = lax.rem(self.item + step, self.n_items)
            return self.i_out.at[pl.ds(pl.multiple_of(first // 2 + to * quarter, 16), quarter)]

        at = pl.ds(first // 2 // self.n_items, quarter)
        return self.copies(part, 0, "items", source, lambda s: self.i_in.at[s - 1, at])

    def z_copies(self, part, first, rows):
        half, quarter, split, last = self.place(first, rows)
        base = first // 2 // self.n_items
        if split:
            def source(step):
                to = lax.rem(self.z + step, self.n_z)
                return self.z_out.at[pl.ds(pl.multiple_of(base + to * last, 16), last)]

            at = pl.ds(base // self.n_z, last)
            return self.copies(part, 0, "z", source, lambda s: self.z_in.at[s - 1, at])
        at = pl.ds(base, quarter)
        return self.copies(part, 0, "z", lambda s: self.z_out.at[at], lambda s: self.z_in.at[self.z, at])

    def plane_copies(self, part, first, rows):
        count = rows // 2 // (self.n_items * self.n_z)

        def source(step):
            item, z = self.spot("plane", step)
            at = first // 2 + (item * self.n_z + z) * count
            return self.i_out.at[pl.ds(pl.multiple_of(at, 16), count)]

        at = pl.ds(first // 2 // (self.n_items * self.n_z), count)
        return self.copies(part, 0, "plane", source, lambda s: self.d_in.at[s - 1, at])

    def held(self, first, rows, level):
        half, quarter, split, last = self.place(first, rows)
        at = first + self.core * half
        count = half
        if level > 0:
            at += self.item * quarter
            count = quarter
        if level > 1 and split:
            at += self.z * last
            count = last
        return self.full.at[pl.ds(pl.multiple_of(at, 16), count)]

    def back_copies(self, part, first, rows, kind):
        level = {"core": 0, "items": 1, "z": 2, "plane": 2}[kind]
        ref = self.held(first, rows, level)
        return self.copies(part, 1, kind, lambda s: ref, lambda s: ref)

    def plane_step(self, part, first, rows, number):
        count = rows // 2 // (self.n_items * self.n_z)
        base = first // 2
        if number == 2:
            self.finish(self.plane_copies(part, first, rows))
            own = base + (self.item * self.n_z + self.z) * count
            value = self.i_out[pl.ds(pl.multiple_of(own, 16), count)].astype(f32)
            at = pl.ds(base // (self.n_items * self.n_z), count)
            for step in self.steps_of("plane"):
                value += self.d_in[step - 1, at].astype(f32)
            self.held(first, rows, 2)[...] = value.astype(bf16)
            self.start(self.back_copies(part, first, rows, "plane"))
        if number == 3:
            self.finish(self.back_copies(part, first, rows, "plane"))
            self.start(self.back_copies(part, first, rows, "core"))
        if number == 4:
            self.finish(self.back_copies(part, first, rows, "core"))

    def step(self, part, first, rows, number, plane=False):
        if plane and number > 1:
            self.plane_step(part, first, rows, number)
            return
        half, quarter, split, last = self.place(first, rows)
        base_c = first // 2
        base_i = base_c // self.n_items
        if number == 0:
            away = pl.ds(pl.multiple_of(first + (1 - self.core) * half, 16), half)
            self.c_out[pl.ds(base_c, half)] = self.partial[away].astype(bf16)
            self.start(self.first_copies(part, first, rows))
        if number == 1:
            self.finish(self.first_copies(part, first, rows))
            here = pl.ds(base_c, half)
            own = pl.ds(pl.multiple_of(first + self.core * half, 16), half)
            self.i_out[here] = (self.partial[own] + self.c_in[here].astype(f32)).astype(bf16)
            if plane:
                self.start(self.plane_copies(part, first, rows))
            else:
                self.start(self.items_copies(part, first, rows))
        if number == 2:
            self.finish(self.items_copies(part, first, rows))
            own = pl.ds(pl.multiple_of(base_c + self.item * quarter, 16), quarter)
            at = pl.ds(base_i, quarter)
            value = self.i_out[own].astype(f32)
            for step in self.steps_of("items"):
                value += self.i_in[step - 1, at].astype(f32)
            self.z_out[at] = value.astype(bf16)
            if not split:
                self.z_in[self.z, at] = value.astype(bf16)
            self.start(self.z_copies(part, first, rows))
        if number == 3:
            self.finish(self.z_copies(part, first, rows))
            if split:
                own = pl.ds(pl.multiple_of(base_i + self.z * last, 16), last)
                at = pl.ds(base_i // self.n_z, last)
                value = self.z_out[own].astype(f32)
                for step in self.steps_of("z"):
                    value += self.z_in[step - 1, at].astype(f32)
            else:
                at = pl.ds(base_i, quarter)
                value = self.z_in[0, at].astype(f32)
                for step in self.steps_of("z"):
                    value += self.z_in[step, at].astype(f32)
            self.held(first, rows, 2)[...] = value.astype(bf16)
            if split:
                self.start(self.back_copies(part, first, rows, "z"))
            else:
                self.start(self.back_copies(part, first, rows, "items"))
        if number == 4 and split:
            self.finish(self.back_copies(part, first, rows, "z"))
            self.start(self.back_copies(part, first, rows, "items"))
        if number == 5:
            self.finish(self.back_copies(part, first, rows, "items"))
            self.start(self.back_copies(part, first, rows, "core"))
        if number == 6:
            self.finish(self.back_copies(part, first, rows, "core"))


def layer_kernel(
    items,
    rows,
    mesh_sizes,
    seq_size,
    lengths_ref,
    pad_ref,
    tokens_ref,
    cot_hbm,
    wqkv_hbm,
    wout_hbm,
    wup_hbm,
    wdown_hbm,
    gain_attn_ref,
    shift_attn_ref,
    gain_ffn_ref,
    shift_ffn_ref,
    output_ref,
    gtok_ref,
    grads_ref,
    gvec_ref,
    x,
    cot,
    alive,
    keys,
    wqkv,
    wout,
    wup,
    wdown,
    h1,
    n1,
    r1,
    proj,
    exps,
    inv,
    att,
    middle,
    n2,
    r2,
    h2,
    dbr,
    hid,
    dpre,
    dmid,
    datt,
    dproj,
    ghalo,
    ghalo_in,
    out,
    gvec,
    vec_buf,
    partial,
    c_out,
    c_in,
    i_out,
    i_in,
    z_out,
    z_in,
    d_in,
    full,
    load_sems,
    store_sems,
    halo_sems,
    vec_sems,
    send_sems,
    recv_sems,
):
    block = rows * ROW
    total = items * block
    gain_attn = gain_attn_ref[...]
    shift_attn = shift_attn_ref[...]
    gain_ffn = gain_ffn_ref[...]
    shift_ffn = shift_ffn_ref[...]
    ff = wup.shape[1]
    chunks = ff // D
    n_items, n_z = mesh_sizes
    item = lax.axis_index("items")
    seq = lax.axis_index("seq")
    MESH = pl.DeviceIdType.MESH
    sums = Sums(
        mesh_sizes, (partial, c_out, c_in, i_out, i_in, z_out, z_in, d_in, full, send_sems, recv_sems)
    )
    parts = [(c * 2 * D, 2 * D) for c in range(chunks + HEADS)]
    direct = D % (16 * n_items * n_z) == 0

    def step(part, number):
        sums.step(part, *parts[part], number, plane=direct and part >= chunks)

    after = {"items": item, "seq": lax.rem(seq + 1, seq_size)}
    ahead = {"items": item, "seq": lax.rem(seq + seq_size - 1, seq_size)}
    barrier = pltpu.get_barrier_semaphore()
    greeted = [after, ahead]
    for kind in ("core", "plane") if direct else ("core", "items", "z"):
        greeted += [sums.partner(kind, s) for s in sums.steps_of(kind)]
    for device in greeted:
        pl.semaphore_signal(barrier, inc=1, device_id=device, device_id_type=MESH)

    loads = [
        (wout_hbm, wout),
        (wup_hbm, wup),
        (wdown_hbm, wdown),
        (cot_hbm, cot),
    ]
    token_loads = [
        pltpu.make_async_copy(tokens_ref.at[i], x.at[i, pl.ds(ROW, block)], load_sems.at[4 + i])
        for i in range(items)
    ]
    weight_loads = [
        pltpu.make_async_copy(source, target, load_sems.at[k])
        for k, (source, target) in enumerate(loads)
    ]
    qkv_loads = [
        pltpu.make_async_copy(
            wqkv_hbm.at[:, pl.ds(p * D + h * HEAD_DIM, HEAD_DIM)],
            wqkv.at[:, pl.ds((h * 3 + p) * HEAD_DIM, HEAD_DIM)],
            load_sems.at[4 + items + h * 3 + p],
        )
        for h in range(HEADS)
        for p in range(3)
    ]
    for copy in qkv_loads:
        copy.start()
    for copy in token_loads:
        copy.start()
    for copy in weight_loads:
        copy.start()

    pl.semaphore_wait(barrier, len(greeted))
    halo_copy = pltpu.make_async_remote_copy(
        src_ref=tokens_ref.at[:, pl.ds(block - ROW, ROW)],
        dst_ref=x.at[:, pl.ds(0, ROW)],
        send_sem=halo_sems.at[0],
        recv_sem=halo_sems.at[1],
        device_id=after,
        device_id_type=MESH,
    )
    halo_copy.start()

    first_pos = seq * block

    def window(start, width):
        spots = sorted({(s * block + (start if s else 0)) % 128 for s in range(seq_size)})
        if start:
            spots = sorted({(s * block + start) % 128 for s in range(1, seq_size)})
        at = jnp.maximum(first_pos + start, 0)
        low = pl.multiple_of(at // 128 * 128, 128)
        wide = (spots[-1] + width + 127) // 128 * 128
        held = pad_ref[:, pl.ds(low, wide)]
        result = held[:, spots[0] : spots[0] + width]
        for spot in spots[1:]:
            result = jnp.where(at % 128 == spot, held[:, spot : spot + width], result)
        return result

    count = jnp.zeros((items, 1), jnp.int32)
    which = lax.broadcasted_iota(jnp.int32, (items, 1), 0)
    for i in range(items):
        count = jnp.where(which == i, lengths_ref[i], count)

    def there(start, width):
        position = first_pos + start + lax.broadcasted_iota(jnp.int32, (items, width), 1)
        good = (position >= 0) & (position < count) & (window(start, width) == 1)
        return jnp.where(good, 1.0, 0.0)

    row_there = [there((r - 1) * ROW, ROW) for r in range(rows + 1)]
    spread = lax.broadcasted_iota(jnp.int32, (items, items * 128), 1) // 128
    spread = jnp.where(spread == lax.broadcasted_iota(jnp.int32, (items, items * 128), 0), 1.0, 0.0)
    for r in range(rows):
        both = jnp.concatenate([row_there[r], row_there[r + 1]], 1)
        keys[r, :items, : 2 * ROW] = (1.0 - both) * masked_value
        column = dot(row_there[r + 1].astype(bf16), spread.astype(bf16), 0, 0)
        for i in range(items):
            alive[i, r * ROW : (r + 1) * ROW] = column[:, i * 128 : (i + 1) * 128]

    def alive_of(i):
        mask = alive[i]
        return jnp.concatenate([mask, mask], 1)

    def first_norm(values):
        normed, factor = normalise(values)
        return (normed * gain_attn + shift_attn).astype(bf16), normed.astype(bf16), factor

    for copy in qkv_loads:
        copy.wait()
    pair = 2 if items % 2 == 0 else 1

    def project(p, _):
        for j in range(pair):
            pltpu.make_async_copy(
                tokens_ref.at[p * pair + j],
                x.at[p * pair + j, pl.ds(ROW, block)],
                load_sems.at[4 + p * pair + j],
            ).wait()
        found = [first_norm(x[p * pair + j, ROW:].astype(f32)) for j in range(pair)]
        results = [dot(low, wqkv[...]).astype(bf16) for low, _, _ in found]
        for j in range(pair):
            low, normed, factor = found[j]
            h1[p * pair + j, ROW:] = low
            n1[p * pair + j, ROW:] = normed
            r1[p * pair + j, ROW:] = jnp.broadcast_to(factor, (block, 128))
            proj[p * pair + j, ROW:] = results[j]
        return _

    lax.fori_loop(0, items // pair, project, 0)
    query_pos = lax.broadcasted_iota(jnp.int32, (ROW, 2 * ROW), 0)
    key_pos = lax.broadcasted_iota(jnp.int32, (ROW, 2 * ROW), 1) - ROW
    causal = jnp.where(key_pos <= query_pos, 0.0, masked_value)
    itself = jnp.where(key_pos == query_pos, 0.0, masked_value)
    for copy in weight_loads:
        copy.wait()

    def part_of(whole, r, count, number, h):
        at = (h * 3 + number) * HEAD_DIM
        return whole[r * ROW : (r + count) * ROW, at : at + HEAD_DIM]

    def weigh(mine, keys_of, units):
        biases = {r: jnp.maximum(jnp.minimum(causal, keys_of(r)), itself) for r, _ in units}
        scores = [
            dot(part_of(mine, r + 1, 1, 0, h), part_of(mine, r, 2, 1, h), 1, 1)
            * (score_scale * log2e)
            + biases[r]
            for r, h in units
        ]
        es = [jnp.exp2(one - jnp.max(one, -1, keepdims=True)) for one in scores]
        shares = [
            jnp.broadcast_to(1.0 / jnp.sum(e, -1, keepdims=True), (ROW, HEAD_DIM)) for e in es
        ]
        lows = [e.astype(bf16) for e in es]
        results = [
            (dot(e, part_of(mine, r, 2, 2, h)) * share).astype(bf16)
            for e, share, (r, h) in zip(lows, shares, units)
        ]
        return lows, shares, results

    def heads(values):
        return jnp.concatenate(values, 1)

    def attend(p, _):
        units = [(r, h) for r in range(1, rows) for h in range(HEADS)]
        found = []
        for j in range(pair):
            i = p * pair + j
            found.append(weigh(proj[i], lambda r: keys[r, pl.ds(i, 1), : 2 * ROW], units))
        for j in range(pair):
            i = p * pair + j
            lows, shares, results = found[j]
            for (r, h), e in zip(units, lows):
                exps[i, r * HEADS + h, :, : 2 * ROW] = e
            for r in range(1, rows):
                at = (r - 1) * HEADS
                inv[i, r * ROW : (r + 1) * ROW] = heads(shares[at : at + HEADS])
                att[i, r * ROW : (r + 1) * ROW] = heads(results[at : at + HEADS])
        return _

    if rows > 1:
        lax.fori_loop(0, items // pair, attend, 0)
    halo_copy.wait()

    def project_halo(p, _):
        low, normed, factor = first_norm(x[:, :ROW].astype(f32).reshape(items * ROW, D))
        results = [
            dot(low, wqkv[:, (h * 3 + 1) * HEAD_DIM : (h * 3 + 3) * HEAD_DIM]).astype(bf16)
            for h in range(HEADS)
        ]
        h1[:, :ROW] = low.reshape(items, ROW, D)
        n1[:, :ROW] = normed.reshape(items, ROW, D)
        r1[:, :ROW] = jnp.broadcast_to(factor, (items * ROW, 128)).reshape(items, ROW, 128)
        for h in range(HEADS):
            at = (h * 3 + 1) * HEAD_DIM
            proj[:, :ROW, at : at + 2 * HEAD_DIM] = results[h].reshape(items, ROW, 2 * HEAD_DIM)
        return _

    lax.fori_loop(0, 1, project_halo, 0)

    def attend_first(p, _):
        units = [(0, h) for h in range(HEADS)]
        found = []
        for j in range(pair):
            i = p * pair + j
            others = att[i, ROW:]
            inputs = x[i, ROW:].astype(f32)
            grad = (branch_scale * (alive_of(i) * cot[i].astype(f32))).astype(bf16)
            lows, shares, results = weigh(
                proj[i, : 2 * ROW], lambda r: keys[r, pl.ds(i, 1), : 2 * ROW], units
            )
            result = heads(results)
            whole = jnp.concatenate([result, others], 0) if rows > 1 else result
            mid = inputs + branch_scale * dot(whole, wout[...])
            normed, factor = normalise(mid)
            low = (normed * gain_ffn + shift_ffn).astype(bf16)
            found.append((lows, shares, result, mid, normed.astype(bf16), factor, low, grad))
        for j in range(pair):
            i = p * pair + j
            lows, shares, result, mid, normed, factor, low, grad = found[j]
            here = pl.ds(pl.multiple_of(i * block, 64), block)
            for h in range(HEADS):
                exps[i, h, :, : 2 * ROW] = lows[h]
            inv[i, :ROW] = heads(shares)
            att[i, :ROW] = result
            middle[i] = mid
            n2[i] = normed
            r2[i] = jnp.broadcast_to(factor, (block, 128))
            h2[here] = low
            dbr[here] = grad
        return _

    lax.fori_loop(0, items // pair, attend_first, 0)

    for c in range(chunks):
        cols = slice(c * D, (c + 1) * D)
        down = slice(c * 2 * D, c * 2 * D + D)
        up = slice(c * 2 * D + D, (c + 1) * 2 * D)

        def feed(t, _):
            normed = h2[...]
            grad = dbr[...]
            u = dot(normed, wup[:, cols])
            back = dot(grad, wdown[cols], 1, 1)
            square = u * u
            s = 0.5 * jnp.tanh(u * (gelu_in + gelu_cube * square)) + 0.5
            hidden = (u * s).astype(bf16)
            slope = s + u * ((s - s * s) * (2 * gelu_in + 6 * gelu_cube * square))
            before = (back * slope).astype(bf16)
            down_grad = dot(hidden, grad, 0, 0)
            up_grad = dot(normed, before, 0, 0)
            hid[:, cols] = hidden
            dpre[:, cols] = before
            partial[down] = down_grad
            partial[up] = up_grad
            return _

        lax.fori_loop(0, 1, feed, 0)
        step(c, 0)
        if c >= 1:
            step(c - 1, 1)

    gvec[...] = jnp.zeros_like(gvec)
    last = chunks * 2 * D

    def at_step(i, when, tasks):
        @pl.when(i == when)
        def _():
            for part, number in tasks:
                step(part, number)

    for h in range(HEADS):
        at = last + h * 2 * D + D
        partial[at : at + D, HEAD_DIM:] = jnp.zeros((D, HEAD_DIM), f32)

    def middle_back(p, _):
        at_step(p, 1, [(3, 1), (0, 2)])
        at_step(p, 2, [(1, 2)])
        here = pl.ds(pl.multiple_of(p * pair * block, 64), pair * block)
        grads = dpre[here]
        found = []
        for j in range(pair):
            i = p * pair + j
            normed = n2[i].astype(f32)
            factor = jnp.concatenate([r2[i]] * 2, 1)
            outer = alive_of(i) * cot[i].astype(f32)
            attended = att[i]
            grad = dot(grads[j * block : (j + 1) * block], wup[...], 1, 1)
            sums_here = fold_rows(grad * normed), fold_rows(grad)
            grad = outer + norm_back(grad, normed, factor, gain_ffn)
            low = (branch_scale * grad).astype(bf16)
            found.append((grad, low, attended, sums_here))
        lows = jnp.concatenate([f[1] for f in found], 0)
        out_grad = dot(jnp.concatenate([f[2] for f in found], 0), lows, 0, 0)
        back = dot(lows, wout[...], 1, 1).astype(bf16)
        for j in range(pair):
            dmid[p * pair + j] = found[j][0]
            datt[p * pair + j] = back[j * block : (j + 1) * block]
        for h in range(HEADS):
            at = last + h * 2 * D + D
            partial[at : at + D, HEAD_DIM:] += out_grad[:, h * HEAD_DIM : (h + 1) * HEAD_DIM]
        gvec[16:24] += sum(f[3][0] for f in found)
        gvec[24:32] += sum(f[3][1] for f in found)
        return _

    lax.fori_loop(0, items // pair, middle_back, 0)

    def attend_back(h, p, _):
        at = h * 3 * HEAD_DIM
        lanes = slice(h * HEAD_DIM, (h + 1) * HEAD_DIM)
        found = []
        for j in range(pair):
            i = p * pair + j
            mine = proj[i, :, at : at + 3 * HEAD_DIM]
            es = [exps[i, r * HEADS + h, :, : 2 * ROW] for r in range(rows)]
            scaled = datt[i, :, lanes].astype(f32) * inv[i, :, lanes]
            product = scaled * att[i, :, lanes].astype(f32)
            low = scaled.astype(bf16)
            dqs, dks, dvs = [], [], []
            dps = [
                dot(low[r * ROW : (r + 1) * ROW], part_of(mine, r, 2, 2, 0), 1, 1)
                for r in range(rows)
            ]
            dss = []
            for r in range(rows):
                row_dot = jnp.sum(product[r * ROW : (r + 1) * ROW], -1, keepdims=True)
                dss.append((es[r].astype(f32) * ((dps[r] - row_dot) * score_scale)).astype(bf16))
            dvs = [dot(es[r], low[r * ROW : (r + 1) * ROW], 0, 0) for r in range(rows)]
            dks = [dot(dss[r], part_of(mine, r + 1, 1, 0, 0), 0, 0) for r in range(rows)]
            dqs = [dot(dss[r], part_of(mine, r, 2, 1, 0)).astype(bf16) for r in range(rows)]

            def gather(grads):
                lines = []
                for r in range(rows + 1):
                    value = 0.0
                    if r < rows:
                        value = grads[r][:ROW]
                    if r > 0:
                        value += grads[r - 1][ROW:]
                    lines.append(value.astype(bf16))
                return jnp.concatenate(lines, 0)

            found.append((jnp.concatenate(dqs, 0), gather(dks), gather(dvs)))
        for j in range(pair):
            i = p * pair + j
            dproj[i, :ROW, at : at + HEAD_DIM] = jnp.zeros((ROW, HEAD_DIM), bf16)
            dproj[i, ROW:, at : at + HEAD_DIM] = found[j][0]
            dproj[i, :, at + HEAD_DIM : at + 2 * HEAD_DIM] = found[j][1]
            dproj[i, :, at + 2 * HEAD_DIM : at + 3 * HEAD_DIM] = found[j][2]
        return _

    def weight_back(h, p, _):
        left = h1[...].reshape(items * (block + ROW), D)
        at = h * 3 * HEAD_DIM
        right = dproj[:, :, at : at + 3 * HEAD_DIM].reshape(items * (block + ROW), 3 * HEAD_DIM)
        grad = dot(left, right, 0, 0)
        start = last + h * 2 * D
        partial[start : start + D] = grad[:, :D]
        partial[start + D : start + 2 * D, :HEAD_DIM] = grad[:, D:]
        return _

    for h in range(HEADS):

        def back(p, _):
            if h == 0:
                at_step(p, 0, [(2, 2)])
                at_step(p, 1, [(0, 3)])
                at_step(p, 2, [(3, 2)])
            else:
                at_step(p, 0, [(1, 3)])
                at_step(p, 1, [(chunks, 1), (2, 3)])
                at_step(p, 2, [(0, 4)])
            return attend_back(h, p, _)

        lax.fori_loop(0, items // pair, back, 0)
        lax.fori_loop(0, 1, functools.partial(weight_back, h), 0)
        step(chunks + h, 0)
    step(3, 3)
    step(1, 4)

    def tokens_back(p, _):
        at_step(p, 1, [(chunks + 1, 1), (2, 4)])
        at_step(p, 2, [(chunks, 2), (0, 5)])
        found = []
        for j in range(pair):
            i = p * pair + j
            grad = dot(dproj[i], wqkv[...], 1, 1)
            normed = n1[i].astype(f32)
            factor = jnp.concatenate([r1[i]] * 2, 1)
            sums_here = fold_rows(grad * normed), fold_rows(grad)
            grad = norm_back(grad, normed, factor, gain_attn)
            found.append((grad[:ROW].astype(bf16), dmid[i] + grad[ROW:], sums_here))
        for j in range(pair):
            ghalo[p * pair + j] = found[j][0]
            dmid[p * pair + j] = found[j][1]
        gvec[0:8] += sum(f[2][0] for f in found)
        gvec[8:16] += sum(f[2][1] for f in found)
        return _

    lax.fori_loop(0, items // pair, tokens_back, 0)
    ghalo_copy = pltpu.make_async_remote_copy(
        src_ref=ghalo,
        dst_ref=ghalo_in,
        send_sem=halo_sems.at[2],
        recv_sem=halo_sems.at[3],
        device_id=ahead,
        device_id_type=MESH,
    )
    ghalo_copy.start()

    own_copy = None
    if rows > 1:
        own = pl.ds(0, block - ROW)
        own_copy = pltpu.make_async_copy(dmid.at[:, own], gtok_ref.at[:, own], store_sems.at[5])
        own_copy.start()

    def vec_copies(kind, number):
        result = []
        place = {"core": sums.core, "items": item, "z": sums.z}[kind]
        base = {"core": 0, "items": 1, "z": n_items}[kind]
        for s in sums.steps_of(kind):
            here = vec_buf.at[number, place]
            result.append(
                pltpu.make_async_remote_copy(
                    src_ref=here,
                    dst_ref=here,
                    send_sem=vec_sems.at[0, base + s - 1],
                    recv_sem=vec_sems.at[1, base + s - 1],
                    device_id=sums.partner(kind, s),
                    device_id_type=MESH,
                )
            )
        return result

    def vec_total(number, size):
        value = vec_buf[number, 0]
        for k in range(1, size):
            value += vec_buf[number, k]
        return value

    lines = [jnp.sum(gvec[8 * k : 8 * k + 8], 0, keepdims=True) for k in range(4)]
    vec_buf[0, sums.core] = jnp.concatenate(lines + [jnp.zeros((4, D), f32)], 0)
    sums.start(vec_copies("core", 0))

    def vec_step(number):
        if number == 1:
            sums.finish(vec_copies("core", 0))
            vec_buf[1, item] = vec_total(0, 2)
            sums.start(vec_copies("items", 1))
        if number == 2:
            sums.finish(vec_copies("items", 1))
            vec_buf[2, sums.z] = vec_total(1, n_items)
            sums.start(vec_copies("z", 2))
        if number == 3:
            sums.finish(vec_copies("z", 2))
            gvec[0:8] = vec_total(2, n_z)

    def finish(p, _):
        at_step(p, 0, [(3, 4), (1, 5)])
        at_step(p, 2, [(chunks + 1, 2)])
        here = pl.ds(pl.multiple_of(p * pair * block, 64), pair * block)
        branch = dot(hid[here], wdown[...])
        results = [
            (alive_of(p * pair + j) * (middle[p * pair + j] + branch_scale * branch[j * block : (j + 1) * block])).astype(bf16)
            for j in range(pair)
        ]
        for j in range(pair):
            out[p * pair + j] = results[j]
        return _

    lax.fori_loop(0, items // pair, finish, 0)
    out_copy = pltpu.make_async_copy(out, output_ref, store_sems.at[0])
    out_copy.start()
    step(2, 5)
    vec_step(1)
    ghalo_copy.wait()
    tail = block - ROW
    for i in range(items):
        dmid[i, tail:] += ghalo_in[i].astype(f32)
    tok_copy = pltpu.make_async_copy(dmid.at[:, pl.ds(tail, ROW)], gtok_ref.at[:, pl.ds(tail, ROW)], store_sems.at[1])
    tok_copy.start()
    step(0, 6)
    step(1, 6)
    step(3, 5)
    vec_step(2)
    stores = []
    if direct:
        order = [(chunks, 3), (2, 6), (3, 6), (chunks + 1, 3)]
    else:
        order = [(2, 6), (3, 6)]
        order += [(chunks + h, n) for n in (3, 4, 5) for h in range(HEADS)]
    for part, number in order:
        step(part, number)
    vec_step(3)
    vec_copy = pltpu.make_async_copy(gvec.at[pl.ds(0, 8)], gvec_ref, store_sems.at[2])
    vec_copy.start()
    early = pl.ds(0, last)
    early_copy = pltpu.make_async_copy(full.at[early], grads_ref.at[early], store_sems.at[3])
    early_copy.start()
    for h in range(HEADS):
        step(chunks + h, 4 if direct else 6)
    late = pl.ds(last, HEADS * 2 * D)
    late_copy = pltpu.make_async_copy(full.at[late], grads_ref.at[late], store_sems.at[4])
    late_copy.start()
    for copy in (out_copy, own_copy, tok_copy, vec_copy, early_copy, late_copy):
        if copy is not None:
            copy.wait()


def split_kernel(
    raw_out,
    raw_tok,
    raw_grads,
    raw_vec,
    output,
    gtok,
    gqkv,
    gout,
    gup,
    gdown,
    gain_attn,
    shift_attn,
    gain_ffn,
    shift_ffn,
    held_out,
    held_tok,
    grads,
    gvec,
    qkv,
    wout,
    up,
    down,
    load_sems,
    store_sems,
):
    chunks = up.shape[1] // D
    items = raw_tok.shape[0]
    last = chunks * 2 * D
    stores = []

    def load(source, target, number):
        copy = pltpu.make_async_copy(source, target, load_sems.at[number])
        copy.start()
        return copy

    def store(source, target):
        copy = pltpu.make_async_copy(source, target, store_sems.at[len(stores)])
        copy.start()
        stores.append(copy)

    early = load(raw_grads.at[pl.ds(0, last)], grads.at[pl.ds(0, last)], 0)
    late_rows = pl.ds(last, HEADS * 2 * D)
    late = load(raw_grads.at[late_rows], grads.at[late_rows], 1)
    vec_load = load(raw_vec, gvec, 2)
    half = items // 2
    tok_loads = [load(raw_tok.at[pl.ds(k * half, half)], held_tok.at[pl.ds(k * half, half)], 3 + k) for k in range(2)]
    out_load = load(raw_out, held_out, 5)
    early.wait()
    for c in range(chunks):
        down[c * D : (c + 1) * D] = grads[c * 2 * D : c * 2 * D + D].astype(f32)
    store(down, gdown)
    for c in range(chunks):
        up[:, c * D : (c + 1) * D] = grads[c * 2 * D + D : (c + 1) * 2 * D].astype(f32)
    store(up, gup)
    late.wait()
    for h in range(HEADS):
        at = last + h * 2 * D
        lanes = slice(h * HEAD_DIM, (h + 1) * HEAD_DIM)
        first = grads[at : at + D].astype(f32)
        second = grads[at + D : at + 2 * D].astype(f32)
        qkv[:, h * HEAD_DIM : (h + 1) * HEAD_DIM] = first[:, :HEAD_DIM]
        qkv[:, D + h * HEAD_DIM : D + (h + 1) * HEAD_DIM] = first[:, HEAD_DIM:]
        qkv[:, 2 * D + h * HEAD_DIM : 2 * D + (h + 1) * HEAD_DIM] = second[:, :HEAD_DIM]
        wout[:, lanes] = second[:, HEAD_DIM:]
    store(qkv, gqkv)
    store(wout, gout)
    for k in range(2):
        tok_loads[k].wait()
        store(held_tok.at[pl.ds(k * half, half)], gtok.at[pl.ds(k * half, half)])
    out_load.wait()
    store(held_out, output)
    vec_load.wait()
    gain_attn[...] = gvec[0:1]
    shift_attn[...] = gvec[1:2]
    gain_ffn[...] = gvec[2:3]
    shift_ffn[...] = gvec[3:4]
    for copy in stores:
        copy.wait()


def shards(
    seq_size,
    mesh_sizes,
    tokens,
    lengths,
    pad_mask,
    w_qkv,
    w_out,
    w_up,
    w_down,
    gain_attn,
    shift_attn,
    gain_ffn,
    shift_ffn,
    cotangent,
):
    items, block, width = tokens.shape
    rows = block // ROW
    total = items * block
    ff = w_up.shape[1]
    ext = block + ROW
    n_items, n_z = mesh_sizes
    grad_rows = 2 * ff + 4 * width
    half = grad_rows // 2
    links = n_items + n_z - 1
    plane = n_items * n_z
    if width % (16 * plane) == 0:
        links = plane
    vmem = pl.BlockSpec(memory_space=pltpu.VMEM)
    anywhere = pl.BlockSpec(memory_space=pl.ANY)
    raw = [
        jax.ShapeDtypeStruct((items, block, width), bf16),
        jax.ShapeDtypeStruct((items, block, width), f32),
        jax.ShapeDtypeStruct((grad_rows, width), bf16),
        jax.ShapeDtypeStruct((8, width), f32),
    ]
    vectors = [v.reshape(1, width) for v in (gain_attn, shift_attn, gain_ffn, shift_ffn)]
    parts = ff // width + HEADS
    vm = pltpu.VMEM
    raw = pl.pallas_call(
        functools.partial(layer_kernel, items, rows, mesh_sizes, seq_size),
        out_shape=raw,
        in_specs=[pl.BlockSpec(memory_space=pltpu.SMEM), vmem] + [anywhere] * 6 + [vmem] * 4,
        out_specs=[anywhere] * 4,
        scratch_shapes=[
            vm((items, ext, width), bf16),
            vm((items, block, width), bf16),
            vm((items, block, 128), f32),
            vm((rows, 8, 256), f32),
            vm((width, 3 * width), bf16),
            vm((width, width), bf16),
            vm((width, ff), bf16),
            vm((ff, width), bf16),
            vm((items, ext, width), bf16),
            vm((items, ext, width), bf16),
            vm((items, ext, 128), f32),
            vm((items, ext, 3 * width), bf16),
            vm((items, rows * HEADS, ROW, 256), bf16),
            vm((items, block, width), f32),
            vm((items, block, width), bf16),
            vm((items, block, width), f32),
            vm((items, block, width), bf16),
            vm((items, block, 128), f32),
            vm((total, width), bf16),
            vm((total, width), bf16),
            vm((total, ff), bf16),
            vm((total, ff), bf16),
            vm((items, block, width), f32),
            vm((items, block, width), bf16),
            vm((items, ext, 3 * width), bf16),
            vm((items, ROW, width), bf16),
            vm((items, ROW, width), bf16),
            vm((items, block, width), bf16),
            vm((32, width), f32),
            vm((3, max(n_items, n_z), 8, width), f32),
            vm((grad_rows, width), f32),
            vm((half, width), bf16),
            vm((half, width), bf16),
            vm((half, width), bf16),
            vm((n_items - 1, half // n_items, width), bf16),
            vm((half // n_items, width), bf16),
            vm((n_z, half // n_items, width), bf16),
            vm((plane - 1, half // plane // 16 * 16 + 16, width), bf16),
            vm((grad_rows, width), bf16),
            pltpu.SemaphoreType.DMA((4 + items + 3 * HEADS,)),
            pltpu.SemaphoreType.DMA((6,)),
            pltpu.SemaphoreType.DMA((4,)),
            pltpu.SemaphoreType.DMA((2, links)),
            pltpu.SemaphoreType.DMA((2 * parts, links)),
            pltpu.SemaphoreType.DMA((2 * parts, links)),
        ],
        compiler_params=pltpu.CompilerParams(
            vmem_limit_bytes=63 * 2**20, collective_id=0, has_side_effects=True
        ),
    )(lengths, pad_mask, tokens, cotangent, w_qkv, w_out, w_up, w_down, *vectors)
    shapes = [
        jax.ShapeDtypeStruct((items, block, width), bf16),
        jax.ShapeDtypeStruct((items, block, width), f32),
        jax.ShapeDtypeStruct((width, 3 * width), f32),
        jax.ShapeDtypeStruct((width, width), f32),
        jax.ShapeDtypeStruct((width, ff), f32),
        jax.ShapeDtypeStruct((ff, width), f32),
    ] + [jax.ShapeDtypeStruct((1, width), f32)] * 4
    outs = pl.pallas_call(
        split_kernel,
        out_shape=shapes,
        in_specs=[anywhere] * 4,
        out_specs=[anywhere] * 6 + [vmem] * 4,
        scratch_shapes=[
            vm((items, block, width), bf16),
            vm((items, block, width), f32),
            vm((grad_rows, width), bf16),
            vm((8, width), f32),
            vm((width, 3 * width), f32),
            vm((width, width), f32),
            vm((width, ff), f32),
            vm((ff, width), f32),
            pltpu.SemaphoreType.DMA((6,)),
            pltpu.SemaphoreType.DMA((7,)),
        ],
        compiler_params=pltpu.CompilerParams(vmem_limit_bytes=63 * 2**20),
    )(*raw)
    return tuple(outs[:6]) + tuple(v.reshape(width) for v in outs[6:])


def solution(mesh):
    split = P("items", "seq", None)
    seq_size = mesh.shape["seq"]
    mesh_sizes = (mesh.shape["items"], seq_size // 2)
    return jax.shard_map(
        functools.partial(shards, seq_size, mesh_sizes),
        mesh=mesh,
        in_specs=(split, P("items"), P("items", None)) + (P(),) * 8 + (split,),
        out_specs=(split, split) + (P(),) * 8,
        check_vma=False,
    )
```

```python
import functools
import math

import jax
import jax.numpy as jnp
from jax import lax
from jax.experimental import pallas as pl
from jax.experimental.pallas import tpu as pltpu
from jax.sharding import PartitionSpec as P

HEADS = 2
HEAD_DIM = 128
ROW = 96
D = HEADS * HEAD_DIM

epsilon = 1e-05
branch_scale = 0.7071067811865476
masked_value = -1e30
score_scale = HEAD_DIM ** (-0.5)
log2e = math.log2(math.e)
gelu_in = math.sqrt(2 / math.pi)
gelu_cube = gelu_in * 0.044715
f32 = jnp.float32
bf16 = jnp.bfloat16


def dot(left, right, left_dim=1, right_dim=0):
    return lax.dot_general(
        left, right, (((left_dim,), (right_dim,)), ((), ())), preferred_element_type=f32
    )


def normalise(inputs):
    average = jnp.mean(inputs, -1, keepdims=True)
    centred = inputs - average
    spread = jnp.mean(centred * centred, -1, keepdims=True)
    factor = lax.rsqrt(spread + epsilon)
    return centred * factor, factor


def norm_back(grad, normed, factor, gain):
    e = grad * gain
    first = jnp.mean(e, -1, keepdims=True)
    second = jnp.mean(e * normed, -1, keepdims=True)
    return factor * (e - first - normed * second)


def fold_rows(values):
    count = values.shape[0] // 8
    return jnp.sum(values.reshape(count, 8, values.shape[1]), 0)


def plan(direct):
    plan = {
        "feed0": [],
        "feed1": [(0, 0)],
        "feed2": [(0, 1)],
        "feed3": [(1, 0)],
        "middle": [(1, 1)],
        "back0": [(0, 2)],
        "weight0": [(2, 0)],
        "back1": [(2, 1), (1, 2)],
        "weight1": [(3, 0)],
        "tokens0": [(0, 3)],
        "tokens1": [(3, 1)],
        "finish0": [("v", 1)],
        "finish1": [(1, 3)],
        "tail": [(0, 4), (2, 2), ("v", 2), (1, 4), (3, 2), (0, 5), (1, 5)],
        "last": [(2, 4), (3, 4)],
    }
    if direct:
        plan["tail"] += [(2, 3), ("v", 3), (3, 3), (0, 6), (1, 6)]
    else:
        plan["tail"] += [(0, 6), (1, 6)] + [(p, n) for n in (3, 4, 5) for p in (2, 3)] + [("v", 3)]
        plan["last"] = [(2, 6), (3, 6)]
    return plan


class Sums:
    def __init__(self, mesh_sizes, refs):
        (self.partial, self.c_out, self.c_in, self.i_out, self.i_in, self.z_out, self.z_in,
         self.d_in, self.full, self.send, self.recv) = refs
        self.n_items, self.n_z = mesh_sizes
        self.item = lax.axis_index("items")
        seq = lax.axis_index("seq")
        self.core = lax.rem(seq, 2)
        self.z = seq // 2

    def partner(self, kind, step):
        if kind == "core":
            return {"items": self.item, "seq": self.z * 2 + 1 - self.core}
        item, z = self.spot(kind, step)
        return {"items": item, "seq": z * 2 + self.core}

    def spot(self, kind, step):
        items_step, z_step = {
            "items": (step, 0),
            "z": (0, step),
            "plane": (step // self.n_z, step % self.n_z),
        }[kind]
        return (
            lax.rem(self.item + items_step, self.n_items),
            lax.rem(self.z + z_step, self.n_z),
        )

    def steps_of(self, kind):
        counts = {"core": 2, "items": self.n_items, "z": self.n_z, "plane": self.n_items * self.n_z}
        return range(1, counts[kind])

    def copies(self, part, phase, kind, source, target):
        number = part * 6 + phase * 3 + {"core": 0, "items": 1, "z": 2, "plane": 1}[kind]
        return number, [
            pltpu.make_async_remote_copy(
                src_ref=source(step),
                dst_ref=target(step),
                send_sem=self.send.at[number],
                recv_sem=self.recv.at[number],
                device_id=self.partner(kind, step),
                device_id_type=pl.DeviceIdType.MESH,
            )
            for step in self.steps_of(kind)
        ]

    def start(self, copies):
        for copy in copies[1]:
            copy.start()

    def finish(self, copies, count):
        number, each = copies
        size = self.full.at[pl.ds(0, len(each) * count)]
        pltpu.make_async_copy(size, size, self.recv.at[number]).wait()
        pltpu.make_async_copy(size, size, self.send.at[number]).wait()

    def place(self, first, rows):
        half = rows // 2
        quarter = half // self.n_items
        split = quarter % (16 * self.n_z) == 0
        last = quarter // self.n_z if split else quarter
        return half, quarter, split, last

    def first_copies(self, part, first, rows):
        half, _, _, _ = self.place(first, rows)
        here = pl.ds(first // 2, half)
        return self.copies(part, 0, "core", lambda s: self.c_out.at[here], lambda s: self.c_in.at[here])

    def items_copies(self, part, first, rows):
        half, quarter, _, _ = self.place(first, rows)

        def source(step):
            to = lax.rem(self.item + step, self.n_items)
            return self.i_out.at[pl.ds(pl.multiple_of(first // 2 + to * quarter, 16), quarter)]

        at = pl.ds(first // 2 // self.n_items, quarter)
        return self.copies(part, 0, "items", source, lambda s: self.i_in.at[s - 1, at])

    def z_copies(self, part, first, rows):
        half, quarter, split, last = self.place(first, rows)
        base = first // 2 // self.n_items
        if split:
            def source(step):
                to = lax.rem(self.z + step, self.n_z)
                return self.z_out.at[pl.ds(pl.multiple_of(base + to * last, 16), last)]

            at = pl.ds(base // self.n_z, last)
            return self.copies(part, 0, "z", source, lambda s: self.z_in.at[s - 1, at])
        at = pl.ds(base, quarter)
        return self.copies(part, 0, "z", lambda s: self.z_out.at[at], lambda s: self.z_in.at[self.z, at])

    def plane_copies(self, part, first, rows):
        count = rows // 2 // (self.n_items * self.n_z)

        def source(step):
            item, z = self.spot("plane", step)
            at = first // 2 + (item * self.n_z + z) * count
            return self.i_out.at[pl.ds(pl.multiple_of(at, 16), count)]

        at = pl.ds(first // 2 // (self.n_items * self.n_z), count)
        return self.copies(part, 0, "plane", source, lambda s: self.d_in.at[s - 1, at])

    def held(self, first, rows, level):
        half, quarter, split, last = self.place(first, rows)
        at = first + self.core * half
        count = half
        if level > 0:
            at += self.item * quarter
            count = quarter
        if level > 1 and split:
            at += self.z * last
            count = last
        return self.full.at[pl.ds(pl.multiple_of(at, 16), count)]

    def back_copies(self, part, first, rows, kind):
        level = {"core": 0, "items": 1, "z": 2, "plane": 2}[kind]
        ref = self.held(first, rows, level)
        return self.copies(part, 1, kind, lambda s: ref, lambda s: ref)

    def plane_step(self, part, first, rows, number):
        count = rows // 2 // (self.n_items * self.n_z)
        base = first // 2
        if number == 2:
            self.finish(self.plane_copies(part, first, rows), count)
            own = base + (self.item * self.n_z + self.z) * count
            value = self.i_out[pl.ds(pl.multiple_of(own, 16), count)].astype(f32)
            at = pl.ds(base // (self.n_items * self.n_z), count)
            for step in self.steps_of("plane"):
                value += self.d_in[step - 1, at].astype(f32)
            self.held(first, rows, 2)[...] = value.astype(bf16)
            self.start(self.back_copies(part, first, rows, "plane"))
        if number == 3:
            self.finish(self.back_copies(part, first, rows, "plane"), count)
            self.start(self.back_copies(part, first, rows, "core"))
        if number == 4:
            self.finish(self.back_copies(part, first, rows, "core"), rows // 2)

    def step(self, part, first, rows, number, plane=False):
        if plane and number > 1:
            self.plane_step(part, first, rows, number)
            return
        half, quarter, split, last = self.place(first, rows)
        base_c = first // 2
        base_i = base_c // self.n_items
        if number == 0:
            away = pl.ds(pl.multiple_of(first + (1 - self.core) * half, 16), half)
            self.c_out[pl.ds(base_c, half)] = self.partial[away].astype(bf16)
            self.start(self.first_copies(part, first, rows))
        if number == 1:
            self.finish(self.first_copies(part, first, rows), half)
            here = pl.ds(base_c, half)
            own = pl.ds(pl.multiple_of(first + self.core * half, 16), half)
            self.i_out[here] = (self.partial[own] + self.c_in[here].astype(f32)).astype(bf16)
            if plane:
                self.start(self.plane_copies(part, first, rows))
            else:
                self.start(self.items_copies(part, first, rows))
        if number == 2:
            self.finish(self.items_copies(part, first, rows), quarter)
            own = pl.ds(pl.multiple_of(base_c + self.item * quarter, 16), quarter)
            at = pl.ds(base_i, quarter)
            value = self.i_out[own].astype(f32)
            for step in self.steps_of("items"):
                value += self.i_in[step - 1, at].astype(f32)
            self.z_out[at] = value.astype(bf16)
            if not split:
                self.z_in[self.z, at] = value.astype(bf16)
            self.start(self.z_copies(part, first, rows))
        if number == 3:
            self.finish(self.z_copies(part, first, rows), last)
            if split:
                own = pl.ds(pl.multiple_of(base_i + self.z * last, 16), last)
                at = pl.ds(base_i // self.n_z, last)
                value = self.z_out[own].astype(f32)
                for step in self.steps_of("z"):
                    value += self.z_in[step - 1, at].astype(f32)
            else:
                at = pl.ds(base_i, quarter)
                value = self.z_in[0, at].astype(f32)
                for step in self.steps_of("z"):
                    value += self.z_in[step, at].astype(f32)
            self.held(first, rows, 2)[...] = value.astype(bf16)
            if split:
                self.start(self.back_copies(part, first, rows, "z"))
            else:
                self.start(self.back_copies(part, first, rows, "items"))
        if number == 4 and split:
            self.finish(self.back_copies(part, first, rows, "z"), last)
            self.start(self.back_copies(part, first, rows, "items"))
        if number == 5:
            self.finish(self.back_copies(part, first, rows, "items"), quarter)
            self.start(self.back_copies(part, first, rows, "core"))
        if number == 6:
            self.finish(self.back_copies(part, first, rows, "core"), rows // 2)


def layer_kernel(
    items,
    rows,
    mesh_sizes,
    seq_size,
    lengths_ref,
    pad_ref,
    tokens_ref,
    cot_hbm,
    wqkv_hbm,
    wout_hbm,
    wup_hbm,
    wdown_hbm,
    gain_attn_ref,
    shift_attn_ref,
    gain_ffn_ref,
    shift_ffn_ref,
    output_ref,
    gtok_ref,
    grads_ref,
    gvec_ref,
    x,
    cot,
    alive,
    keys,
    wqkv,
    wout,
    wup,
    wdown,
    h1,
    n1,
    r1,
    proj,
    exps,
    inv,
    att,
    middle,
    n2,
    r2,
    h2,
    dbr,
    hid,
    dpre,
    dmid,
    datt,
    dproj,
    ghalo,
    ghalo_in,
    out,
    gvec,
    vec_buf,
    partial,
    c_out,
    c_in,
    i_out,
    i_in,
    z_out,
    z_in,
    d_in,
    full,
    load_sems,
    store_sems,
    halo_sems,
    vec_sems,
    send_sems,
    recv_sems,
):
    block = rows * ROW
    total = items * block
    gain_attn = gain_attn_ref[...]
    shift_attn = shift_attn_ref[...]
    gain_ffn = gain_ffn_ref[...]
    shift_ffn = shift_ffn_ref[...]
    ff = wup.shape[1]
    chunks = ff // D
    n_items, n_z = mesh_sizes
    item = lax.axis_index("items")
    seq = lax.axis_index("seq")
    MESH = pl.DeviceIdType.MESH
    sums = Sums(
        mesh_sizes, (partial, c_out, c_in, i_out, i_in, z_out, z_in, d_in, full, send_sems, recv_sems)
    )
    wide = chunks // 2
    parts = [(k * wide * 2 * D, wide * 2 * D) for k in range(2)]
    parts += [((chunks + h) * 2 * D, 2 * D) for h in range(HEADS)]
    direct = D % (16 * n_items * n_z) == 0
    schedule = plan(direct)

    def hook(name):
        for part, number in schedule[name]:
            if part == "v":
                vec_step(number)
            else:
                sums.step(part, *parts[part], number, plane=direct and part >= 2)

    after = {"items": item, "seq": lax.rem(seq + 1, seq_size)}
    ahead = {"items": item, "seq": lax.rem(seq + seq_size - 1, seq_size)}
    barrier = pltpu.get_barrier_semaphore()
    greeted = [after, ahead]
    for kind in ("core", "plane") if direct else ("core", "items", "z"):
        greeted += [sums.partner(kind, s) for s in sums.steps_of(kind)]
    loads = [
        (wout_hbm, wout),
        (wup_hbm, wup),
        (wdown_hbm, wdown),
        (cot_hbm, cot),
    ]
    token_loads = [
        pltpu.make_async_copy(tokens_ref.at[i], x.at[i, pl.ds(ROW, block)], load_sems.at[4 + i])
        for i in range(items)
    ]
    weight_loads = [
        pltpu.make_async_copy(source, target, load_sems.at[k])
        for k, (source, target) in enumerate(loads)
    ]
    qkv_loads = [
        pltpu.make_async_copy(
            wqkv_hbm.at[:, pl.ds(p * D + h * HEAD_DIM, HEAD_DIM)],
            wqkv.at[:, pl.ds((h * 3 + p) * HEAD_DIM, HEAD_DIM)],
            load_sems.at[4 + items + h * 3 + p],
        )
        for h in range(HEADS)
        for p in range(3)
    ]
    for copy in qkv_loads:
        copy.start()
    for copy in token_loads:
        copy.start()
    for copy in weight_loads:
        copy.start()

    for device in greeted:
        pl.semaphore_signal(barrier, inc=1, device_id=device, device_id_type=MESH)

    first_pos = seq * block

    def window(start, width):
        spots = sorted({(s * block + (start if s else 0)) % 128 for s in range(seq_size)})
        if start:
            spots = sorted({(s * block + start) % 128 for s in range(1, seq_size)})
        at = jnp.maximum(first_pos + start, 0)
        low = pl.multiple_of(at // 128 * 128, 128)
        wide = (spots[-1] + width + 127) // 128 * 128
        held = pad_ref[:, pl.ds(low, wide)]
        result = held[:, spots[0] : spots[0] + width]
        for spot in spots[1:]:
            result = jnp.where(at % 128 == spot, held[:, spot : spot + width], result)
        return result

    count = jnp.zeros((items, 1), jnp.int32)
    which = lax.broadcasted_iota(jnp.int32, (items, 1), 0)
    for i in range(items):
        count = jnp.where(which == i, lengths_ref[i], count)

    def there(start, width):
        position = first_pos + start + lax.broadcasted_iota(jnp.int32, (items, width), 1)
        good = (position >= 0) & (position < count) & (window(start, width) == 1)
        return jnp.where(good, 1.0, 0.0)

    row_there = [there((r - 1) * ROW, ROW) for r in range(rows + 1)]
    spread = lax.broadcasted_iota(jnp.int32, (items, items * 128), 1) // 128
    spread = jnp.where(spread == lax.broadcasted_iota(jnp.int32, (items, items * 128), 0), 1.0, 0.0)
    for r in range(rows):
        both = jnp.concatenate([row_there[r], row_there[r + 1]], 1)
        keys[r, :items, : 2 * ROW] = (1.0 - both) * masked_value
        column = dot(row_there[r + 1].astype(bf16), spread.astype(bf16), 0, 0)
        for i in range(items):
            alive[i, r * ROW : (r + 1) * ROW] = column[:, i * 128 : (i + 1) * 128]

    def alive_of(i):
        mask = alive[i]
        return jnp.concatenate([mask, mask], 1)

    def first_norm(values):
        normed, factor = normalise(values)
        return (normed * gain_attn + shift_attn).astype(bf16), normed.astype(bf16), factor

    for copy in qkv_loads:
        copy.wait()
    for copy in token_loads:
        copy.wait()
    found = [first_norm(x[i, ROW:].astype(f32)) for i in range(items)]
    results = [dot(low, wqkv[...]).astype(bf16) for low, _, _ in found]
    for i in range(items):
        low, normed, factor = found[i]
        h1[i, ROW:] = low
        n1[i, ROW:] = normed
        r1[i, ROW:] = jnp.broadcast_to(factor, (block, 128))
        proj[i, ROW:] = results[i]

    pl.semaphore_wait(barrier, len(greeted))
    halo_copy = pltpu.make_async_remote_copy(
        src_ref=tokens_ref.at[:, pl.ds(block - ROW, ROW)],
        dst_ref=x.at[:, pl.ds(0, ROW)],
        send_sem=halo_sems.at[0],
        recv_sem=halo_sems.at[1],
        device_id=after,
        device_id_type=MESH,
    )
    halo_copy.start()

    query_pos = lax.broadcasted_iota(jnp.int32, (ROW, 2 * ROW), 0)
    key_pos = lax.broadcasted_iota(jnp.int32, (ROW, 2 * ROW), 1) - ROW
    causal = jnp.where(key_pos <= query_pos, 0.0, masked_value)
    itself = jnp.where(key_pos == query_pos, 0.0, masked_value)
    for copy in weight_loads:
        copy.wait()

    def part_of(whole, r, count, number, h):
        at = (h * 3 + number) * HEAD_DIM
        return whole[r * ROW : (r + count) * ROW, at : at + HEAD_DIM]

    def weigh(mine, keys_of, units):
        biases = {r: jnp.maximum(jnp.minimum(causal, keys_of(r)), itself) for r, _ in units}
        scores = [
            dot(part_of(mine, r + 1, 1, 0, h), part_of(mine, r, 2, 1, h), 1, 1)
            * (score_scale * log2e)
            + biases[r]
            for r, h in units
        ]
        es = [jnp.exp2(one - jnp.max(one, -1, keepdims=True)) for one in scores]
        shares = [
            jnp.broadcast_to(1.0 / jnp.sum(e, -1, keepdims=True), (ROW, HEAD_DIM)) for e in es
        ]
        lows = [e.astype(bf16) for e in es]
        results = [
            (dot(e, part_of(mine, r, 2, 2, h)) * share).astype(bf16)
            for e, share, (r, h) in zip(lows, shares, units)
        ]
        return lows, shares, results

    def heads(values):
        return jnp.concatenate(values, 1)

    def attend(first, end):
        units = [(r, h) for r in range(first, end) for h in range(HEADS)]
        here = slice(first * ROW, end * ROW)
        count = (end - first) * ROW
        mask = alive[:, here]
        grads = jnp.concatenate([mask, mask], 2) * cot[:, here].astype(f32)
        grads = (branch_scale * grads).astype(bf16)
        all_shares, all_results, all_lows = [], [], []
        for i in range(items):
            lows, shares, results = weigh(proj[i], lambda r: keys[r, i : i + 1, : 2 * ROW], units)
            all_lows.append(lows)
            for values, joined in ((shares, all_shares), (results, all_results)):
                lines = [heads(values[k : k + HEADS]) for k in range(0, len(units), HEADS)]
                joined.append(jnp.concatenate(lines, 0))
        attended = jnp.concatenate(all_results, 0)
        inputs = x[:, ROW + first * ROW : ROW + end * ROW].astype(f32).reshape(items * count, D)
        mid = inputs + branch_scale * dot(attended, wout[...])
        normed, factor = normalise(mid)
        low = (normed * gain_ffn + shift_ffn).astype(bf16)
        for i in range(items):
            mine = slice(i * count, (i + 1) * count)
            flat = slice(i * block + first * ROW, i * block + end * ROW)
            for (r, h), e in zip(units, all_lows[i]):
                exps[i, r * HEADS + h, :, : 2 * ROW] = e
            inv[i, here] = all_shares[i]
            att[i, here] = all_results[i]
            middle[i, here] = mid[mine]
            n2[i, here] = normed[mine].astype(bf16)
            r2[i, here] = jnp.broadcast_to(factor[mine], (count, 128))
            h2[flat] = low[mine]
            dbr[flat] = grads[i]

    attend(1, rows)
    halo_copy.wait()
    low, normed, factor = first_norm(x[:, :ROW].astype(f32).reshape(items * ROW, D))
    results = [
        dot(low, wqkv[:, (h * 3 + 1) * HEAD_DIM : (h * 3 + 3) * HEAD_DIM]).astype(bf16)
        for h in range(HEADS)
    ]
    h1[:, :ROW] = low.reshape(items, ROW, D)
    n1[:, :ROW] = normed.reshape(items, ROW, D)
    r1[:, :ROW] = jnp.broadcast_to(factor, (items * ROW, 128)).reshape(items, ROW, 128)
    for h in range(HEADS):
        at = (h * 3 + 1) * HEAD_DIM
        proj[:, :ROW, at : at + 2 * HEAD_DIM] = results[h].reshape(items, ROW, 2 * HEAD_DIM)
    attend(0, 1)

    for c in range(chunks):
        cols = slice(c * D, (c + 1) * D)
        down = slice(c * 2 * D, c * 2 * D + D)
        up = slice(c * 2 * D + D, (c + 1) * 2 * D)

        normed = h2[...]
        grad = dbr[...]
        u = dot(normed, wup[:, cols])
        back = dot(grad, wdown[cols], 1, 1)
        square = u * u
        s = 0.5 * jnp.tanh(u * (gelu_in + gelu_cube * square)) + 0.5
        hidden = (u * s).astype(bf16)
        slope = s + u * ((s - s * s) * (2 * gelu_in + 6 * gelu_cube * square))
        before = (back * slope).astype(bf16)
        down_grad = dot(hidden, grad, 0, 0)
        up_grad = dot(normed, before, 0, 0)
        hid[:, cols] = hidden
        dpre[:, cols] = before
        partial[down] = down_grad
        partial[up] = up_grad
        hook("feed%d" % c)

    last = chunks * 2 * D

    found = []
    for i in range(items):
        normed = n2[i].astype(f32)
        factor = jnp.concatenate([r2[i]] * 2, 1)
        outer = alive_of(i) * cot[i].astype(f32)
        grad = dot(dpre[i * block : (i + 1) * block], wup[...], 1, 1)
        sums_here = fold_rows(grad * normed), fold_rows(grad)
        grad = outer + norm_back(grad, normed, factor, gain_ffn)
        found.append((grad, (branch_scale * grad).astype(bf16), sums_here))
    lows = jnp.concatenate([f[1] for f in found], 0)
    out_grad = dot(att[...].reshape(total, D), lows, 0, 0)
    back = dot(lows, wout[...], 1, 1).astype(bf16)
    for i in range(items):
        dmid[i] = found[i][0]
        datt[i] = back[i * block : (i + 1) * block]
    for h in range(HEADS):
        at = last + h * 2 * D + D
        partial[at : at + D, HEAD_DIM:] = out_grad[:, h * HEAD_DIM : (h + 1) * HEAD_DIM]
    gvec[16:24] = sum(f[2][0] for f in found)
    gvec[24:32] = sum(f[2][1] for f in found)
    hook("middle")

    def attend_back(h):
        at = h * 3 * HEAD_DIM
        lanes = slice(h * HEAD_DIM, (h + 1) * HEAD_DIM)
        found = []
        for i in range(items):
            mine = proj[i, :, at : at + 3 * HEAD_DIM]
            es = [exps[i, r * HEADS + h, :, : 2 * ROW] for r in range(rows)]
            scaled = datt[i, :, lanes].astype(f32) * inv[i, :, lanes]
            product = scaled * att[i, :, lanes].astype(f32)
            low = scaled.astype(bf16)
            dqs, dks, dvs = [], [], []
            dps = [
                dot(low[r * ROW : (r + 1) * ROW], part_of(mine, r, 2, 2, 0), 1, 1)
                for r in range(rows)
            ]
            dss = []
            for r in range(rows):
                row_dot = jnp.sum(product[r * ROW : (r + 1) * ROW], -1, keepdims=True)
                dss.append((es[r].astype(f32) * ((dps[r] - row_dot) * score_scale)).astype(bf16))
            dvs = [dot(es[r], low[r * ROW : (r + 1) * ROW], 0, 0) for r in range(rows)]
            dks = [dot(dss[r], part_of(mine, r + 1, 1, 0, 0), 0, 0) for r in range(rows)]
            dqs = [dot(dss[r], part_of(mine, r, 2, 1, 0)).astype(bf16) for r in range(rows)]

            def gather(grads):
                lines = []
                for r in range(rows + 1):
                    value = 0.0
                    if r < rows:
                        value = grads[r][:ROW]
                    if r > 0:
                        value += grads[r - 1][ROW:]
                    lines.append(value.astype(bf16))
                return jnp.concatenate(lines, 0)

            found.append((jnp.concatenate(dqs, 0), gather(dks), gather(dvs)))
        for i in range(items):
            dproj[i, :ROW, at : at + HEAD_DIM] = jnp.zeros((ROW, HEAD_DIM), bf16)
            dproj[i, ROW:, at : at + HEAD_DIM] = found[i][0]
            dproj[i, :, at + HEAD_DIM : at + 2 * HEAD_DIM] = found[i][1]
            dproj[i, :, at + 2 * HEAD_DIM : at + 3 * HEAD_DIM] = found[i][2]

    def weight_back(h):
        left = h1[...].reshape(items * (block + ROW), D)
        at = h * 3 * HEAD_DIM
        right = dproj[:, :, at : at + 3 * HEAD_DIM].reshape(items * (block + ROW), 3 * HEAD_DIM)
        grad = dot(left, right, 0, 0)
        start = last + h * 2 * D
        partial[start : start + D] = grad[:, :D]
        partial[start + D : start + 2 * D, :HEAD_DIM] = grad[:, D:]

    attend_back(0)
    hook("back0")
    weight_back(0)
    hook("weight0")
    attend_back(1)
    hook("back1")
    weight_back(1)
    hook("weight1")

    def tokens_back(first, end):
        found = []
        for i in range(first, end):
            grad = dot(dproj[i], wqkv[...], 1, 1)
            normed = n1[i].astype(f32)
            factor = jnp.concatenate([r1[i]] * 2, 1)
            sums_here = fold_rows(grad * normed), fold_rows(grad)
            grad = norm_back(grad, normed, factor, gain_attn)
            found.append((grad[:ROW].astype(bf16), dmid[i] + grad[ROW:], sums_here))
        for i in range(first, end):
            ghalo[i] = found[i - first][0]
            dmid[i] = found[i - first][1]
        return sum(f[2][0] for f in found), sum(f[2][1] for f in found)

    half = items // 2
    one = tokens_back(0, half)
    hook("tokens0")
    two = tokens_back(half, items)
    gvec[0:8] = one[0] + two[0]
    gvec[8:16] = one[1] + two[1]
    ghalo_copy = pltpu.make_async_remote_copy(
        src_ref=ghalo,
        dst_ref=ghalo_in,
        send_sem=halo_sems.at[2],
        recv_sem=halo_sems.at[3],
        device_id=ahead,
        device_id_type=MESH,
    )
    ghalo_copy.start()

    own_copy = None
    if rows > 1:
        own = pl.ds(0, block - ROW)
        own_copy = pltpu.make_async_copy(dmid.at[:, own], gtok_ref.at[:, own], store_sems.at[5])
        own_copy.start()

    def vec_copies(kind, number):
        result = []
        place = {"core": sums.core, "items": item, "z": sums.z}[kind]
        base = {"core": 0, "items": 1, "z": n_items}[kind]
        for s in sums.steps_of(kind):
            here = vec_buf.at[number, place]
            result.append(
                pltpu.make_async_remote_copy(
                    src_ref=here,
                    dst_ref=here,
                    send_sem=vec_sems.at[0, base + s - 1],
                    recv_sem=vec_sems.at[1, base + s - 1],
                    device_id=sums.partner(kind, s),
                    device_id_type=MESH,
                )
            )
        return result

    def start_all(copies):
        for copy in copies:
            copy.start()

    def finish_all(copies):
        for copy in copies:
            copy.wait()

    def vec_total(number, size):
        value = vec_buf[number, 0]
        for k in range(1, size):
            value += vec_buf[number, k]
        return value

    lines = [jnp.sum(gvec[8 * k : 8 * k + 8], 0, keepdims=True) for k in range(4)]
    vec_buf[0, sums.core] = jnp.concatenate(lines + [jnp.zeros((4, D), f32)], 0)
    start_all(vec_copies("core", 0))

    def vec_step(number):
        if number == 1:
            finish_all(vec_copies("core", 0))
            vec_buf[1, item] = vec_total(0, 2)
            start_all(vec_copies("items", 1))
        if number == 2:
            finish_all(vec_copies("items", 1))
            vec_buf[2, sums.z] = vec_total(1, n_items)
            start_all(vec_copies("z", 2))
        if number == 3:
            finish_all(vec_copies("z", 2))
            gvec[0:8] = vec_total(2, n_z)

    def finish(first, end):
        branch = dot(hid[first * block : end * block], wdown[...])
        results = [
            alive_of(i)
            * (middle[i] + branch_scale * branch[(i - first) * block : (i - first + 1) * block])
            for i in range(first, end)
        ]
        for i in range(first, end):
            out[i] = results[i - first].astype(bf16)

    hook("tokens1")
    finish(0, half)
    hook("finish0")
    finish(half, items)
    out_copy = pltpu.make_async_copy(out, output_ref, store_sems.at[0])
    out_copy.start()
    hook("finish1")
    ghalo_copy.wait()
    tail = block - ROW
    for i in range(items):
        dmid[i, tail:] += ghalo_in[i].astype(f32)
    tok_copy = pltpu.make_async_copy(dmid.at[:, pl.ds(tail, ROW)], gtok_ref.at[:, pl.ds(tail, ROW)], store_sems.at[1])
    tok_copy.start()
    hook("tail")
    vec_copy = pltpu.make_async_copy(gvec.at[pl.ds(0, 8)], gvec_ref, store_sems.at[2])
    vec_copy.start()
    early = pl.ds(0, last)
    early_copy = pltpu.make_async_copy(full.at[early], grads_ref.at[early], store_sems.at[3])
    early_copy.start()
    hook("last")
    late = pl.ds(last, HEADS * 2 * D)
    late_copy = pltpu.make_async_copy(full.at[late], grads_ref.at[late], store_sems.at[4])
    late_copy.start()
    for copy in (out_copy, own_copy, tok_copy, vec_copy, early_copy, late_copy):
        if copy is not None:
            copy.wait()


def split_kernel(
    raw_out,
    raw_tok,
    raw_grads,
    raw_vec,
    output,
    gtok,
    gqkv,
    gout,
    gup,
    gdown,
    gain_attn,
    shift_attn,
    gain_ffn,
    shift_ffn,
    held_out,
    held_tok,
    grads,
    gvec,
    qkv,
    wout,
    up,
    down,
    load_sems,
    store_sems,
):
    chunks = up.shape[1] // D
    items = raw_tok.shape[0]
    last = chunks * 2 * D
    stores = []

    def load(source, target, number):
        copy = pltpu.make_async_copy(source, target, load_sems.at[number])
        copy.start()
        return copy

    def store(source, target):
        copy = pltpu.make_async_copy(source, target, store_sems.at[len(stores)])
        copy.start()
        stores.append(copy)

    early = load(raw_grads.at[pl.ds(0, last)], grads.at[pl.ds(0, last)], 0)
    late_rows = pl.ds(last, HEADS * 2 * D)
    late = load(raw_grads.at[late_rows], grads.at[late_rows], 1)
    vec_load = load(raw_vec, gvec, 2)
    half = items // 2
    tok_loads = [load(raw_tok.at[pl.ds(k * half, half)], held_tok.at[pl.ds(k * half, half)], 3 + k) for k in range(2)]
    out_load = load(raw_out, held_out, 5)
    early.wait()
    for c in range(chunks):
        down[c * D : (c + 1) * D] = grads[c * 2 * D : c * 2 * D + D].astype(f32)
    store(down, gdown)
    for c in range(chunks):
        up[:, c * D : (c + 1) * D] = grads[c * 2 * D + D : (c + 1) * 2 * D].astype(f32)
    store(up, gup)
    late.wait()
    for h in range(HEADS):
        at = last + h * 2 * D
        lanes = slice(h * HEAD_DIM, (h + 1) * HEAD_DIM)
        first = grads[at : at + D].astype(f32)
        second = grads[at + D : at + 2 * D].astype(f32)
        qkv[:, h * HEAD_DIM : (h + 1) * HEAD_DIM] = first[:, :HEAD_DIM]
        qkv[:, D + h * HEAD_DIM : D + (h + 1) * HEAD_DIM] = first[:, HEAD_DIM:]
        qkv[:, 2 * D + h * HEAD_DIM : 2 * D + (h + 1) * HEAD_DIM] = second[:, :HEAD_DIM]
        wout[:, lanes] = second[:, HEAD_DIM:]
    store(qkv, gqkv)
    store(wout, gout)
    for k in range(2):
        tok_loads[k].wait()
        store(held_tok.at[pl.ds(k * half, half)], gtok.at[pl.ds(k * half, half)])
    out_load.wait()
    store(held_out, output)
    vec_load.wait()
    gain_attn[...] = gvec[0:1]
    shift_attn[...] = gvec[1:2]
    gain_ffn[...] = gvec[2:3]
    shift_ffn[...] = gvec[3:4]
    for copy in stores:
        copy.wait()


def shards(
    seq_size,
    mesh_sizes,
    tokens,
    lengths,
    pad_mask,
    w_qkv,
    w_out,
    w_up,
    w_down,
    gain_attn,
    shift_attn,
    gain_ffn,
    shift_ffn,
    cotangent,
):
    items, block, width = tokens.shape
    rows = block // ROW
    total = items * block
    ff = w_up.shape[1]
    ext = block + ROW
    n_items, n_z = mesh_sizes
    grad_rows = 2 * ff + 4 * width
    half = grad_rows // 2
    links = n_items + n_z - 1
    plane = n_items * n_z
    if width % (16 * plane) == 0:
        links = plane
    vmem = pl.BlockSpec(memory_space=pltpu.VMEM)
    anywhere = pl.BlockSpec(memory_space=pl.ANY)
    raw = [
        jax.ShapeDtypeStruct((items, block, width), bf16),
        jax.ShapeDtypeStruct((items, block, width), f32),
        jax.ShapeDtypeStruct((grad_rows, width), bf16),
        jax.ShapeDtypeStruct((8, width), f32),
    ]
    vectors = [v.reshape(1, width) for v in (gain_attn, shift_attn, gain_ffn, shift_ffn)]
    parts = 2 + HEADS
    vm = pltpu.VMEM
    raw = pl.pallas_call(
        functools.partial(layer_kernel, items, rows, mesh_sizes, seq_size),
        out_shape=raw,
        in_specs=[pl.BlockSpec(memory_space=pltpu.SMEM), vmem] + [anywhere] * 6 + [vmem] * 4,
        out_specs=[anywhere] * 4,
        scratch_shapes=[
            vm((items, ext, width), bf16),
            vm((items, block, width), bf16),
            vm((items, block, 128), f32),
            vm((rows, 8, 256), f32),
            vm((width, 3 * width), bf16),
            vm((width, width), bf16),
            vm((width, ff), bf16),
            vm((ff, width), bf16),
            vm((items, ext, width), bf16),
            vm((items, ext, width), bf16),
            vm((items, ext, 128), f32),
            vm((items, ext, 3 * width), bf16),
            vm((items, rows * HEADS, ROW, 256), bf16),
            vm((items, block, width), f32),
            vm((items, block, width), bf16),
            vm((items, block, width), f32),
            vm((items, block, width), bf16),
            vm((items, block, 128), f32),
            vm((total, width), bf16),
            vm((total, width), bf16),
            vm((total, ff), bf16),
            vm((total, ff), bf16),
            vm((items, block, width), f32),
            vm((items, block, width), bf16),
            vm((items, ext, 3 * width), bf16),
            vm((items, ROW, width), bf16),
            vm((items, ROW, width), bf16),
            vm((items, block, width), bf16),
            vm((32, width), f32),
            vm((3, max(n_items, n_z), 8, width), f32),
            vm((grad_rows, width), f32),
            vm((half, width), bf16),
            vm((half, width), bf16),
            vm((half, width), bf16),
            vm((n_items - 1, half // n_items, width), bf16),
            vm((half // n_items, width), bf16),
            vm((n_z, half // n_items, width), bf16),
            vm((plane - 1, half // plane // 16 * 16 + 16, width), bf16),
            vm((grad_rows, width), bf16),
            pltpu.SemaphoreType.DMA((4 + items + 3 * HEADS,)),
            pltpu.SemaphoreType.DMA((6,)),
            pltpu.SemaphoreType.DMA((4,)),
            pltpu.SemaphoreType.DMA((2, links)),
            pltpu.SemaphoreType.DMA((6 * parts,)),
            pltpu.SemaphoreType.DMA((6 * parts,)),
        ],
        compiler_params=pltpu.CompilerParams(
            vmem_limit_bytes=63 * 2**20, collective_id=0, has_side_effects=True
        ),
    )(lengths, pad_mask, tokens, cotangent, w_qkv, w_out, w_up, w_down, *vectors)
    shapes = [
        jax.ShapeDtypeStruct((items, block, width), bf16),
        jax.ShapeDtypeStruct((items, block, width), f32),
        jax.ShapeDtypeStruct((width, 3 * width), f32),
        jax.ShapeDtypeStruct((width, width), f32),
        jax.ShapeDtypeStruct((width, ff), f32),
        jax.ShapeDtypeStruct((ff, width), f32),
    ] + [jax.ShapeDtypeStruct((1, width), f32)] * 4
    outs = pl.pallas_call(
        split_kernel,
        out_shape=shapes,
        in_specs=[anywhere] * 4,
        out_specs=[anywhere] * 6 + [vmem] * 4,
        scratch_shapes=[
            vm((items, block, width), bf16),
            vm((items, block, width), f32),
            vm((grad_rows, width), bf16),
            vm((8, width), f32),
            vm((width, 3 * width), f32),
            vm((width, width), f32),
            vm((width, ff), f32),
            vm((ff, width), f32),
            pltpu.SemaphoreType.DMA((6,)),
            pltpu.SemaphoreType.DMA((7,)),
        ],
        compiler_params=pltpu.CompilerParams(vmem_limit_bytes=63 * 2**20),
    )(*raw)
    return tuple(outs[:6]) + tuple(v.reshape(width) for v in outs[6:])


def solution(mesh):
    split = P("items", "seq", None)
    seq_size = mesh.shape["seq"]
    mesh_sizes = (mesh.shape["items"], seq_size // 2)
    return jax.shard_map(
        functools.partial(shards, seq_size, mesh_sizes),
        mesh=mesh,
        in_specs=(split, P("items"), P("items", None)) + (P(),) * 8 + (split,),
        out_specs=(split, split) + (P(),) * 8,
        check_vma=False,
    )
```

```python
import functools
import math

import jax
import jax.numpy as jnp
from jax import lax
from jax.experimental import pallas as pl
from jax.experimental.pallas import tpu as pltpu
from jax.sharding import PartitionSpec as P

HEADS = 2
HEAD_DIM = 128
ROW = 96
D = HEADS * HEAD_DIM

epsilon = 1e-05
branch_scale = 0.7071067811865476
masked_value = -1e30
score_scale = HEAD_DIM ** (-0.5)
log2e = math.log2(math.e)
gelu_in = math.sqrt(2 / math.pi)
gelu_cube = gelu_in * 0.044715
f32 = jnp.float32
bf16 = jnp.bfloat16


def dot(left, right, left_dim=1, right_dim=0):
    return lax.dot_general(
        left, right, (((left_dim,), (right_dim,)), ((), ())), preferred_element_type=f32
    )


def normalise(inputs):
    average = jnp.mean(inputs, -1, keepdims=True)
    centred = inputs - average
    spread = jnp.mean(centred * centred, -1, keepdims=True)
    factor = lax.rsqrt(spread + epsilon)
    return centred * factor, factor


def norm_back(grad, normed, factor, gain):
    e = grad * gain
    first = jnp.mean(e, -1, keepdims=True)
    second = jnp.mean(e * normed, -1, keepdims=True)
    return factor * (e - first - normed * second)


def fold_rows(values):
    count = values.shape[0] // 8
    return jnp.sum(values.reshape(count, 8, values.shape[1]), 0)


def plan():
    plan = {
        "feed0": [],
        "feed1": [(0, 0)],
        "feed2": [(0, 1)],
        "feed3": [(1, 0)],
        "middle": [(1, 1)],
        "back0": [(0, 2)],
        "weight0": [(2, 0)],
        "back1": [(2, 1), (1, 2)],
        "weight1": [(3, 0)],
        "tokens0": [(0, 3)],
        "tokens1": [(3, 1)],
        "finish0": [("v", 1), (2, 2)],
        "finish1": [(1, 3)],
        "tail": [(0, 4), (3, 2), ("v", 2), (1, 4), (2, 3), (0, 5), (3, 3), (1, 5), (2, 5), (0, 6), (3, 5), (1, 6), ("v", 3)],
        "last": [(2, 6), (3, 6)],
    }
    return plan


class Sums:
    def __init__(self, mesh_sizes, refs):
        (self.partial, self.c_out, self.c_in, self.i_out, self.i_in, self.z_out, self.z_in,
         self.full, self.send, self.recv) = refs
        self.n_items, self.n_z = mesh_sizes
        self.item = lax.axis_index("items")
        seq = lax.axis_index("seq")
        self.core = lax.rem(seq, 2)
        self.z = seq // 2

    def partner(self, kind, step):
        if kind == "core":
            return {"items": self.item, "seq": self.z * 2 + 1 - self.core}
        if kind == "items":
            return {"items": lax.rem(self.item + step, self.n_items), "seq": self.z * 2 + self.core}
        return {"items": self.item, "seq": lax.rem(self.z + step, self.n_z) * 2 + self.core}

    def steps_of(self, kind):
        return range(1, {"core": 2, "items": self.n_items, "z": self.n_z}[kind])

    def copies(self, part, phase, kind, source, target):
        number = part * 6 + phase * 3 + {"core": 0, "items": 1, "z": 2}[kind]
        return number, [
            pltpu.make_async_remote_copy(
                src_ref=source(step),
                dst_ref=target(step),
                send_sem=self.send.at[number],
                recv_sem=self.recv.at[number],
                device_id=self.partner(kind, step),
                device_id_type=pl.DeviceIdType.MESH,
            )
            for step in self.steps_of(kind)
        ]

    def start(self, copies):
        for copy in copies[1]:
            copy.start()

    def finish(self, copies, count):
        number, each = copies
        size = self.full.at[pl.ds(0, len(each) * count)]
        pltpu.make_async_copy(size, size, self.recv.at[number]).wait()
        pltpu.make_async_copy(size, size, self.send.at[number]).wait()

    def place(self, first, rows):
        half = rows // 2
        quarter = half // self.n_items
        split = quarter % (16 * self.n_z) == 0 and rows > 2 * D
        last = quarter // self.n_z if split else quarter
        return half, quarter, split, last

    def first_copies(self, part, first, rows):
        half, _, _, _ = self.place(first, rows)
        here = pl.ds(first // 2, half)
        return self.copies(part, 0, "core", lambda s: self.c_out.at[here], lambda s: self.c_in.at[here])

    def items_copies(self, part, first, rows):
        half, quarter, _, _ = self.place(first, rows)

        def source(step):
            to = lax.rem(self.item + step, self.n_items)
            return self.i_out.at[pl.ds(pl.multiple_of(first // 2 + to * quarter, 16), quarter)]

        at = pl.ds(first // 2 // self.n_items, quarter)
        return self.copies(part, 0, "items", source, lambda s: self.i_in.at[s - 1, at])

    def z_copies(self, part, first, rows):
        half, quarter, split, last = self.place(first, rows)
        base = first // 2 // self.n_items
        if split:
            def source(step):
                to = lax.rem(self.z + step, self.n_z)
                return self.z_out.at[pl.ds(pl.multiple_of(base + to * last, 16), last)]

            at = pl.ds(base // self.n_z, last)
            return self.copies(part, 0, "z", source, lambda s: self.z_in.at[s - 1, at])
        at = pl.ds(base, quarter)
        return self.copies(part, 0, "z", lambda s: self.z_out.at[at], lambda s: self.z_in.at[self.z, at])

    def held(self, first, rows, level):
        half, quarter, split, last = self.place(first, rows)
        at = first + self.core * half
        count = half
        if level > 0:
            at += self.item * quarter
            count = quarter
        if level > 1 and split:
            at += self.z * last
            count = last
        return self.full.at[pl.ds(pl.multiple_of(at, 16), count)]

    def back_copies(self, part, first, rows, kind):
        level = {"core": 0, "items": 1, "z": 2}[kind]
        ref = self.held(first, rows, level)
        return self.copies(part, 1, kind, lambda s: ref, lambda s: ref)

    def step(self, part, first, rows, number):
        half, quarter, split, last = self.place(first, rows)
        base_c = first // 2
        base_i = base_c // self.n_items
        if number == 0:
            away = pl.ds(pl.multiple_of(first + (1 - self.core) * half, 16), half)
            self.c_out[pl.ds(base_c, half)] = self.partial[away].astype(bf16)
            self.start(self.first_copies(part, first, rows))
        if number == 1:
            self.finish(self.first_copies(part, first, rows), half)
            here = pl.ds(base_c, half)
            own = pl.ds(pl.multiple_of(first + self.core * half, 16), half)
            self.i_out[here] = (self.partial[own] + self.c_in[here].astype(f32)).astype(bf16)
            self.start(self.items_copies(part, first, rows))
        if number == 2:
            self.finish(self.items_copies(part, first, rows), quarter)
            own = pl.ds(pl.multiple_of(base_c + self.item * quarter, 16), quarter)
            at = pl.ds(base_i, quarter)
            value = self.i_out[own].astype(f32)
            for step in self.steps_of("items"):
                value += self.i_in[step - 1, at].astype(f32)
            self.z_out[at] = value.astype(bf16)
            if not split:
                self.z_in[self.z, at] = value.astype(bf16)
            self.start(self.z_copies(part, first, rows))
        if number == 3:
            self.finish(self.z_copies(part, first, rows), last)
            if split:
                own = pl.ds(pl.multiple_of(base_i + self.z * last, 16), last)
                at = pl.ds(base_i // self.n_z, last)
                value = self.z_out[own].astype(f32)
                for step in self.steps_of("z"):
                    value += self.z_in[step - 1, at].astype(f32)
            else:
                at = pl.ds(base_i, quarter)
                value = self.z_in[0, at].astype(f32)
                for step in self.steps_of("z"):
                    value += self.z_in[step, at].astype(f32)
            self.held(first, rows, 2)[...] = value.astype(bf16)
            if split:
                self.start(self.back_copies(part, first, rows, "z"))
            else:
                self.start(self.back_copies(part, first, rows, "items"))
        if number == 4 and split:
            self.finish(self.back_copies(part, first, rows, "z"), last)
            self.start(self.back_copies(part, first, rows, "items"))
        if number == 5:
            self.finish(self.back_copies(part, first, rows, "items"), quarter)
            self.start(self.back_copies(part, first, rows, "core"))
        if number == 6:
            self.finish(self.back_copies(part, first, rows, "core"), rows // 2)


def layer_kernel(
    items,
    rows,
    mesh_sizes,
    seq_size,
    lengths_ref,
    pad_ref,
    tokens_ref,
    cot_hbm,
    wqkv_hbm,
    wout_hbm,
    wup_hbm,
    wdown_hbm,
    gain_attn_ref,
    shift_attn_ref,
    gain_ffn_ref,
    shift_ffn_ref,
    output_ref,
    gtok_ref,
    grads_ref,
    gvec_ref,
    x,
    cot,
    alive,
    keys,
    wqkv,
    wout,
    wup,
    wdown,
    h1,
    n1,
    r1,
    proj,
    exps,
    inv,
    att,
    middle,
    n2,
    r2,
    h2,
    dbr,
    hid,
    dpre,
    ghalo,
    ghalo_in,
    gvec,
    vec_buf,
    partial,
    c_out,
    c_in,
    i_out,
    i_in,
    z_out,
    z_in,
    load_sems,
    halo_sems,
    vec_sems,
    send_sems,
    recv_sems,
):
    block = rows * ROW
    total = items * block
    gain_attn = gain_attn_ref[...]
    shift_attn = shift_attn_ref[...]
    gain_ffn = gain_ffn_ref[...]
    shift_ffn = shift_ffn_ref[...]
    ff = wup.shape[1]
    chunks = ff // D
    n_items, n_z = mesh_sizes
    item = lax.axis_index("items")
    seq = lax.axis_index("seq")
    MESH = pl.DeviceIdType.MESH
    sums = Sums(
        mesh_sizes, (partial, c_out, c_in, i_out, i_in, z_out, z_in, grads_ref, send_sems, recv_sems)
    )
    wide = chunks // 2
    parts = [(k * wide * 2 * D, wide * 2 * D) for k in range(2)]
    parts += [((chunks + h) * 2 * D, 2 * D) for h in range(HEADS)]
    schedule = plan()

    def hook(name):
        for part, number in schedule[name]:
            if part == "v":
                vec_step(number)
            else:
                sums.step(part, *parts[part], number)

    after = {"items": item, "seq": lax.rem(seq + 1, seq_size)}
    ahead = {"items": item, "seq": lax.rem(seq + seq_size - 1, seq_size)}
    barrier = pltpu.get_barrier_semaphore()
    greeted = [after, ahead]
    for kind in ("core", "items", "z"):
        greeted += [sums.partner(kind, s) for s in sums.steps_of(kind)]
    for device in greeted:
        pl.semaphore_signal(barrier, inc=1, device_id=device, device_id_type=MESH)

    loads = [
        (wout_hbm, wout),
        (wup_hbm, wup),
        (wdown_hbm, wdown),
        (cot_hbm, cot),
    ]
    token_loads = [
        pltpu.make_async_copy(tokens_ref.at[i], x.at[i, pl.ds(ROW, block)], load_sems.at[4 + i])
        for i in range(items)
    ]
    weight_loads = [
        pltpu.make_async_copy(source, target, load_sems.at[k])
        for k, (source, target) in enumerate(loads)
    ]
    qkv_loads = [
        pltpu.make_async_copy(
            wqkv_hbm.at[:, pl.ds(p * D + h * HEAD_DIM, HEAD_DIM)],
            wqkv.at[:, pl.ds((h * 3 + p) * HEAD_DIM, HEAD_DIM)],
            load_sems.at[4 + items + h * 3 + p],
        )
        for h in range(HEADS)
        for p in range(3)
    ]
    for copy in qkv_loads:
        copy.start()
    for copy in token_loads:
        copy.start()
    for copy in weight_loads:
        copy.start()


    first_pos = seq * block

    def window(start, width):
        spots = sorted({(s * block + (start if s else 0)) % 128 for s in range(seq_size)})
        if start:
            spots = sorted({(s * block + start) % 128 for s in range(1, seq_size)})
        at = jnp.maximum(first_pos + start, 0)
        low = pl.multiple_of(at // 128 * 128, 128)
        wide = (spots[-1] + width + 127) // 128 * 128
        held = pad_ref[:, pl.ds(low, wide)]
        result = held[:, spots[0] : spots[0] + width]
        for spot in spots[1:]:
            result = jnp.where(at % 128 == spot, held[:, spot : spot + width], result)
        return result

    count = jnp.zeros((items, 1), jnp.int32)
    which = lax.broadcasted_iota(jnp.int32, (items, 1), 0)
    for i in range(items):
        count = jnp.where(which == i, lengths_ref[i], count)

    def there(start, width):
        position = first_pos + start + lax.broadcasted_iota(jnp.int32, (items, width), 1)
        good = (position >= 0) & (position < count) & (window(start, width) == 1)
        return jnp.where(good, 1.0, 0.0)

    row_there = [there((r - 1) * ROW, ROW) for r in range(rows + 1)]
    spread = lax.broadcasted_iota(jnp.int32, (items, items * 128), 1) // 128
    spread = jnp.where(spread == lax.broadcasted_iota(jnp.int32, (items, items * 128), 0), 1.0, 0.0)
    for r in range(rows):
        both = jnp.concatenate([row_there[r], row_there[r + 1]], 1)
        keys[r, :items, : 2 * ROW] = (1.0 - both) * masked_value
        column = dot(row_there[r + 1].astype(bf16), spread.astype(bf16), 0, 0)
        for i in range(items):
            alive[i, r * ROW : (r + 1) * ROW] = column[:, i * 128 : (i + 1) * 128]

    def alive_of(i):
        mask = alive[i]
        return jnp.concatenate([mask, mask], 1)

    def first_norm(values):
        normed, factor = normalise(values)
        return (normed * gain_attn + shift_attn).astype(bf16), normed.astype(bf16), factor

    for copy in qkv_loads:
        copy.wait()
    def project(first, end):
        for i in range(first, end):
            token_loads[i].wait()
        found = [first_norm(x[i, ROW:].astype(f32)) for i in range(first, end)]
        results = [dot(low, wqkv[...]).astype(bf16) for low, _, _ in found]
        for i in range(first, end):
            low, normed, factor = found[i - first]
            h1[i, ROW:] = low
            n1[i, ROW:] = normed
            r1[i, ROW:] = jnp.broadcast_to(factor, (block, 128))
            proj[i, ROW:] = results[i - first]

    early = items // 3
    project(0, early)
    pl.semaphore_wait(barrier, len(greeted))
    halo_copy = pltpu.make_async_remote_copy(
        src_ref=tokens_ref.at[:, pl.ds(block - ROW, ROW)],
        dst_ref=x.at[:, pl.ds(0, ROW)],
        send_sem=halo_sems.at[0],
        recv_sem=halo_sems.at[1],
        device_id=after,
        device_id_type=MESH,
    )
    halo_copy.start()
    project(early, items)

    query_pos = lax.broadcasted_iota(jnp.int32, (ROW, 2 * ROW), 0)
    key_pos = lax.broadcasted_iota(jnp.int32, (ROW, 2 * ROW), 1) - ROW
    causal = jnp.where(key_pos <= query_pos, 0.0, masked_value)
    itself = jnp.where(key_pos == query_pos, 0.0, masked_value)
    for copy in weight_loads:
        copy.wait()

    def part_of(whole, r, count, number, h):
        at = (h * 3 + number) * HEAD_DIM
        return whole[r * ROW : (r + count) * ROW, at : at + HEAD_DIM]

    def weigh(mine, keys_of, units):
        biases = {r: jnp.maximum(jnp.minimum(causal, keys_of(r)), itself) for r, _ in units}
        scores = [
            dot(part_of(mine, r + 1, 1, 0, h), part_of(mine, r, 2, 1, h), 1, 1)
            * (score_scale * log2e)
            + biases[r]
            for r, h in units
        ]
        es = [jnp.exp2(one - jnp.max(one, -1, keepdims=True)) for one in scores]
        shares = [
            jnp.broadcast_to(1.0 / jnp.sum(e, -1, keepdims=True), (ROW, HEAD_DIM)) for e in es
        ]
        lows = [e.astype(bf16) for e in es]
        results = [
            (dot(e, part_of(mine, r, 2, 2, h)) * share).astype(bf16)
            for e, share, (r, h) in zip(lows, shares, units)
        ]
        return lows, shares, results

    def heads(values):
        return jnp.concatenate(values, 1)

    def attend(first, end):
        units = [(r, h) for r in range(first, end) for h in range(HEADS)]
        here = slice(first * ROW, end * ROW)
        count = (end - first) * ROW
        mask = alive[:, here]
        grads = jnp.concatenate([mask, mask], 2) * cot[:, here].astype(f32)
        grads = (branch_scale * grads).astype(bf16)
        all_shares, all_results, all_lows = [], [], []
        for i in range(items):
            lows, shares, results = weigh(proj[i], lambda r: keys[r, i : i + 1, : 2 * ROW], units)
            all_lows.append(lows)
            for values, joined in ((shares, all_shares), (results, all_results)):
                lines = [heads(values[k : k + HEADS]) for k in range(0, len(units), HEADS)]
                joined.append(jnp.concatenate(lines, 0))
        attended = jnp.concatenate(all_results, 0)
        inputs = x[:, ROW + first * ROW : ROW + end * ROW].astype(f32).reshape(items * count, D)
        mid = inputs + branch_scale * dot(attended, wout[...])
        normed, factor = normalise(mid)
        low = (normed * gain_ffn + shift_ffn).astype(bf16)
        for i in range(items):
            mine = slice(i * count, (i + 1) * count)
            flat = slice(i * block + first * ROW, i * block + end * ROW)
            for (r, h), e in zip(units, all_lows[i]):
                exps[i, r * HEADS + h, :, : 2 * ROW] = e
            inv[i, here] = all_shares[i]
            att[i, here] = all_results[i]
            middle[i, here] = mid[mine]
            n2[i, here] = normed[mine].astype(bf16)
            r2[i, here] = jnp.broadcast_to(factor[mine], (count, 128))
            h2[flat] = low[mine]
            dbr[flat] = grads[i]

    attend(1, rows)
    halo_copy.wait()
    low, normed, factor = first_norm(x[:, :ROW].astype(f32).reshape(items * ROW, D))
    results = [
        dot(low, wqkv[:, (h * 3 + 1) * HEAD_DIM : (h * 3 + 3) * HEAD_DIM]).astype(bf16)
        for h in range(HEADS)
    ]
    h1[:, :ROW] = low.reshape(items, ROW, D)
    n1[:, :ROW] = normed.reshape(items, ROW, D)
    r1[:, :ROW] = jnp.broadcast_to(factor, (items * ROW, 128)).reshape(items, ROW, 128)
    for h in range(HEADS):
        at = (h * 3 + 1) * HEAD_DIM
        proj[:, :ROW, at : at + 2 * HEAD_DIM] = results[h].reshape(items, ROW, 2 * HEAD_DIM)
    attend(0, 1)

    for c in range(chunks):
        cols = slice(c * D, (c + 1) * D)
        down = slice(c * 2 * D, c * 2 * D + D)
        up = slice(c * 2 * D + D, (c + 1) * 2 * D)

        normed = h2[...]
        grad = dbr[...]
        u = dot(normed, wup[:, cols])
        back = dot(grad, wdown[cols], 1, 1)
        square = u * u
        s = 0.5 * jnp.tanh(u * (gelu_in + gelu_cube * square)) + 0.5
        hidden = (u * s).astype(bf16)
        slope = s + u * ((s - s * s) * (2 * gelu_in + 6 * gelu_cube * square))
        before = (back * slope).astype(bf16)
        down_grad = dot(hidden, grad, 0, 0)
        up_grad = dot(normed, before, 0, 0)
        hid[:, cols] = hidden
        dpre[:, cols] = before
        partial[down] = down_grad
        partial[up] = up_grad
        hook("feed%d" % c)

    last = chunks * 2 * D

    found = []
    for i in range(items):
        normed = n2[i].astype(f32)
        factor = jnp.concatenate([r2[i]] * 2, 1)
        outer = alive_of(i) * cot[i].astype(f32)
        grad = dot(dpre[i * block : (i + 1) * block], wup[...], 1, 1)
        sums_here = fold_rows(grad * normed), fold_rows(grad)
        grad = outer + norm_back(grad, normed, factor, gain_ffn)
        found.append((grad, (branch_scale * grad).astype(bf16), sums_here))
    lows = jnp.concatenate([f[1] for f in found], 0)
    out_grad = dot(att[...].reshape(total, D), lows, 0, 0)
    back = dot(lows, wout[...], 1, 1).astype(bf16)
    for i in range(items):
        gtok_ref[i] = found[i][0]
    h2[...] = back
    for h in range(HEADS):
        at = last + h * 2 * D + D
        partial[at : at + D, HEAD_DIM:] = out_grad[:, h * HEAD_DIM : (h + 1) * HEAD_DIM]
    gvec[16:24] = sum(f[2][0] for f in found)
    gvec[24:32] = sum(f[2][1] for f in found)
    hook("middle")

    def attend_back(h):
        at = h * 3 * HEAD_DIM
        lanes = slice(h * HEAD_DIM, (h + 1) * HEAD_DIM)
        found = []
        for i in range(items):
            mine = proj[i, :, at : at + 3 * HEAD_DIM]
            es = [exps[i, r * HEADS + h, :, : 2 * ROW] for r in range(rows)]
            scaled = h2[i * block : (i + 1) * block, lanes].astype(f32) * inv[i, :, lanes]
            product = scaled * att[i, :, lanes].astype(f32)
            low = scaled.astype(bf16)
            dqs, dks, dvs = [], [], []
            dps = [
                dot(low[r * ROW : (r + 1) * ROW], part_of(mine, r, 2, 2, 0), 1, 1)
                for r in range(rows)
            ]
            dss = []
            for r in range(rows):
                row_dot = jnp.sum(product[r * ROW : (r + 1) * ROW], -1, keepdims=True)
                dss.append((es[r].astype(f32) * ((dps[r] - row_dot) * score_scale)).astype(bf16))
            dvs = [dot(es[r], low[r * ROW : (r + 1) * ROW], 0, 0) for r in range(rows)]
            dks = [dot(dss[r], part_of(mine, r + 1, 1, 0, 0), 0, 0) for r in range(rows)]
            dqs = [dot(dss[r], part_of(mine, r, 2, 1, 0)).astype(bf16) for r in range(rows)]

            def gather(grads):
                lines = []
                for r in range(rows + 1):
                    value = 0.0
                    if r < rows:
                        value = grads[r][:ROW]
                    if r > 0:
                        value += grads[r - 1][ROW:]
                    lines.append(value.astype(bf16))
                return jnp.concatenate(lines, 0)

            found.append((jnp.concatenate(dqs, 0), gather(dks), gather(dvs)))
        for i in range(items):
            proj[i, :ROW, at : at + HEAD_DIM] = jnp.zeros((ROW, HEAD_DIM), bf16)
            proj[i, ROW:, at : at + HEAD_DIM] = found[i][0]
            proj[i, :, at + HEAD_DIM : at + 2 * HEAD_DIM] = found[i][1]
            proj[i, :, at + 2 * HEAD_DIM : at + 3 * HEAD_DIM] = found[i][2]

    def weight_back(h):
        left = h1[...].reshape(items * (block + ROW), D)
        at = h * 3 * HEAD_DIM
        right = proj[:, :, at : at + 3 * HEAD_DIM].reshape(items * (block + ROW), 3 * HEAD_DIM)
        grad = dot(left, right, 0, 0)
        start = last + h * 2 * D
        partial[start : start + D] = grad[:, :D]
        partial[start + D : start + 2 * D, :HEAD_DIM] = grad[:, D:]

    attend_back(0)
    hook("back0")
    weight_back(0)
    hook("weight0")
    attend_back(1)
    hook("back1")
    weight_back(1)
    hook("weight1")

    def tokens_back(first, end):
        found = []
        for i in range(first, end):
            grad = dot(proj[i], wqkv[...], 1, 1)
            normed = n1[i].astype(f32)
            factor = jnp.concatenate([r1[i]] * 2, 1)
            sums_here = fold_rows(grad * normed), fold_rows(grad)
            grad = norm_back(grad, normed, factor, gain_attn)
            found.append((grad[:ROW].astype(bf16), gtok_ref[i] + grad[ROW:], sums_here))
        for i in range(first, end):
            ghalo[i] = found[i - first][0]
            gtok_ref[i] = found[i - first][1]
        return sum(f[2][0] for f in found), sum(f[2][1] for f in found)

    half = items // 2
    one = tokens_back(0, half)
    hook("tokens0")
    two = tokens_back(half, items)
    gvec[0:8] = one[0] + two[0]
    gvec[8:16] = one[1] + two[1]
    ghalo_copy = pltpu.make_async_remote_copy(
        src_ref=ghalo,
        dst_ref=ghalo_in,
        send_sem=halo_sems.at[2],
        recv_sem=halo_sems.at[3],
        device_id=ahead,
        device_id_type=MESH,
    )
    ghalo_copy.start()

    def vec_copies(kind, number):
        result = []
        place = {"core": sums.core, "items": item, "z": sums.z}[kind]
        base = {"core": 0, "items": 1, "z": n_items}[kind]
        for s in sums.steps_of(kind):
            here = vec_buf.at[number, place]
            result.append(
                pltpu.make_async_remote_copy(
                    src_ref=here,
                    dst_ref=here,
                    send_sem=vec_sems.at[0, base + s - 1],
                    recv_sem=vec_sems.at[1, base + s - 1],
                    device_id=sums.partner(kind, s),
                    device_id_type=MESH,
                )
            )
        return result

    def start_all(copies):
        for copy in copies:
            copy.start()

    def finish_all(copies):
        for copy in copies:
            copy.wait()

    def vec_total(number, size):
        value = vec_buf[number, 0]
        for k in range(1, size):
            value += vec_buf[number, k]
        return value

    lines = [jnp.sum(gvec[8 * k : 8 * k + 8], 0, keepdims=True) for k in range(4)]
    vec_buf[0, sums.core] = jnp.concatenate(lines + [jnp.zeros((4, D), f32)], 0)
    start_all(vec_copies("core", 0))

    def vec_step(number):
        if number == 1:
            finish_all(vec_copies("core", 0))
            vec_buf[1, item] = vec_total(0, 2)
            start_all(vec_copies("items", 1))
        if number == 2:
            finish_all(vec_copies("items", 1))
            vec_buf[2, sums.z] = vec_total(1, n_items)
            start_all(vec_copies("z", 2))
        if number == 3:
            finish_all(vec_copies("z", 2))
            gvec_ref[...] = vec_total(2, n_z)

    def finish(first, end):
        branch = dot(hid[first * block : end * block], wdown[...])
        results = [
            alive_of(i)
            * (middle[i] + branch_scale * branch[(i - first) * block : (i - first + 1) * block])
            for i in range(first, end)
        ]
        for i in range(first, end):
            output_ref[i] = results[i - first].astype(bf16)

    hook("tokens1")
    finish(0, half)
    hook("finish0")
    finish(half, items)
    hook("finish1")
    ghalo_copy.wait()
    tail = block - ROW
    for i in range(items):
        gtok_ref[i, tail:] += ghalo_in[i].astype(f32)
    hook("tail")
    hook("last")


def split_kernel(
    raw_out,
    raw_tok,
    grads,
    gvec,
    output,
    gtok,
    gqkv,
    gout,
    gup,
    gdown,
    gain_attn,
    shift_attn,
    gain_ffn,
    shift_ffn,
    qkv,
    wout,
    up,
    down,
    store_sems,
):
    chunks = up.shape[1] // D
    last = chunks * 2 * D
    stores = []

    def store(source, target):
        copy = pltpu.make_async_copy(source, target, store_sems.at[len(stores)])
        copy.start()
        stores.append(copy)

    store(raw_tok, gtok)
    store(raw_out, output)
    for c in range(chunks):
        down[c * D : (c + 1) * D] = grads[c * 2 * D : c * 2 * D + D].astype(f32)
    store(down, gdown)
    for c in range(chunks):
        up[:, c * D : (c + 1) * D] = grads[c * 2 * D + D : (c + 1) * 2 * D].astype(f32)
    store(up, gup)
    for h in range(HEADS):
        at = last + h * 2 * D
        lanes = slice(h * HEAD_DIM, (h + 1) * HEAD_DIM)
        first = grads[at : at + D].astype(f32)
        second = grads[at + D : at + 2 * D].astype(f32)
        qkv[:, h * HEAD_DIM : (h + 1) * HEAD_DIM] = first[:, :HEAD_DIM]
        qkv[:, D + h * HEAD_DIM : D + (h + 1) * HEAD_DIM] = first[:, HEAD_DIM:]
        qkv[:, 2 * D + h * HEAD_DIM : 2 * D + (h + 1) * HEAD_DIM] = second[:, :HEAD_DIM]
        wout[:, lanes] = second[:, HEAD_DIM:]
    store(qkv, gqkv)
    store(wout, gout)
    gain_attn[...] = gvec[0:1]
    shift_attn[...] = gvec[1:2]
    gain_ffn[...] = gvec[2:3]
    shift_ffn[...] = gvec[3:4]
    for copy in stores:
        copy.wait()


def shards(
    seq_size,
    mesh_sizes,
    tokens,
    lengths,
    pad_mask,
    w_qkv,
    w_out,
    w_up,
    w_down,
    gain_attn,
    shift_attn,
    gain_ffn,
    shift_ffn,
    cotangent,
):
    items, block, width = tokens.shape
    rows = block // ROW
    total = items * block
    ff = w_up.shape[1]
    ext = block + ROW
    n_items, n_z = mesh_sizes
    grad_rows = 2 * ff + 4 * width
    half = grad_rows // 2
    links = n_items + n_z - 1
    vmem = pl.BlockSpec(memory_space=pltpu.VMEM)
    anywhere = pl.BlockSpec(memory_space=pl.ANY)
    raw = [
        pltpu.VMEM((items, block, width), bf16),
        pltpu.VMEM((items, block, width), f32),
        pltpu.VMEM((grad_rows, width), bf16),
        pltpu.VMEM((8, width), f32),
    ]
    vectors = [v.reshape(1, width) for v in (gain_attn, shift_attn, gain_ffn, shift_ffn)]
    parts = 2 + HEADS
    vm = pltpu.VMEM
    raw = pl.pallas_call(
        functools.partial(layer_kernel, items, rows, mesh_sizes, seq_size),
        out_shape=raw,
        in_specs=[pl.BlockSpec(memory_space=pltpu.SMEM), vmem] + [anywhere] * 6 + [vmem] * 4,
        out_specs=[vmem] * 4,
        scratch_shapes=[
            vm((items, ext, width), bf16),
            vm((items, block, width), bf16),
            vm((items, block, 128), f32),
            vm((rows, 8, 256), f32),
            vm((width, 3 * width), bf16),
            vm((width, width), bf16),
            vm((width, ff), bf16),
            vm((ff, width), bf16),
            vm((items, ext, width), bf16),
            vm((items, ext, width), bf16),
            vm((items, ext, 128), f32),
            vm((items, ext, 3 * width), bf16),
            vm((items, rows * HEADS, ROW, 256), bf16),
            vm((items, block, width), f32),
            vm((items, block, width), bf16),
            vm((items, block, width), f32),
            vm((items, block, width), bf16),
            vm((items, block, 128), f32),
            vm((total, width), bf16),
            vm((total, width), bf16),
            vm((total, ff), bf16),
            vm((total, ff), bf16),
            vm((items, ROW, width), bf16),
            vm((items, ROW, width), bf16),
            vm((32, width), f32),
            vm((3, max(n_items, n_z), 8, width), f32),
            vm((grad_rows, width), f32),
            vm((half, width), bf16),
            vm((half, width), bf16),
            vm((half, width), bf16),
            vm((n_items - 1, half // n_items, width), bf16),
            vm((half // n_items, width), bf16),
            vm((n_z, half // n_items, width), bf16),
            pltpu.SemaphoreType.DMA((4 + items + 3 * HEADS,)),
            pltpu.SemaphoreType.DMA((4,)),
            pltpu.SemaphoreType.DMA((2, links)),
            pltpu.SemaphoreType.DMA((6 * parts,)),
            pltpu.SemaphoreType.DMA((6 * parts,)),
        ],
        compiler_params=pltpu.CompilerParams(
            vmem_limit_bytes=52 * 2**20, collective_id=0, has_side_effects=True
        ),
    )(lengths, pad_mask, tokens, cotangent, w_qkv, w_out, w_up, w_down, *vectors)
    shapes = [
        jax.ShapeDtypeStruct((items, block, width), bf16),
        jax.ShapeDtypeStruct((items, block, width), f32),
        jax.ShapeDtypeStruct((width, 3 * width), f32),
        jax.ShapeDtypeStruct((width, width), f32),
        jax.ShapeDtypeStruct((width, ff), f32),
        jax.ShapeDtypeStruct((ff, width), f32),
    ] + [jax.ShapeDtypeStruct((1, width), f32)] * 4
    outs = pl.pallas_call(
        split_kernel,
        out_shape=shapes,
        in_specs=[vmem] * 4,
        out_specs=[anywhere] * 6 + [vmem] * 4,
        scratch_shapes=[
            vm((width, 3 * width), f32),
            vm((width, width), f32),
            vm((width, ff), f32),
            vm((ff, width), f32),
            pltpu.SemaphoreType.DMA((6,)),
        ],
        compiler_params=pltpu.CompilerParams(vmem_limit_bytes=8 * 2**20),
    )(*raw)
    return tuple(outs[:6]) + tuple(v.reshape(width) for v in outs[6:])


def solution(mesh):
    split = P("items", "seq", None)
    seq_size = mesh.shape["seq"]
    mesh_sizes = (mesh.shape["items"], seq_size // 2)
    return jax.shard_map(
        functools.partial(shards, seq_size, mesh_sizes),
        mesh=mesh,
        in_specs=(split, P("items"), P("items", None)) + (P(),) * 8 + (split,),
        out_specs=(split, split) + (P(),) * 8,
        check_vma=False,
    )
```

```python
import functools
import math

import jax
import jax.numpy as jnp
from jax import lax
from jax.experimental import pallas as pl
from jax.experimental.pallas import tpu as pltpu
from jax.sharding import PartitionSpec as P

HEADS = 2
HEAD_DIM = 128
ROW = 96
D = HEADS * HEAD_DIM

epsilon = 1e-05
branch_scale = 0.7071067811865476
masked_value = -1e30
score_scale = HEAD_DIM ** (-0.5)
log2e = math.log2(math.e)
gelu_in = math.sqrt(2 / math.pi)
gelu_cube = gelu_in * 0.044715
f32 = jnp.float32
bf16 = jnp.bfloat16


def dot(left, right, left_dim=1, right_dim=0):
    return lax.dot_general(
        left, right, (((left_dim,), (right_dim,)), ((), ())), preferred_element_type=f32
    )


def normalise(inputs):
    average = jnp.mean(inputs, -1, keepdims=True)
    centred = inputs - average
    spread = jnp.mean(centred * centred, -1, keepdims=True)
    factor = lax.rsqrt(spread + epsilon)
    return centred * factor, factor


def norm_back(grad, normed, factor, gain):
    e = grad * gain
    first = jnp.mean(e, -1, keepdims=True)
    second = jnp.mean(e * normed, -1, keepdims=True)
    return factor * (e - first - normed * second)


def fold_rows(values):
    count = values.shape[0] // 8
    return jnp.sum(values.reshape(count, 8, values.shape[1]), 0)


def plan():
    plan = {
        "feed0": [],
        "feed1": [(0, 0)],
        "feed2": [(0, 1)],
        "feed3": [(1, 0)],
        "middle": [(1, 1)],
        "back0": [],
        "weight0": [(2, 0), (0, 2)],
        "back1": [(2, 1), (1, 2), (0, 3)],
        "weight1": [(3, 0)],
        "tokens0": [],
        "tokens1": [(3, 1)],
        "finish0": [],
        "finish1": [("v", 1), (0, 4), (2, 2), (1, 3)],
        "tail": [
            (3, 2), ("v", 2), (1, 4), (2, 3), (0, 5), (3, 3),
            (1, 5), (2, 5), (0, 6), (3, 5), (1, 6), ("v", 3),
        ],
        "last": [(2, 6), (3, 6)],
    }
    return plan


class Sums:
    def __init__(self, mesh_sizes, refs):
        (self.partial, self.c_out, self.c_in, self.i_out, self.i_in, self.z_out, self.z_in,
         self.full, self.send, self.recv) = refs
        self.n_items, self.n_z = mesh_sizes
        self.item = lax.axis_index("items")
        seq = lax.axis_index("seq")
        self.core = lax.rem(seq, 2)
        self.z = seq // 2
        self.sent = []

    def partner(self, kind, step):
        if kind == "core":
            return {"items": self.item, "seq": self.z * 2 + 1 - self.core}
        if kind == "items":
            return {"items": lax.rem(self.item + step, self.n_items), "seq": self.z * 2 + self.core}
        return {"items": self.item, "seq": lax.rem(self.z + step, self.n_z) * 2 + self.core}

    def steps_of(self, kind):
        return range(1, {"core": 2, "items": self.n_items, "z": self.n_z}[kind])

    def copies(self, part, phase, kind, source, target):
        number = part * 6 + phase * 3 + {"core": 0, "items": 1, "z": 2}[kind]
        return number, [
            pltpu.make_async_remote_copy(
                src_ref=source(step),
                dst_ref=target(step),
                send_sem=self.send.at[number],
                recv_sem=self.recv.at[number],
                device_id=self.partner(kind, step),
                device_id_type=pl.DeviceIdType.MESH,
            )
            for step in self.steps_of(kind)
        ]

    def start(self, copies):
        for copy in copies[1]:
            copy.start()

    def finish(self, copies, count):
        number, each = copies
        size = self.full.at[pl.ds(0, len(each) * count)]
        pltpu.make_async_copy(size, size, self.recv.at[number]).wait()
        self.sent.append((number, len(each) * count))

    def drain(self):
        for number, count in self.sent:
            size = self.full.at[pl.ds(0, count)]
            pltpu.make_async_copy(size, size, self.send.at[number]).wait()

    def place(self, first, rows):
        half = rows // 2
        quarter = half // self.n_items
        split = quarter % (16 * self.n_z) == 0 and rows > 2 * D
        last = quarter // self.n_z if split else quarter
        return half, quarter, split, last

    def first_copies(self, part, first, rows):
        half, _, _, _ = self.place(first, rows)
        here = pl.ds(first // 2, half)
        return self.copies(part, 0, "core", lambda s: self.c_out.at[here], lambda s: self.c_in.at[here])

    def items_copies(self, part, first, rows):
        half, quarter, _, _ = self.place(first, rows)

        def source(step):
            to = lax.rem(self.item + step, self.n_items)
            return self.i_out.at[pl.ds(pl.multiple_of(first // 2 + to * quarter, 16), quarter)]

        at = pl.ds(first // 2 // self.n_items, quarter)
        return self.copies(part, 0, "items", source, lambda s: self.i_in.at[s - 1, at])

    def z_copies(self, part, first, rows):
        half, quarter, split, last = self.place(first, rows)
        base = first // 2 // self.n_items
        if split:
            def source(step):
                to = lax.rem(self.z + step, self.n_z)
                return self.z_out.at[pl.ds(pl.multiple_of(base + to * last, 16), last)]

            at = pl.ds(base // self.n_z, last)
            return self.copies(part, 0, "z", source, lambda s: self.z_in.at[s - 1, at])
        at = pl.ds(base, quarter)
        return self.copies(part, 0, "z", lambda s: self.z_out.at[at], lambda s: self.z_in.at[self.z, at])

    def held(self, first, rows, level):
        half, quarter, split, last = self.place(first, rows)
        at = first + self.core * half
        count = half
        if level > 0:
            at += self.item * quarter
            count = quarter
        if level > 1 and split:
            at += self.z * last
            count = last
        return self.full.at[pl.ds(pl.multiple_of(at, 16), count)]

    def back_copies(self, part, first, rows, kind):
        level = {"core": 0, "items": 1, "z": 2}[kind]
        ref = self.held(first, rows, level)
        return self.copies(part, 1, kind, lambda s: ref, lambda s: ref)

    def step(self, part, first, rows, number):
        half, quarter, split, last = self.place(first, rows)
        base_c = first // 2
        base_i = base_c // self.n_items
        if number == 0:
            away = pl.ds(pl.multiple_of(first + (1 - self.core) * half, 16), half)
            self.c_out[pl.ds(base_c, half)] = self.partial[away].astype(bf16)
            self.start(self.first_copies(part, first, rows))
        if number == 1:
            self.finish(self.first_copies(part, first, rows), half)
            here = pl.ds(base_c, half)
            own = pl.ds(pl.multiple_of(first + self.core * half, 16), half)
            self.i_out[here] = (self.partial[own] + self.c_in[here].astype(f32)).astype(bf16)
            self.start(self.items_copies(part, first, rows))
        if number == 2:
            self.finish(self.items_copies(part, first, rows), quarter)
            own = pl.ds(pl.multiple_of(base_c + self.item * quarter, 16), quarter)
            at = pl.ds(base_i, quarter)
            value = self.i_out[own].astype(f32)
            for step in self.steps_of("items"):
                value += self.i_in[step - 1, at].astype(f32)
            self.z_out[at] = value.astype(bf16)
            if not split:
                self.z_in[self.z, at] = value.astype(bf16)
            self.start(self.z_copies(part, first, rows))
        if number == 3:
            self.finish(self.z_copies(part, first, rows), last)
            if split:
                own = pl.ds(pl.multiple_of(base_i + self.z * last, 16), last)
                at = pl.ds(base_i // self.n_z, last)
                value = self.z_out[own].astype(f32)
                for step in self.steps_of("z"):
                    value += self.z_in[step - 1, at].astype(f32)
            else:
                at = pl.ds(base_i, quarter)
                value = self.z_in[0, at].astype(f32)
                for step in self.steps_of("z"):
                    value += self.z_in[step, at].astype(f32)
            self.held(first, rows, 2)[...] = value.astype(bf16)
            if split:
                self.start(self.back_copies(part, first, rows, "z"))
            else:
                self.start(self.back_copies(part, first, rows, "items"))
        if number == 4 and split:
            self.finish(self.back_copies(part, first, rows, "z"), last)
            self.start(self.back_copies(part, first, rows, "items"))
        if number == 5:
            self.finish(self.back_copies(part, first, rows, "items"), quarter)
            self.start(self.back_copies(part, first, rows, "core"))
        if number == 6:
            self.finish(self.back_copies(part, first, rows, "core"), rows // 2)


def layer_kernel(
    items,
    rows,
    mesh_sizes,
    seq_size,
    lengths_ref,
    pad_ref,
    tokens_ref,
    cot_hbm,
    wqkv_hbm,
    wout_hbm,
    wup_hbm,
    wdown_hbm,
    gain_attn_ref,
    shift_attn_ref,
    gain_ffn_ref,
    shift_ffn_ref,
    output_ref,
    gtok_ref,
    grads_ref,
    gvec_ref,
    x,
    cot,
    alive,
    keys,
    wqkv,
    wout,
    wup,
    wdown,
    h1,
    n1,
    r1,
    proj,
    exps,
    inv,
    att,
    middle,
    n2,
    r2,
    h2,
    dbr,
    hid,
    dpre,
    ghalo,
    ghalo_in,
    gvec,
    vec_buf,
    partial,
    c_out,
    c_in,
    i_out,
    i_in,
    z_out,
    z_in,
    load_sems,
    halo_sems,
    vec_sems,
    send_sems,
    recv_sems,
):
    block = rows * ROW
    total = items * block
    gain_attn = gain_attn_ref[...]
    shift_attn = shift_attn_ref[...]
    gain_ffn = gain_ffn_ref[...]
    shift_ffn = shift_ffn_ref[...]
    ff = wup.shape[1]
    chunks = ff // D
    n_items, n_z = mesh_sizes
    item = lax.axis_index("items")
    seq = lax.axis_index("seq")
    MESH = pl.DeviceIdType.MESH
    sums = Sums(
        mesh_sizes, (partial, c_out, c_in, i_out, i_in, z_out, z_in, grads_ref, send_sems, recv_sems)
    )
    wide = chunks // 2
    parts = [(k * wide * 2 * D, wide * 2 * D) for k in range(2)]
    parts += [((chunks + h) * 2 * D, 2 * D) for h in range(HEADS)]
    schedule = plan()

    def hook(name):
        for part, number in schedule[name]:
            if part == "v":
                vec_step(number)
            else:
                sums.step(part, *parts[part], number)

    after = {"items": item, "seq": lax.rem(seq + 1, seq_size)}
    ahead = {"items": item, "seq": lax.rem(seq + seq_size - 1, seq_size)}
    barrier = pltpu.get_barrier_semaphore()
    greeted = [after, ahead]
    for kind in ("core", "items", "z"):
        greeted += [sums.partner(kind, s) for s in sums.steps_of(kind)]
    for device in greeted:
        pl.semaphore_signal(barrier, inc=1, device_id=device, device_id_type=MESH)

    loads = [
        (wout_hbm, wout),
        (wup_hbm, wup),
        (wdown_hbm, wdown),
        (cot_hbm, cot),
    ]
    token_loads = [
        pltpu.make_async_copy(tokens_ref.at[i], x.at[i, pl.ds(ROW, block)], load_sems.at[4 + i])
        for i in range(items)
    ]
    weight_loads = [
        pltpu.make_async_copy(source, target, load_sems.at[k])
        for k, (source, target) in enumerate(loads)
    ]
    qkv_loads = [
        pltpu.make_async_copy(
            wqkv_hbm.at[:, pl.ds(p * D + h * HEAD_DIM, HEAD_DIM)],
            wqkv.at[:, pl.ds((h * 3 + p) * HEAD_DIM, HEAD_DIM)],
            load_sems.at[4 + items + h * 3 + p],
        )
        for h in range(HEADS)
        for p in range(3)
    ]
    for copy in qkv_loads:
        copy.start()
    for copy in token_loads:
        copy.start()
    for copy in weight_loads:
        copy.start()


    first_pos = seq * block

    def window(start, width):
        spots = sorted({(s * block + (start if s else 0)) % 128 for s in range(seq_size)})
        if start:
            spots = sorted({(s * block + start) % 128 for s in range(1, seq_size)})
        at = jnp.maximum(first_pos + start, 0)
        low = pl.multiple_of(at // 128 * 128, 128)
        wide = (spots[-1] + width + 127) // 128 * 128
        held = pad_ref[:, pl.ds(low, wide)]
        result = held[:, spots[0] : spots[0] + width]
        for spot in spots[1:]:
            result = jnp.where(at % 128 == spot, held[:, spot : spot + width], result)
        return result

    count = jnp.zeros((items, 1), jnp.int32)
    which = lax.broadcasted_iota(jnp.int32, (items, 1), 0)
    for i in range(items):
        count = jnp.where(which == i, lengths_ref[i], count)

    def there(start, width):
        position = first_pos + start + lax.broadcasted_iota(jnp.int32, (items, width), 1)
        good = (position >= 0) & (position < count) & (window(start, width) == 1)
        return jnp.where(good, 1.0, 0.0)

    row_there = [there((r - 1) * ROW, ROW) for r in range(rows + 1)]
    spread = lax.broadcasted_iota(jnp.int32, (items, items * 128), 1) // 128
    spread = jnp.where(spread == lax.broadcasted_iota(jnp.int32, (items, items * 128), 0), 1.0, 0.0)
    for r in range(rows):
        both = jnp.concatenate([row_there[r], row_there[r + 1]], 1)
        keys[r, :items, : 2 * ROW] = (1.0 - both) * masked_value
        column = dot(row_there[r + 1].astype(bf16), spread.astype(bf16), 0, 0)
        for i in range(items):
            alive[i, r * ROW : (r + 1) * ROW] = column[:, i * 128 : (i + 1) * 128]

    def alive_of(i):
        mask = alive[i]
        return jnp.concatenate([mask, mask], 1)

    def first_norm(values):
        normed, factor = normalise(values)
        return (normed * gain_attn + shift_attn).astype(bf16), normed.astype(bf16), factor

    for copy in qkv_loads:
        copy.wait()
    def project(first, end):
        for i in range(first, end):
            token_loads[i].wait()
        found = [first_norm(x[i, ROW:].astype(f32)) for i in range(first, end)]
        results = [dot(low, wqkv[...]).astype(bf16) for low, _, _ in found]
        for i in range(first, end):
            low, normed, factor = found[i - first]
            h1[i, ROW:] = low
            n1[i, ROW:] = normed
            r1[i, ROW:] = jnp.broadcast_to(factor, (block, 128))
            proj[i, ROW:] = results[i - first]

    early = items // 3
    project(0, early)
    pl.semaphore_wait(barrier, len(greeted))
    halo_copy = pltpu.make_async_remote_copy(
        src_ref=tokens_ref.at[:, pl.ds(block - ROW, ROW)],
        dst_ref=x.at[:, pl.ds(0, ROW)],
        send_sem=halo_sems.at[0],
        recv_sem=halo_sems.at[1],
        device_id=after,
        device_id_type=MESH,
    )

    @pl.when(seq < seq_size - 1)
    def _():
        halo_copy.start()

    @pl.when(seq == 0)
    def _():
        x[:, :ROW] = jnp.zeros((items, ROW, D), bf16)
    project(early, items)

    query_pos = lax.broadcasted_iota(jnp.int32, (ROW, 2 * ROW), 0)
    key_pos = lax.broadcasted_iota(jnp.int32, (ROW, 2 * ROW), 1) - ROW
    causal = jnp.where(key_pos <= query_pos, 0.0, masked_value)
    itself = jnp.where(key_pos == query_pos, 0.0, masked_value)
    for copy in weight_loads:
        copy.wait()

    def part_of(whole, r, count, number, h):
        at = (h * 3 + number) * HEAD_DIM
        return whole[r * ROW : (r + count) * ROW, at : at + HEAD_DIM]

    def weigh(mine, keys_of, units):
        biases = {r: jnp.maximum(jnp.minimum(causal, keys_of(r)), itself) for r, _ in units}
        scores = [
            dot(part_of(mine, r + 1, 1, 0, h), part_of(mine, r, 2, 1, h), 1, 1)
            * (score_scale * log2e)
            + biases[r]
            for r, h in units
        ]
        es = [jnp.exp2(one - jnp.max(one, -1, keepdims=True)) for one in scores]
        shares = [
            jnp.broadcast_to(1.0 / jnp.sum(e, -1, keepdims=True), (ROW, HEAD_DIM)) for e in es
        ]
        lows = [e.astype(bf16) for e in es]
        results = [
            (dot(e, part_of(mine, r, 2, 2, h)) * share).astype(bf16)
            for e, share, (r, h) in zip(lows, shares, units)
        ]
        return lows, shares, results

    def heads(values):
        return jnp.concatenate(values, 1)

    def attend(first, end):
        units = [(r, h) for r in range(first, end) for h in range(HEADS)]
        here = slice(first * ROW, end * ROW)
        count = (end - first) * ROW
        mask = alive[:, here]
        grads = jnp.concatenate([mask, mask], 2) * cot[:, here].astype(f32)
        grads = (branch_scale * grads).astype(bf16)
        all_shares, all_results, all_lows = [], [], []
        for i in range(items):
            lows, shares, results = weigh(proj[i], lambda r: keys[r, i : i + 1, : 2 * ROW], units)
            all_lows.append(lows)
            for values, joined in ((shares, all_shares), (results, all_results)):
                lines = [heads(values[k : k + HEADS]) for k in range(0, len(units), HEADS)]
                joined.append(jnp.concatenate(lines, 0))
        attended = jnp.concatenate(all_results, 0)
        inputs = x[:, ROW + first * ROW : ROW + end * ROW].astype(f32).reshape(items * count, D)
        mid = inputs + branch_scale * dot(attended, wout[...])
        normed, factor = normalise(mid)
        low = (normed * gain_ffn + shift_ffn).astype(bf16)
        for i in range(items):
            mine = slice(i * count, (i + 1) * count)
            flat = slice(i * block + first * ROW, i * block + end * ROW)
            for (r, h), e in zip(units, all_lows[i]):
                exps[i, r * HEADS + h, :, : 2 * ROW] = e
            inv[i, here] = all_shares[i]
            att[i, here] = all_results[i]
            middle[i, here] = mid[mine]
            n2[i, here] = normed[mine].astype(bf16)
            r2[i, here] = jnp.broadcast_to(factor[mine], (count, 128))
            h2[flat] = low[mine]
            dbr[flat] = grads[i]

    attend(1, rows)

    @pl.when(seq < seq_size - 1)
    def _():
        halo_copy.wait_send()

    @pl.when(seq > 0)
    def _():
        halo_copy.wait_recv()

    low, normed, factor = first_norm(x[:, :ROW].astype(f32).reshape(items * ROW, D))
    results = [
        dot(low, wqkv[:, (h * 3 + 1) * HEAD_DIM : (h * 3 + 3) * HEAD_DIM]).astype(bf16)
        for h in range(HEADS)
    ]
    h1[:, :ROW] = low.reshape(items, ROW, D)
    n1[:, :ROW] = normed.reshape(items, ROW, D)
    r1[:, :ROW] = jnp.broadcast_to(factor, (items * ROW, 128)).reshape(items, ROW, 128)
    for h in range(HEADS):
        at = (h * 3 + 1) * HEAD_DIM
        proj[:, :ROW, at : at + 2 * HEAD_DIM] = results[h].reshape(items, ROW, 2 * HEAD_DIM)
    attend(0, 1)

    for c in range(chunks):
        cols = slice(c * D, (c + 1) * D)
        down = slice(c * 2 * D, c * 2 * D + D)
        up = slice(c * 2 * D + D, (c + 1) * 2 * D)

        normed = h2[...]
        grad = dbr[...]
        u = dot(normed, wup[:, cols])
        back = dot(grad, wdown[cols], 1, 1)
        square = u * u
        s = 0.5 * jnp.tanh(u * (gelu_in + gelu_cube * square)) + 0.5
        hidden = (u * s).astype(bf16)
        slope = s + u * ((s - s * s) * (2 * gelu_in + 6 * gelu_cube * square))
        before = (back * slope).astype(bf16)
        down_grad = dot(hidden, grad, 0, 0)
        up_grad = dot(normed, before, 0, 0)
        hid[:, cols] = hidden
        dpre[:, cols] = before
        partial[down] = down_grad
        partial[up] = up_grad
        hook("feed%d" % c)

    last = chunks * 2 * D

    found = []
    for i in range(items):
        normed = n2[i].astype(f32)
        factor = jnp.concatenate([r2[i]] * 2, 1)
        outer = alive_of(i) * cot[i].astype(f32)
        grad = dot(dpre[i * block : (i + 1) * block], wup[...], 1, 1)
        sums_here = fold_rows(grad * normed), fold_rows(grad)
        grad = outer + norm_back(grad, normed, factor, gain_ffn)
        found.append((grad, (branch_scale * grad).astype(bf16), sums_here))
    lows = jnp.concatenate([f[1] for f in found], 0)
    out_grad = dot(att[...].reshape(total, D), lows, 0, 0)
    back = dot(lows, wout[...], 1, 1).astype(bf16)
    for i in range(items):
        gtok_ref[i] = found[i][0]
    h2[...] = back
    partial[last + D : last + 2 * D] = out_grad
    gvec[16:24] = sum(f[2][0] for f in found)
    gvec[24:32] = sum(f[2][1] for f in found)
    hook("middle")

    def attend_back(h):
        at = h * 3 * HEAD_DIM
        lanes = slice(h * HEAD_DIM, (h + 1) * HEAD_DIM)
        found = []
        for i in range(items):
            mine = proj[i, :, at : at + 3 * HEAD_DIM]
            es = [exps[i, r * HEADS + h, :, : 2 * ROW] for r in range(rows)]
            scaled = h2[i * block : (i + 1) * block, lanes].astype(f32) * inv[i, :, lanes]
            product = scaled * att[i, :, lanes].astype(f32)
            low = scaled.astype(bf16)
            dqs, dks, dvs = [], [], []
            dps = [
                dot(low[r * ROW : (r + 1) * ROW], part_of(mine, r, 2, 2, 0), 1, 1)
                for r in range(rows)
            ]
            dss = []
            for r in range(rows):
                row_dot = jnp.sum(product[r * ROW : (r + 1) * ROW], -1, keepdims=True)
                dss.append((es[r].astype(f32) * ((dps[r] - row_dot) * score_scale)).astype(bf16))
            dvs = [dot(es[r], low[r * ROW : (r + 1) * ROW], 0, 0) for r in range(rows)]
            dks = [dot(dss[r], part_of(mine, r + 1, 1, 0, 0), 0, 0) for r in range(rows)]
            dqs = [dot(dss[r], part_of(mine, r, 2, 1, 0)).astype(bf16) for r in range(rows)]

            def gather(grads):
                lines = []
                for r in range(rows + 1):
                    value = 0.0
                    if r < rows:
                        value = grads[r][:ROW]
                    if r > 0:
                        value += grads[r - 1][ROW:]
                    lines.append(value.astype(bf16))
                return jnp.concatenate(lines, 0)

            found.append((jnp.concatenate(dqs, 0), gather(dks), gather(dvs)))
        for i in range(items):
            proj[i, :ROW, at : at + HEAD_DIM] = jnp.zeros((ROW, HEAD_DIM), bf16)
            proj[i, ROW:, at : at + HEAD_DIM] = found[i][0]
            proj[i, :, at + HEAD_DIM : at + 2 * HEAD_DIM] = found[i][1]
            proj[i, :, at + 2 * HEAD_DIM : at + 3 * HEAD_DIM] = found[i][2]

    def weight_back(first, end, rows_at):
        left = h1[...].reshape(items * (block + ROW), D)
        right = proj[:, :, first * D : end * D].reshape(items * (block + ROW), (end - first) * D)
        grad = dot(left, right, 0, 0)
        for k in range(end - first):
            at = last + (rows_at + k) * D
            partial[at : at + D] = grad[:, k * D : (k + 1) * D]

    attend_back(0)
    hook("back0")
    weight_back(0, 1, 0)
    hook("weight0")
    attend_back(1)
    hook("back1")
    weight_back(1, 3, 2)
    hook("weight1")

    grad = 0.0
    for h in range(HEADS):
        cols = slice((h * 3 + 1) * HEAD_DIM, (h * 3 + 3) * HEAD_DIM)
        grad += dot(proj[:, :ROW, cols].reshape(items * ROW, 2 * HEAD_DIM), wqkv[:, cols], 1, 1)
    normed = n1[:, :ROW].reshape(items * ROW, D).astype(f32)
    factor = r1[:, :ROW].reshape(items * ROW, 128)
    halo_sums = fold_rows(grad * normed), fold_rows(grad)
    grad = norm_back(grad, normed, jnp.concatenate([factor, factor], 1), gain_attn)
    ghalo[...] = grad.astype(bf16).reshape(items, ROW, D)
    ghalo_copy = pltpu.make_async_remote_copy(
        src_ref=ghalo,
        dst_ref=ghalo_in,
        send_sem=halo_sems.at[2],
        recv_sem=halo_sems.at[3],
        device_id=ahead,
        device_id_type=MESH,
    )

    @pl.when(seq > 0)
    def _():
        ghalo_copy.start()

    def tokens_back(first, end):
        found = []
        for i in range(first, end):
            grad = dot(proj[i, ROW:], wqkv[...], 1, 1)
            normed = n1[i, ROW:].astype(f32)
            factor = jnp.concatenate([r1[i, ROW:]] * 2, 1)
            sums_here = fold_rows(grad * normed), fold_rows(grad)
            found.append((gtok_ref[i] + norm_back(grad, normed, factor, gain_attn), sums_here))
        for i in range(first, end):
            gtok_ref[i] = found[i - first][0]
        return sum(f[1][0] for f in found), sum(f[1][1] for f in found)

    half = items // 2
    one = tokens_back(0, half)
    hook("tokens0")
    two = tokens_back(half, items)
    gvec[0:8] = one[0] + two[0] + halo_sums[0]
    gvec[8:16] = one[1] + two[1] + halo_sums[1]

    def vec_copies(kind, number):
        result = []
        place = {"core": sums.core, "items": item, "z": sums.z}[kind]
        base = {"core": 0, "items": 1, "z": n_items}[kind]
        for s in sums.steps_of(kind):
            here = vec_buf.at[number, place]
            result.append(
                pltpu.make_async_remote_copy(
                    src_ref=here,
                    dst_ref=here,
                    send_sem=vec_sems.at[0, base + s - 1],
                    recv_sem=vec_sems.at[1, base + s - 1],
                    device_id=sums.partner(kind, s),
                    device_id_type=MESH,
                )
            )
        return result

    def start_all(copies):
        for copy in copies:
            copy.start()

    def finish_all(copies):
        for copy in copies:
            copy.wait()

    def vec_total(number, size):
        value = vec_buf[number, 0]
        for k in range(1, size):
            value += vec_buf[number, k]
        return value

    lines = [jnp.sum(gvec[8 * k : 8 * k + 8], 0, keepdims=True) for k in range(4)]
    vec_buf[0, sums.core] = jnp.concatenate(lines + [jnp.zeros((4, D), f32)], 0)
    start_all(vec_copies("core", 0))

    def vec_step(number):
        if number == 1:
            finish_all(vec_copies("core", 0))
            vec_buf[1, item] = vec_total(0, 2)
            start_all(vec_copies("items", 1))
        if number == 2:
            finish_all(vec_copies("items", 1))
            vec_buf[2, sums.z] = vec_total(1, n_items)
            start_all(vec_copies("z", 2))
        if number == 3:
            finish_all(vec_copies("z", 2))
            gvec_ref[...] = vec_total(2, n_z)

    def finish(first, end):
        branch = dot(hid[first * block : end * block], wdown[...])
        results = [
            alive_of(i)
            * (middle[i] + branch_scale * branch[(i - first) * block : (i - first + 1) * block])
            for i in range(first, end)
        ]
        for i in range(first, end):
            output_ref[i] = results[i - first].astype(bf16)

    hook("tokens1")
    finish(0, half)
    hook("finish0")
    finish(half, items)
    hook("finish1")

    @pl.when(seq > 0)
    def _():
        ghalo_copy.wait_send()

    @pl.when(seq < seq_size - 1)
    def _():
        ghalo_copy.wait_recv()
        for i in range(items):
            gtok_ref[i, block - ROW :] += ghalo_in[i].astype(f32)

    hook("tail")
    hook("last")
    sums.drain()


def split_kernel(
    raw_out,
    raw_tok,
    grads,
    gvec,
    output,
    gtok,
    gqkv,
    gout,
    gup,
    gdown,
    gain_attn,
    shift_attn,
    gain_ffn,
    shift_ffn,
    qkv,
    wout,
    up,
    down,
    store_sems,
):
    chunks = up.shape[1] // D
    last = chunks * 2 * D
    stores = []

    def store(source, target):
        copy = pltpu.make_async_copy(source, target, store_sems.at[len(stores)])
        copy.start()
        stores.append(copy)

    store(raw_tok, gtok)
    store(raw_out, output)
    for c in range(chunks):
        down[c * D : (c + 1) * D] = grads[c * 2 * D : c * 2 * D + D].astype(f32)
    store(down, gdown)
    for c in range(chunks):
        up[:, c * D : (c + 1) * D] = grads[c * 2 * D + D : (c + 1) * 2 * D].astype(f32)
    store(up, gup)
    wout[...] = grads[last + D : last + 2 * D].astype(f32)
    for k, rows_at in enumerate((0, 2, 3)):
        value = grads[last + rows_at * D : last + (rows_at + 1) * D].astype(f32)
        for half in range(2):
            h, p = divmod(2 * k + half, 3)
            at = p * D + h * HEAD_DIM
            qkv[:, at : at + HEAD_DIM] = value[:, half * HEAD_DIM : (half + 1) * HEAD_DIM]
    store(qkv, gqkv)
    store(wout, gout)
    gain_attn[...] = gvec[0:1]
    shift_attn[...] = gvec[1:2]
    gain_ffn[...] = gvec[2:3]
    shift_ffn[...] = gvec[3:4]
    for copy in stores:
        copy.wait()


def shards(
    seq_size,
    mesh_sizes,
    tokens,
    lengths,
    pad_mask,
    w_qkv,
    w_out,
    w_up,
    w_down,
    gain_attn,
    shift_attn,
    gain_ffn,
    shift_ffn,
    cotangent,
):
    items, block, width = tokens.shape
    rows = block // ROW
    total = items * block
    ff = w_up.shape[1]
    ext = block + ROW
    n_items, n_z = mesh_sizes
    grad_rows = 2 * ff + 4 * width
    half = grad_rows // 2
    links = n_items + n_z - 1
    vmem = pl.BlockSpec(memory_space=pltpu.VMEM)
    anywhere = pl.BlockSpec(memory_space=pl.ANY)
    raw = [
        pltpu.VMEM((items, block, width), bf16),
        pltpu.VMEM((items, block, width), f32),
        pltpu.VMEM((grad_rows, width), bf16),
        pltpu.VMEM((8, width), f32),
    ]
    vectors = [v.reshape(1, width) for v in (gain_attn, shift_attn, gain_ffn, shift_ffn)]
    parts = 2 + HEADS
    vm = pltpu.VMEM
    raw = pl.pallas_call(
        functools.partial(layer_kernel, items, rows, mesh_sizes, seq_size),
        out_shape=raw,
        in_specs=[pl.BlockSpec(memory_space=pltpu.SMEM), vmem] + [anywhere] * 6 + [vmem] * 4,
        out_specs=[vmem] * 4,
        scratch_shapes=[
            vm((items, ext, width), bf16),
            vm((items, block, width), bf16),
            vm((items, block, 128), f32),
            vm((rows, 8, 256), f32),
            vm((width, 3 * width), bf16),
            vm((width, width), bf16),
            vm((width, ff), bf16),
            vm((ff, width), bf16),
            vm((items, ext, width), bf16),
            vm((items, ext, width), bf16),
            vm((items, ext, 128), f32),
            vm((items, ext, 3 * width), bf16),
            vm((items, rows * HEADS, ROW, 256), bf16),
            vm((items, block, width), f32),
            vm((items, block, width), bf16),
            vm((items, block, width), f32),
            vm((items, block, width), bf16),
            vm((items, block, 128), f32),
            vm((total, width), bf16),
            vm((total, width), bf16),
            vm((total, ff), bf16),
            vm((total, ff), bf16),
            vm((items, ROW, width), bf16),
            vm((items, ROW, width), bf16),
            vm((32, width), f32),
            vm((3, max(n_items, n_z), 8, width), f32),
            vm((grad_rows, width), f32),
            vm((half, width), bf16),
            vm((half, width), bf16),
            vm((half, width), bf16),
            vm((n_items - 1, half // n_items, width), bf16),
            vm((half // n_items, width), bf16),
            vm((n_z, half // n_items, width), bf16),
            pltpu.SemaphoreType.DMA((4 + items + 3 * HEADS,)),
            pltpu.SemaphoreType.DMA((4,)),
            pltpu.SemaphoreType.DMA((2, links)),
            pltpu.SemaphoreType.DMA((6 * parts,)),
            pltpu.SemaphoreType.DMA((6 * parts,)),
        ],
        compiler_params=pltpu.CompilerParams(
            vmem_limit_bytes=52 * 2**20, collective_id=0, has_side_effects=True
        ),
    )(lengths, pad_mask, tokens, cotangent, w_qkv, w_out, w_up, w_down, *vectors)
    shapes = [
        jax.ShapeDtypeStruct((items, block, width), bf16),
        jax.ShapeDtypeStruct((items, block, width), f32),
        jax.ShapeDtypeStruct((width, 3 * width), f32),
        jax.ShapeDtypeStruct((width, width), f32),
        jax.ShapeDtypeStruct((width, ff), f32),
        jax.ShapeDtypeStruct((ff, width), f32),
    ] + [jax.ShapeDtypeStruct((1, width), f32)] * 4
    outs = pl.pallas_call(
        split_kernel,
        out_shape=shapes,
        in_specs=[vmem] * 4,
        out_specs=[anywhere] * 6 + [vmem] * 4,
        scratch_shapes=[
            vm((width, 3 * width), f32),
            vm((width, width), f32),
            vm((width, ff), f32),
            vm((ff, width), f32),
            pltpu.SemaphoreType.DMA((6,)),
        ],
        compiler_params=pltpu.CompilerParams(vmem_limit_bytes=8 * 2**20),
    )(*raw)
    return tuple(outs[:6]) + tuple(v.reshape(width) for v in outs[6:])


def solution(mesh):
    split = P("items", "seq", None)
    seq_size = mesh.shape["seq"]
    mesh_sizes = (mesh.shape["items"], seq_size // 2)
    return jax.shard_map(
        functools.partial(shards, seq_size, mesh_sizes),
        mesh=mesh,
        in_specs=(split, P("items"), P("items", None)) + (P(),) * 8 + (split,),
        out_specs=(split, split) + (P(),) * 8,
        check_vma=False,
    )
```
